128 devices in a mesh: logic: 8 (over z, core), slab: 16 (over y, x).
Axes of the slice: x: 4, y: 4, z: 4, core: 2. Of those that a mesh axis runs over, the one named last changes fastest.
Arguments:
- initial_heat_state: float32 [128, 512, 1024], P('slab', 'logic'), may hold values from 0 to 2
- dynamic_wattage: bfloat16 [262144, 256], P(('logic', 'slab')), may hold values from 0.099609375 to 1
- drain_multiplier: float32 [262144], P(('logic', 'slab')), may hold values from 0.2 to 2
- holder_processor: int32 [262144, 1], P(('logic', 'slab')), may hold values from 0 to 127; in each aligned block of 2048 rows (0 to 2047, 2048 to 4095, ...) at most 32 rows name the same one
- patch_target_slot: int32 [262144], P(('logic', 'slab')), may hold values from 0 to 2047
- active_patch_number: int32 [128], P(('logic', 'slab')), may hold values from 1024 to 2048, as said below
- prior_reduced_heat_map: float32 [128, 32, 4], replicated, may hold values from 0 to 2
- conductivity_lookup: float32 [8, 3], replicated, may hold values from 0.02 to 0.15
- substance_of_slab: int32 [128], replicated, may hold values from 0 to 7
Outputs:
- new_temperature: float32 [128, 512, 1024], P('slab', 'logic')
- coarse_map: float32 [128, 32, 4], replicated
The draws below stay inside these ranges and needn't reach their ends.
Inputs may be any that keep to these rules, and one draw needn't show every extreme that they name: `holder_processor`: among the rows of one device, at most 32 name the same owner, a bound that some block reaches. `active_patch_number`: at least half the slots are live; some device has all 2048 live.
All inputs are finite; a program needn't handle non-finite values.
Results may differ from the reference program's by a relative error of at most 0.00069.
Values may be sent and summed in bfloat16 or wider, within the bound.
No kernel may reach another device: no remote copies, remote signals or barrier semaphores. Data moves between devices by JAX's collectives and lax.ppermute only.
A program may use at most 64 MiB of HBM per device.

```python
import math
import jax
import jax.numpy as jnp
import numpy as np

CZ = 8
CY = 64
SITES_ALONG_LINE = 1024
TILES_DEV = 2048
STEPS = 4
MATERIALS = 8
SOURCES = 128
CAP = 32
TILES = 262144
SLAB_STACK_SIZE = 128
MESH_LINES = 512
OWN_TILES = 2048
N_SLAB = 16


def draw_active_patch_number(key, part):
    key = jax.random.fold_in(key, 11)
    first_key, second_key = jax.random.split(key)
    counts = jax.random.randint(first_key, (SOURCES,), TILES_DEV // 2, TILES_DEV + 1)
    chosen = jax.random.randint(second_key, (), 0, SOURCES)
    return jnp.where(jnp.arange(SOURCES) == chosen, TILES_DEV, counts).astype(jnp.int32)


def set_ends(array, rng, least, high):
    spot = [jax.random.randint(jax.random.fold_in(rng, axis), (), 0, length) for axis, length in enumerate(array.shape)]
    main_axis = array.shape.index(max(array.shape))
    beside = spot[:main_axis] + [(spot[main_axis] + 1) % array.shape[main_axis]] + spot[main_axis + 1:]
    return array.at[tuple(spot)].set(least).at[tuple(beside)].set(high)


def steps_of(rng, dims, shards, smallest, largest):
    factor_of, own = 1.0, jax.random.fold_in(rng, 6)
    for dim, shards_of in shards:
        steps = jnp.exp(jax.random.uniform(jax.random.fold_in(own, dim), (shards_of,), jnp.float32, smallest / len(shards), largest / len(shards)))
        factor_of = factor_of * jnp.repeat(steps, dims[dim] // shards_of).reshape([-1 if axis == dim else 1 for axis in range(len(dims))])
    return factor_of


def routed_block(key, own, number, rows, count, top, limit, skew):
    sequence = jax.random.permutation(key, count)
    heavy_load, usual = portions_of(count, rows * top, limit, skew, True), portions_of(count, rows * top, limit, skew, False)
    places = jnp.arange(count)

    def named(sizes, turn):
        used = int((sizes > 0).sum())
        fixed = max(1, used // 4)
        passed = fixed + (places - fixed + turn * (used - fixed)) % max(1, count - fixed)
        return jnp.zeros((count,), jnp.int32).at[sequence[jnp.where(places < fixed, places, passed)]].set(jnp.asarray(sizes, jnp.int32))

    sizes = jnp.where(number % 4 == 0, named(heavy_load, number // 4), named(usual, number - number // 4 - 1))
    mixed = jax.random.permutation(jax.random.fold_in(own, 3), count)
    giver, taker = mixed[0:count // 2 * 2:2], mixed[1:count // 2 * 2:2]
    margin = jnp.minimum(sizes[giver] - 1, limit - sizes[taker]) // 2
    margin = jnp.where((giver == sequence[0]) | (taker == sequence[0]) | (sizes[taker] == 0), 0, jnp.maximum(margin, 0))
    passed = jax.random.randint(jax.random.fold_in(own, 4), (count // 2,), 0, 1 << 20) % (margin + 1)
    sizes = sizes.at[giver].add(-passed).at[taker].add(passed)
    members = jnp.searchsorted(jnp.cumsum(sizes), jnp.arange(rows * top), side="right").astype(jnp.int32)
    grid = members.reshape(top, rows).T
    grid = grid[jax.random.permutation(jax.random.fold_in(own, 1), rows)]
    turn = jax.random.randint(jax.random.fold_in(own, 2), (rows, 1), 0, top)
    return jnp.take_along_axis(grid, (jnp.arange(top)[None, :] + turn) % top, axis=1)


def portions_of(count, total, most, skew, full):
    loads = [(1 << 20) // math.isqrt(rank ** skew) + 1 for rank in range(1, count + 1)]
    largest = most if full else min(most, max(-(-total // count), total * loads[0] // sum(loads)))
    least = 1 if total - largest >= count - 1 else 0
    given, spare = [largest] + [least] * (count - 1), total - largest - least * (count - 1)
    while spare > 0:
        candidates = [i for i in range(1, count) if given[i] < largest] or [i for i in range(1, count) if given[i] < most]
        pool, left = sum([loads[i] for i in candidates]), spare
        for i in candidates:
            more = min(most - given[i], max(1, left * loads[i] // pool), spare)
            given[i] = given[i] + more
            spare = spare - more
    return np.array(given)


def setup_inputs(seed: int = 0) -> dict:
    keys = jax.random.split(jax.random.key(seed), 10)
    initial_heat_state = jnp.clip(2.0 * jax.random.uniform(keys[0], (SLAB_STACK_SIZE, MESH_LINES, SITES_ALONG_LINE), jnp.float32) ** steps_of(keys[0], (SLAB_STACK_SIZE, MESH_LINES, SITES_ALONG_LINE), ((0, 16), (1, 8)), -0.2, 0.2), 0.0, 2.0)
    dynamic_wattage = jnp.clip(jnp.exp(math.log(1.0) - 2.306499 * jax.random.uniform(keys[1], (TILES, 256), jnp.float32) ** steps_of(keys[1], (TILES, 256), ((0, 128),), -0.2, 0.2)), 0.099609375, 1.0).astype(jnp.bfloat16)
    drain_multiplier = jnp.clip(jnp.exp(math.log(2.0) - 2.3025851 * jax.random.uniform(keys[2], (TILES,), jnp.float32) ** steps_of(keys[2], (TILES,), ((0, 128),), -0.2, 0.2)), 0.2, 2.0)
    holder_processor_keys = jax.random.split(jax.random.fold_in(keys[3], 1), TILES // TILES_DEV)
    holder_processor_turns = jax.random.permutation(jax.random.fold_in(keys[3], 3), TILES // TILES_DEV)
    holder_processor = jax.vmap(lambda own, number: routed_block(jax.random.fold_in(keys[3], 2), own, number, TILES_DEV, SOURCES, 1, CAP, 2))(holder_processor_keys, holder_processor_turns).reshape((TILES, 1))
    patch_target_slot = set_ends(jax.random.randint(keys[4], (TILES,), 0, OWN_TILES), jax.random.fold_in(keys[4], 1), 0, OWN_TILES - 1).astype(jnp.int32)
    active_patch_number = draw_active_patch_number(jax.random.fold_in(keys[9], 71), 0)
    prior_reduced_heat_map = jnp.clip(jax.random.uniform(keys[6], (SLAB_STACK_SIZE, MESH_LINES // 16, SITES_ALONG_LINE // 256), jnp.float32, 0.0, 2.0), 0.0, 2.0)
    conductivity_lookup = jnp.clip(jnp.exp(jax.random.uniform(keys[7], (MATERIALS, 3), jnp.float32, math.log(0.02), math.log(0.15))), 0.02, 0.15)
    substance_of_slab = set_ends(jax.random.randint(keys[8], (SLAB_STACK_SIZE,), 0, MATERIALS), jax.random.fold_in(keys[8], 1), 0, MATERIALS - 1).astype(jnp.int32)
    return dict(initial_heat_state=initial_heat_state, dynamic_wattage=dynamic_wattage, drain_multiplier=drain_multiplier, holder_processor=holder_processor, patch_target_slot=patch_target_slot, active_patch_number=active_patch_number, prior_reduced_heat_map=prior_reduced_heat_map, conductivity_lookup=conductivity_lookup, substance_of_slab=substance_of_slab)


LEAK_BETA = 0.7
THERMAL_FACTOR = 0.1


def conductances(conductivity_lookup, substance_of_slab, first, count, total):
    layers = first + jnp.arange(count, dtype=jnp.int32)

    def lookup(index):
        labels = substance_of_slab[jnp.clip(index, 0, total - 1)]
        match = labels[:, None] == jnp.arange(conductivity_lookup.shape[0], dtype=jnp.int32)[None, :]
        return jnp.sum(jnp.where(match[:, :, None], conductivity_lookup[None], jnp.float32(0.0)), axis=1)

    here = lookup(layers)
    above = lookup(layers + 1)
    below = lookup(layers - 1)
    higher_neighbour = 2.0 * here[:, 2] * above[:, 2] / (here[:, 2] + above[:, 2])
    lower_neighbour = 2.0 * here[:, 2] * below[:, 2] / (here[:, 2] + below[:, 2])
    shaped = lambda v: v.reshape(count, 1, 1)
    return shaped(here[:, 0]), shaped(here[:, 1]), shaped(higher_neighbour), shaped(lower_neighbour)


def march_forward(thermal_state, heat_input, horizontal_conductivity, vertical_conductivity, higher_neighbour, lower_neighbour):
    bordered_array = jnp.pad(thermal_state, ((1, 1), (1, 1), (1, 1)))
    horizontal_flux = bordered_array[1:-1, 1:-1, 2:] + bordered_array[1:-1, 1:-1, :-2] - 2.0 * thermal_state
    vertical_flux = bordered_array[1:-1, 2:, 1:-1] + bordered_array[1:-1, :-2, 1:-1] - 2.0 * thermal_state
    heat_flow_higher = bordered_array[2:, 1:-1, 1:-1] - thermal_state
    heat_flow_lower = bordered_array[:-2, 1:-1, 1:-1] - thermal_state
    return thermal_state + horizontal_conductivity * horizontal_flux + vertical_conductivity * vertical_flux + higher_neighbour * heat_flow_higher + lower_neighbour * heat_flow_lower + THERMAL_FACTOR * heat_input


def reference(initial_heat_state, dynamic_wattage, drain_multiplier, holder_processor, patch_target_slot, active_patch_number, prior_reduced_heat_map, conductivity_lookup, substance_of_slab):
    partition_blocks = SITES_ALONG_LINE // 256
    rows_all = SOURCES * TILES_DEV
    position = jnp.arange(rows_all, dtype=jnp.int32)
    device_of = position // TILES_DEV
    live = (position % TILES_DEV) < active_patch_number[device_of]
    owners = holder_processor[:, 0]
    slab_position = (owners % N_SLAB) * CZ + patch_target_slot // (CY * partition_blocks)
    line_position = (owners // N_SLAB) * CY + (patch_target_slot // partition_blocks) % CY
    column_position = patch_target_slot % partition_blocks
    reduced_current = prior_reduced_heat_map[slab_position, line_position // 16, column_position]
    power = (dynamic_wattage.astype(jnp.float32) * (1.0 + drain_multiplier * jnp.exp(LEAK_BETA * reduced_current))[:, None]).astype(jnp.bfloat16)
    total_tiles = SLAB_STACK_SIZE * MESH_LINES * partition_blocks
    index = jnp.where(live, (slab_position * MESH_LINES + line_position) * partition_blocks + column_position, total_tiles).astype(jnp.int32)
    heat_input = jax.ops.segment_sum(power.astype(jnp.float32), index, num_segments=total_tiles + 1)[:total_tiles]
    heat_input = heat_input.reshape(SLAB_STACK_SIZE, MESH_LINES, SITES_ALONG_LINE)
    horizontal_conductivity, vertical_conductivity, higher_neighbour, lower_neighbour = conductances(conductivity_lookup, substance_of_slab, 0, SLAB_STACK_SIZE, SLAB_STACK_SIZE)
    thermal_state = initial_heat_state
    for step in range(STEPS):
        thermal_state = march_forward(thermal_state, heat_input, horizontal_conductivity, vertical_conductivity, higher_neighbour, lower_neighbour)
    reduced_map = thermal_state.reshape(SLAB_STACK_SIZE, MESH_LINES // 16, 16, partition_blocks, 256).mean(axis=(2, 4))
    return thermal_state, reduced_map
```

```python
import functools

import jax
import jax.numpy as jnp
from jax import lax
from jax.experimental import pallas as pl
from jax.experimental.pallas import tpu as pltpu
from jax.sharding import PartitionSpec as P

LEAK_BETA = 0.7
THERMAL_FACTOR = 0.1

DEV = 128
CAP = 32
TILES = 2048
NZ = 8
NY = 64
LAYERS = 128
SLABS = 16
LOGICS = 8
ROWS = 72
GROUP = 16
VMEM = 48 * 1024 * 1024
F32 = jnp.float32
BF16 = jnp.bfloat16
I32 = jnp.int32


def iota(shape, dim):
    return lax.broadcasted_iota(I32, shape, dim)


def pack_kernel(
    count_ref, owner_ref, target_ref, drain_ref, prior_ref, watt_ref, out_ref,
    member_ref, pick_ref, high_ref, low_ref, power_ref,
):
    owner = owner_ref[...]
    target = target_ref[...]
    live = iota((1, TILES), 1) < count_ref[0]
    layer = (owner & (SLABS - 1)) * NZ + (target >> 8)
    column = (owner >> 4) * 16 + ((target >> 6) & 3) * 4 + (target & 3)
    at_layer = jnp.where(iota((LAYERS, TILES), 0) == layer, 1.0, 0.0).astype(BF16)
    prior = prior_ref[...]
    first = prior.astype(BF16)
    rest = prior - first.astype(F32)
    second = rest.astype(BF16)
    third = (rest - second.astype(F32)).astype(BF16)
    lookup = lambda part: lax.dot_general(
        part, at_layer, (((0,), (0,)), ((), ())), preferred_element_type=F32
    )
    picked = lookup(first) + lookup(second) + lookup(third)
    heat = jnp.sum(
        jnp.where(iota((LAYERS, TILES), 0) == column, picked, 0.0), axis=0, keepdims=True
    )
    scale = 1.0 + drain_ref[...] * jnp.exp(LEAK_BETA * heat)
    for b in range(TILES // 128):
        rows = pl.ds(128 * b, 128)
        spread = jnp.transpose(jnp.broadcast_to(scale[:, 128 * b : 128 * b + 128], (128, 128)))
        for h in range(2):
            cols = pl.ds(128 * h, 128)
            power_ref[rows, cols] = (watt_ref[rows, cols].astype(F32) * spread).astype(BF16)
    member = jnp.where(iota((DEV, TILES), 0) == jnp.where(live, owner, -1), 1.0, 0.0)
    member_ref[...] = member
    before = jnp.where(iota((256, 256), 0) < iota((256, 256), 1), 1.0, 0.0).astype(BF16)
    carry = jnp.zeros((DEV, 1), F32)
    ranks = []
    for b in range(TILES // 256):
        part = member[:, 256 * b : 256 * b + 256]
        earlier = jnp.dot(part.astype(BF16), before, preferred_element_type=F32) + carry
        ranks.append(jnp.sum(earlier * part, axis=0, keepdims=True))
        carry = carry + jnp.sum(part, axis=1, keepdims=True)
    rank = jnp.where(live, jnp.concatenate(ranks, axis=1).astype(I32), -1)
    pick_ref[...] = jnp.where(iota((CAP, TILES), 0) == rank, 1.0, 0.0).astype(BF16)
    slot = (iota((128, TILES), 0) & (CAP - 1)) == rank
    flat = member.astype(BF16)
    spot = lambda value: lax.dot_general(
        flat,
        jnp.where(slot, value.astype(F32), 0.0).astype(BF16),
        (((1,), (1,)), ((), ())),
        preferred_element_type=F32,
    )
    high_ref[...] = spot((target >> 6) + 1)
    low_ref[...] = spot(target & 63)
    row8 = iota((8, 128), 0)

    def group(g, _):
        pick = pick_ref[...]
        parts = []
        for j in range(GROUP):
            d = g * GROUP + j
            parts.append(pick * member_ref[pl.ds(d, 1), :].astype(BF16))
            label = jnp.where(
                row8 == 0,
                high_ref[pl.ds(d, 1), :],
                jnp.where(row8 == 1, low_ref[pl.ds(d, 1), :], 0.0),
            )
            out_ref[d, 64:72, :] = label.astype(BF16)
        packed = jnp.dot(
            jnp.concatenate(parts, axis=0), power_ref[...], preferred_element_type=F32
        ).astype(BF16)
        here = pl.ds(g * GROUP, GROUP)
        out_ref[here, 0:32, :] = packed[:, :128].reshape(GROUP, CAP, 128)
        out_ref[here, 32:64, :] = packed[:, 128:].reshape(GROUP, CAP, 128)
        return 0

    lax.fori_loop(0, DEV // GROUP, group, 0)


def scatter_kernel(got_ref, source_ref, low_ref, high_ref, front_ref, back_ref, label_ref):
    labels = got_ref[:, 64:72, :].reshape(DEV * 8, 128)
    row = iota((DEV * 8, 128), 0)
    lane = iota((DEV * 8, 128), 1)
    labels = jnp.where((lane >> 5) == ((row >> 3) & 3), labels.astype(F32), 0.0).astype(BF16)
    g = iota((32, DEV * 8), 0)
    col = iota((32, DEV * 8), 1)
    weight = jnp.where((col & 7) == 0, 64.0, jnp.where((col & 7) == 1, 1.0, 0.0))
    weight = jnp.where((col >> 5) == g, weight, 0.0).astype(BF16)
    target = jnp.dot(weight, labels, preferred_element_type=F32).astype(I32) - 64
    label_ref[...] = target
    left = got_ref[:, 0:32, :].reshape(DEV * CAP, 128)
    right = got_ref[:, 32:64, :].reshape(DEV * CAP, 128)
    both = jnp.concatenate([left, right], axis=1)
    wanted = iota((512, 128), 0) * 4
    for c in range(4):
        chosen = jnp.concatenate(
            [
                jnp.where(wanted == label_ref[k : k + 1, :] - c, 1.0, 0.0).astype(BF16)
                for k in range(32)
            ],
            axis=1,
        )
        total = THERMAL_FACTOR * jnp.dot(chosen, both, preferred_element_type=F32)
        for h in range(2):
            xb = 2 * c + h
            part = total[:, 128 * h : 128 * h + 128]
            cells = part.reshape(NZ * 8, 8, 128)
            source_ref[:, xb] = cells
            short = part.astype(BF16).reshape(NZ * 4, 16, 128)
            low_ref[:, xb] = short[:12]
            high_ref[:, xb] = short[20:]
            for z in range(NZ):
                front_ref[z, xb] = cells[8 * z].astype(BF16)
                back_ref[z, xb] = cells[8 * z + 7].astype(BF16)


def fill_coefficients(coef_ref, table_ref, label_ref, halo):
    base = lax.axis_index("slab") * NZ - halo
    spot = iota((8, 128), 0) * 128 + iota((8, 128), 1)

    def layer(i, _):
        z = base + i
        inside = jnp.where((z >= 0) & (z < LAYERS), 1.0, 0.0).astype(F32)
        material = lambda at: label_ref[jnp.clip(at, 0, LAYERS - 1)]
        here = material(z)
        splat = lambda m, k: jnp.full((8, 128), table_ref[m, k], F32)
        kx = splat(here, 0)
        ky = splat(here, 1)
        a = splat(here, 2)
        above = splat(material(z + 1), 2)
        below = splat(material(z - 1), 2)
        up = 2.0 * a * above / (a + above)
        down = 2.0 * a * below / (a + below)
        keep = jnp.full((8, 128), inside, F32)
        coef_ref[i, 0] = keep * (1.0 - 2.0 * kx - 2.0 * ky - up - down)
        coef_ref[i, 1] = keep * jnp.where(spot == 0, 0.0, kx)
        coef_ref[i, 2] = keep * jnp.where(spot == 1023, 0.0, kx)
        coef_ref[i, 3] = keep * ky
        coef_ref[i, 4] = keep * up
        coef_ref[i, 5] = keep * down
        return 0

    lax.fori_loop(0, NZ + 2 * halo, layer, 0)


def diffuse(coef_ref, read, write, layers, rows, low, high):
    lane = iota((8, 128), 1)

    def layer(z, _):
        coef = [coef_ref[z, j] for j in range(6)]
        before, cell = read(z, rows[0] - 1), read(z, rows[0])
        for y in range(rows[0], rows[1]):
            after = read(z, y + 1)
            step = pltpu.roll(cell, 127, 1)
            right = jnp.where(lane == 127, pltpu.roll(step, 7, 0), step)
            step = pltpu.roll(cell, 1, 1)
            left = jnp.where(lane == 0, pltpu.roll(step, 1, 0), step)
            value = (
                coef[0] * cell
                + coef[1] * left
                + coef[2] * right
                + coef[3] * (before + after)
                + coef[4] * read(z + 1, y)
                + coef[5] * read(z - 1, y)
            )
            if y < 0:
                value = value * low
            if y >= NY:
                value = value * high
            write(z, y, value)
            before, cell = cell, after
        return 0

    lax.fori_loop(layers[0], layers[1], layer, 0)


def edges():
    at = lax.axis_index("logic")
    low = jnp.full((8, 128), jnp.where(at > 0, 1.0, 0.0), F32)
    high = jnp.full((8, 128), jnp.where(at < LOGICS - 1, 1.0, 0.0), F32)
    return low, high


def row_of(z, y, halo):
    return pl.ds(pl.multiple_of((z * (NY + 8) + (y + 4)) * 8, 8), 8)


def temperature_kernel(
    table_ref, label_ref, state_ref, low_ref, high_ref, front_ref, back_ref,
    corner_low_ref, corner_high_ref, out_ref, coef_ref, cells_ref, a_ref, b_ref,
):
    halo = 4
    fill_coefficients(coef_ref, table_ref, label_ref, halo)

    def spread(z, block, value):
        for xb in range(8):
            cells_ref[z, block, pl.ds(xb * 8, 8), :] = value[:, 128 * xb : 128 * xb + 128]

    def gather(z, rows):
        for y in rows:
            block, at = (y + 8) // 8, (y + 8) % 8
            a_ref[row_of(z, y, halo), :] = cells_ref[z, block, pl.ds(at, 8, stride=8), :]

    def own(z, _):
        for block in range(8):
            spread(z + halo, block + 1, state_ref[z, 8 * block : 8 * block + 8, :])
        spread(z + halo, 0, front_ref[z].astype(F32))
        spread(z + halo, 9, back_ref[z].astype(F32))
        gather(z + halo, range(-4, NY + 4))
        return 0

    lax.fori_loop(0, NZ, own, 0)

    def outer(z, _):
        for base, body, corner in ((0, low_ref, corner_low_ref), (12, high_ref, corner_high_ref)):
            for block in range(4):
                two = body[z, 16 * block : 16 * block + 16, :].astype(F32)
                spread(z + base, 2 * block + 1, two[:8])
                spread(z + base, 2 * block + 2, two[8:])
            spread(z + base, 0, corner[0, z].astype(F32))
            spread(z + base, 9, corner[1, z].astype(F32))
            gather(z + base, range(-4, NY + 4))
        return 0

    lax.fori_loop(0, halo, outer, 0)
    low, high = edges()
    bufs = (a_ref, b_ref)
    for step in range(4):
        src, dst = bufs[step % 2], bufs[(step + 1) % 2]
        reach = 3 - step

        def read(z, y, src=src):
            return src[row_of(z, y, halo), :]

        def write(z, y, value, dst=dst, step=step):
            if step == 3:
                out_ref[pl.ds(pl.multiple_of(((z - halo) * NY + y) * 8, 8), 8), :] = value
            else:
                dst[row_of(z, y, halo), :] = value

        diffuse(
            coef_ref, read, write, (halo - reach, halo + NZ + reach), (-reach, NY + reach), low, high
        )


def source_kernel(
    table_ref, label_ref, source_ref, base_ref, low_ref, high_ref, front_ref, back_ref,
    corner_low_ref, corner_high_ref, out_ref, coarse_ref, coef_ref, cells_ref, s_ref, a_ref, b_ref,
    sums_ref,
):
    halo = 3
    fill_coefficients(coef_ref, table_ref, label_ref, halo)

    def gather(z, rows):
        for y in rows:
            block, at = (y + 8) // 8, (y + 8) % 8
            s_ref[row_of(z, y, halo), :] = cells_ref[z, block, pl.ds(at, 8, stride=8), :]

    def own(z, _):
        for y in range(NY):
            start = (z * 8 + y // 8) * 64 + y % 8
            s_ref[row_of(z + halo, y, halo), :] = source_ref[pl.ds(start, 8, stride=8), :]
        for xb in range(8):
            cells_ref[z + halo, 0, pl.ds(xb * 8, 8), :] = front_ref[z, xb].astype(F32)
            cells_ref[z + halo, 9, pl.ds(xb * 8, 8), :] = back_ref[z, xb].astype(F32)
        gather(z + halo, (-3, -2, -1, NY, NY + 1, NY + 2))
        return 0

    lax.fori_loop(0, NZ, own, 0)

    def outer(z, _):
        for base, body, corner in ((0, low_ref, corner_low_ref), (11, high_ref, corner_high_ref)):
            for xb in range(8):
                for block in range(4):
                    two = body[z * 4 + block, xb].astype(F32)
                    cells_ref[z + base, 2 * block + 1, pl.ds(xb * 8, 8), :] = two[:8]
                    cells_ref[z + base, 2 * block + 2, pl.ds(xb * 8, 8), :] = two[8:]
                cells_ref[z + base, 0, pl.ds(xb * 8, 8), :] = corner[0, z, xb].astype(F32)
                cells_ref[z + base, 9, pl.ds(xb * 8, 8), :] = corner[1, z, xb].astype(F32)
            gather(z + base, range(-3, NY + 3))
        return 0

    lax.fori_loop(0, halo, outer, 0)
    low, high = edges()
    for step in range(3):
        src = (s_ref, a_ref, b_ref)[step]
        dst = (a_ref, b_ref, None)[step]
        reach = 2 - step

        def read(z, y, src=src):
            return src[row_of(z, y, halo), :]

        def write(z, y, value, dst=dst, step=step):
            value = value + s_ref[row_of(z, y, halo), :]
            if step < 2:
                dst[row_of(z, y, halo), :] = value
                return
            own = z - halo
            value = value + base_ref[pl.ds(pl.multiple_of((own * NY + y) * 8, 8), 8), :]
            out_ref[own, y // 8, pl.ds(y % 8, 8, stride=8), :] = value
            here = pl.ds(pl.multiple_of((own * 4 + y // 16) * 8, 8), 8)
            if y % 16 == 0:
                sums_ref[here, :] = value
            else:
                sums_ref[here, :] = sums_ref[here, :] + value

        diffuse(
            coef_ref, read, write, (halo - reach, halo + NZ + reach), (-reach, NY + reach), low, high
        )
    exact = lax.Precision.HIGHEST
    lines = lax.dot_general(
        jnp.ones((8, 128), F32), sums_ref[...], (((1,), (1,)), ((), ())),
        precision=exact, preferred_element_type=F32,
    )
    pairs = jnp.where((iota((256, 128), 0) >> 1) == iota((256, 128), 1), 1.0 / 4096.0, 0.0)
    means = jnp.dot(lines, pairs, precision=exact, preferred_element_type=F32)
    coarse_ref[...] = jnp.broadcast_to(means[0:1, :], (DEV, 128))


def vmem(count):
    return [pl.BlockSpec(memory_space=pltpu.VMEM)] * count


def smem(count):
    return [pl.BlockSpec(memory_space=pltpu.SMEM)] * count


def params():
    return pltpu.CompilerParams(vmem_limit_bytes=VMEM)


def cost(flops, moved):
    return pl.CostEstimate(flops=flops, bytes_accessed=moved, transcendentals=0)


def shift(value, axis, by):
    count = lax.axis_size(axis)
    if by > 0:
        pairs = [(i, i + 1) for i in range(count - 1)]
    else:
        pairs = [(i + 1, i) for i in range(count - 1)]
    return lax.ppermute(value, axis, pairs)


def per_device(
    initial_heat_state,
    dynamic_wattage,
    drain_multiplier,
    holder_processor,
    patch_target_slot,
    active_patch_number,
    prior_reduced_heat_map,
    conductivity_lookup,
    substance_of_slab,
):
    state = initial_heat_state
    both = ("logic", "slab")
    shape = jax.ShapeDtypeStruct
    low = shift(state[4:].astype(BF16), "slab", 1)
    high = shift(state[:4].astype(BF16), "slab", -1)
    front = shift(state[:, 56:].astype(BF16), "logic", 1)
    back = shift(state[:, :8].astype(BF16), "logic", -1)
    corner_low = shift(jnp.stack([front[4:], back[4:]]), "slab", 1)
    corner_high = shift(jnp.stack([front[:4], back[:4]]), "slab", -1)

    packed = pl.pallas_call(
        pack_kernel,
        out_shape=shape((DEV, ROWS, 128), BF16),
        in_specs=smem(1) + vmem(5),
        out_specs=pl.BlockSpec(memory_space=pltpu.VMEM),
        scratch_shapes=[
            pltpu.VMEM((DEV, TILES), F32),
            pltpu.VMEM((CAP, TILES), BF16),
            pltpu.VMEM((DEV, 128), F32),
            pltpu.VMEM((DEV, 128), F32),
            pltpu.VMEM((TILES, 256), BF16),
        ],
        compiler_params=params(),
        cost_estimate=cost(5_000_000_000, 4_000_000),
        name="pack",
    )(
        active_patch_number,
        holder_processor.reshape(1, TILES),
        patch_target_slot.reshape(1, TILES),
        drain_multiplier.reshape(1, TILES),
        prior_reduced_heat_map.reshape(LAYERS, 128),
        dynamic_wattage,
    )
    got = lax.all_to_all(packed, both, split_axis=0, concat_axis=0, tiled=True)

    base = pl.pallas_call(
        temperature_kernel,
        out_shape=shape((NZ * NY * 8, 128), F32),
        in_specs=smem(2) + vmem(7),
        out_specs=pl.BlockSpec(memory_space=pltpu.VMEM),
        scratch_shapes=[
            pltpu.VMEM((16, 6, 8, 128), F32),
            pltpu.VMEM((16, 10, 64, 128), F32),
            pltpu.VMEM((16 * 72 * 8, 128), F32),
            pltpu.VMEM((16 * 72 * 8, 128), F32),
        ],
        compiler_params=params(),
        cost_estimate=cost(100_000_000, 20_000_000),
        name="diffuse_temperature",
    )(
        conductivity_lookup, substance_of_slab, state, low, high, front, back, corner_low, corner_high
    )

    source, lower, upper, first, last = pl.pallas_call(
        scatter_kernel,
        out_shape=[
            shape((64, 8, 8, 128), F32),
            shape((12, 8, 16, 128), BF16),
            shape((12, 8, 16, 128), BF16),
            shape((8, 8, 8, 128), BF16),
            shape((8, 8, 8, 128), BF16),
        ],
        in_specs=vmem(1),
        out_specs=vmem(5),
        scratch_shapes=[pltpu.VMEM((32, 128), I32)],
        compiler_params=params(),
        cost_estimate=cost(5_000_000_000, 6_000_000),
        name="place_tiles",
    )(got)
    s_low = shift(upper, "slab", 1)
    s_high = shift(lower, "slab", -1)
    s_front = shift(last, "logic", 1)
    s_back = shift(first, "logic", -1)
    s_corner_low = shift(jnp.stack([s_front[5:], s_back[5:]]), "slab", 1)
    s_corner_high = shift(jnp.stack([s_front[:3], s_back[:3]]), "slab", -1)

    new_state, coarse = pl.pallas_call(
        source_kernel,
        out_shape=[shape((NZ, 8, 64, 128), F32), shape((DEV, 128), F32)],
        in_specs=smem(2) + vmem(8),
        out_specs=vmem(2),
        scratch_shapes=[
            pltpu.VMEM((14, 6, 8, 128), F32),
            pltpu.VMEM((14, 10, 64, 128), F32),
            pltpu.VMEM((14 * 72 * 8, 128), F32),
            pltpu.VMEM((14 * 72 * 8, 128), F32),
            pltpu.VMEM((14 * 72 * 8, 128), F32),
            pltpu.VMEM((256, 128), F32),
        ],
        compiler_params=params(),
        cost_estimate=cost(100_000_000, 20_000_000),
        name="diffuse_source",
    )(
        conductivity_lookup, substance_of_slab, source.reshape(4096, 128), base,
        s_low, s_high, s_front, s_back, s_corner_low, s_corner_high,
    )
    thermal_state = (
        new_state.reshape(NZ, 8, 8, 8, 128).transpose(0, 1, 3, 2, 4).reshape(NZ, NY, 1024)
    )
    gathered = lax.all_to_all(coarse, both, split_axis=0, concat_axis=0, tiled=True)
    reduced_map = gathered.reshape(LOGICS, SLABS, NZ, 4, 4)
    reduced_map = jnp.transpose(reduced_map, (1, 2, 0, 3, 4)).reshape(LAYERS, 32, 4)
    return (thermal_state, reduced_map)


def solution(mesh):
    return jax.shard_map(
        per_device,
        mesh=mesh,
        in_specs=(
            P("slab", "logic", None),
            P(("logic", "slab"), None),
            P(("logic", "slab")),
            P(("logic", "slab"), None),
            P(("logic", "slab")),
            P(("logic", "slab")),
            P(),
            P(),
            P(),
        ),
        out_specs=(P("slab", "logic", None), P()),
        check_vma=False,
    )
```

```python
import functools

import jax
import jax.numpy as jnp
from jax import lax
from jax.experimental import pallas as pl
from jax.experimental.pallas import tpu as pltpu
from jax.sharding import PartitionSpec as P

LEAK_BETA = 0.7
THERMAL_FACTOR = 0.1

DEV = 128
CAP = 32
TILES = 2048
NZ = 8
NY = 64
LAYERS = 128
SLABS = 16
LOGICS = 8
ROWS = 72
GROUP = 16
VMEM = 28 * 1024 * 1024
F32 = jnp.float32
BF16 = jnp.bfloat16
I32 = jnp.int32


def iota(shape, dim):
    return lax.broadcasted_iota(I32, shape, dim)


def edge_kernel(lower_ref, upper_ref, to_high_ref, to_low_ref, first_ref, last_ref):
    to_low_ref[...] = lower_ref[...].astype(BF16)
    to_high_ref[...] = upper_ref[...].astype(BF16)
    for half, ref in ((0, lower_ref), (1, upper_ref)):
        for xb in range(8):
            cols = slice(128 * xb, 128 * xb + 128)
            first_ref[half, 0, xb] = ref[0, :8, cols].astype(BF16)
            last_ref[half, 0, xb] = ref[0, NY - 8 :, cols].astype(BF16)


def corner_kernel(front_ref, back_ref, low_ref, high_ref):
    for side, ref in ((0, front_ref), (1, back_ref)):
        for kind in range(2):
            low_ref[side, kind] = ref[kind, NZ - 3 :]
            high_ref[side, kind] = ref[kind, :3]


def pack_kernel(
    count_ref, owner_hbm, target_hbm, drain_hbm, prior_hbm, watt_hbm, out_hbm,
    owner_ref, target_ref, drain_ref, prior_ref, watt_ref, out_ref,
    member_ref, pick_ref, high_ref, low_ref, power_ref, in_sems, out_sems,
):
    loads = [
        pltpu.make_async_copy(src, dst, in_sems.at[i])
        for i, (src, dst) in enumerate(
            (
                (owner_hbm, owner_ref),
                (target_hbm, target_ref),
                (prior_hbm, prior_ref),
                (drain_hbm, drain_ref),
                (watt_hbm, watt_ref),
            )
        )
    ]
    for load in loads:
        load.start()
    for load in loads[:4]:
        load.wait()
    owner = owner_ref[...]
    target = target_ref[...]
    live = iota((1, TILES), 1) < count_ref[0]
    layer = (owner & (SLABS - 1)) * NZ + (target >> 8)
    column = (owner >> 4) * 16 + ((target >> 6) & 3) * 4 + (target & 3)
    at_layer = jnp.where(iota((LAYERS, TILES), 0) == layer, 1.0, 0.0).astype(BF16)
    prior = prior_ref[...]
    first = prior.astype(BF16)
    rest = prior - first.astype(F32)
    second = rest.astype(BF16)
    third = (rest - second.astype(F32)).astype(BF16)
    lookup = lambda part: lax.dot_general(
        part, at_layer, (((1,), (0,)), ((), ())), preferred_element_type=F32
    )
    picked = lookup(first) + lookup(second) + lookup(third)
    heat = jnp.sum(
        jnp.where(iota((LAYERS, TILES), 0) == column, picked, 0.0), axis=0, keepdims=True
    )
    scale = 1.0 + drain_ref[...] * jnp.exp(LEAK_BETA * heat)
    member = jnp.where(iota((DEV, TILES), 0) == jnp.where(live, owner, -1), 1.0, 0.0)
    member_ref[...] = member
    before = jnp.where(iota((256, 256), 0) < iota((256, 256), 1), 1.0, 0.0).astype(BF16)
    carry = jnp.zeros((DEV, 1), F32)
    ranks = []
    for b in range(TILES // 256):
        part = member[:, 256 * b : 256 * b + 256]
        earlier = jnp.dot(part.astype(BF16), before, preferred_element_type=F32) + carry
        ranks.append(jnp.sum(earlier * part, axis=0, keepdims=True))
        carry = carry + jnp.sum(part, axis=1, keepdims=True)
    rank = jnp.where(live, jnp.concatenate(ranks, axis=1).astype(I32), -1)
    pick_ref[...] = jnp.where(iota((CAP, TILES), 0) == rank, 1.0, 0.0).astype(BF16)
    slot = (iota((128, TILES), 0) & (CAP - 1)) == rank
    flat = member.astype(BF16)
    spot = lambda value: lax.dot_general(
        flat,
        jnp.where(slot, value.astype(F32), 0.0).astype(BF16),
        (((1,), (1,)), ((), ())),
        preferred_element_type=F32,
    )
    high_ref[...] = spot((target >> 6) + 1)
    low_ref[...] = spot(target & 63)
    row8 = iota((8, 128), 0)
    loads[4].wait()
    for b in range(TILES // 128):
        rows = pl.ds(128 * b, 128)
        spread = jnp.transpose(jnp.broadcast_to(scale[:, 128 * b : 128 * b + 128], (128, 128)))
        for h in range(2):
            cols = pl.ds(128 * h, 128)
            power_ref[rows, cols] = (watt_ref[rows, cols].astype(F32) * spread).astype(BF16)

    def store(g):
        here = pl.ds(g * GROUP, GROUP)
        return pltpu.make_async_copy(out_ref.at[here], out_hbm.at[here], out_sems.at[g])

    def group(g, _):
        pick = pick_ref[...]
        parts = []
        for j in range(GROUP):
            d = g * GROUP + j
            parts.append(pick * member_ref[pl.ds(d, 1), :].astype(BF16))
            label = jnp.where(
                row8 == 0,
                high_ref[pl.ds(d, 1), :],
                jnp.where(row8 == 1, low_ref[pl.ds(d, 1), :], 0.0),
            )
            out_ref[d, 64:72, :] = label.astype(BF16)
        packed = jnp.dot(
            jnp.concatenate(parts, axis=0), power_ref[...], preferred_element_type=F32
        ).astype(BF16)
        here = pl.ds(g * GROUP, GROUP)
        out_ref[here, 0:32, :] = packed[:, :128].reshape(GROUP, CAP, 128)
        out_ref[here, 32:64, :] = packed[:, 128:].reshape(GROUP, CAP, 128)
        store(g).start()
        return 0

    lax.fori_loop(0, DEV // GROUP, group, 0)
    for g in range(DEV // GROUP):
        store(g).wait()


def scatter_kernel(
    got_ref, first_ref, last_ref, source_ref, low_ref, high_ref, front_ref, back_ref, label_ref,
):
    labels = got_ref[:, 64:72, :].reshape(DEV * 8, 128)
    row = iota((DEV * 8, 128), 0)
    lane = iota((DEV * 8, 128), 1)
    labels = jnp.where((lane >> 5) == ((row >> 3) & 3), labels.astype(F32), 0.0).astype(BF16)
    g = iota((32, DEV * 8), 0)
    col = iota((32, DEV * 8), 1)
    weight = jnp.where((col & 7) == 0, 64.0, jnp.where((col & 7) == 1, 1.0, 0.0))
    weight = jnp.where((col >> 5) == g, weight, 0.0).astype(BF16)
    target = jnp.dot(weight, labels, preferred_element_type=F32).astype(I32) - 64
    label_ref[...] = target
    left = got_ref[:, 0:32, :].reshape(DEV * CAP, 128)
    right = got_ref[:, 32:64, :].reshape(DEV * CAP, 128)
    both = jnp.concatenate([left, right], axis=1)
    wanted = iota((512, 128), 0) * 4
    for c in range(4):
        chosen = jnp.concatenate(
            [
                jnp.where(wanted == label_ref[k : k + 1, :] - c, 1.0, 0.0).astype(BF16)
                for k in range(32)
            ],
            axis=1,
        )
        total = THERMAL_FACTOR * jnp.dot(chosen, both, preferred_element_type=F32)
        for h in range(2):
            xb = 2 * c + h
            part = total[:, 128 * h : 128 * h + 128]
            cells = part.reshape(NZ * 8, 8, 128)
            source_ref[:, xb] = cells
            short = part.astype(BF16).reshape(NZ * 4, 16, 128)
            low_ref[:, xb] = short[:12]
            high_ref[:, xb] = short[20:]
            for z in range(NZ):
                front_ref[0, z, xb] = cells[8 * z].astype(BF16)
                back_ref[0, z, xb] = cells[8 * z + 7].astype(BF16)
    front_ref[1] = first_ref[...]
    back_ref[1] = last_ref[...]


def fill_coefficients(coef_ref, table_ref, label_ref, halo):
    base = lax.axis_index("slab") * NZ - halo
    spot = iota((8, 128), 0) * 128 + iota((8, 128), 1)

    def layer(i, _):
        z = base + i
        inside = jnp.where((z >= 0) & (z < LAYERS), 1.0, 0.0).astype(F32)
        material = lambda at: label_ref[jnp.clip(at, 0, LAYERS - 1)]
        here = material(z)
        splat = lambda m, k: jnp.full((8, 128), table_ref[m, k], F32)
        kx = splat(here, 0)
        ky = splat(here, 1)
        a = splat(here, 2)
        above = splat(material(z + 1), 2)
        below = splat(material(z - 1), 2)
        up = 2.0 * a * above / (a + above)
        down = 2.0 * a * below / (a + below)
        keep = jnp.full((8, 128), inside, F32)
        coef_ref[i, 0] = keep * (1.0 - 2.0 * kx - 2.0 * ky - up - down)
        coef_ref[i, 1] = keep * jnp.where(spot == 0, 0.0, kx)
        coef_ref[i, 2] = keep * jnp.where(spot == 1023, 0.0, kx)
        coef_ref[i, 3] = keep * ky
        coef_ref[i, 4] = keep * up
        coef_ref[i, 5] = keep * down
        return 0

    lax.fori_loop(0, NZ + 2 * halo, layer, 0)


def diffuse(coef_ref, read, write, layers, rows, low, high):
    lane = iota((8, 128), 1)

    def layer(z, _):
        coef = [coef_ref[z, j] for j in range(6)]
        before, cell = read(z, rows[0] - 1), read(z, rows[0])
        for y in range(rows[0], rows[1]):
            after = read(z, y + 1)
            step = pltpu.roll(cell, 127, 1)
            right = jnp.where(lane == 127, pltpu.roll(step, 7, 0), step)
            step = pltpu.roll(cell, 1, 1)
            left = jnp.where(lane == 0, pltpu.roll(step, 1, 0), step)
            value = (
                coef[0] * cell
                + coef[1] * left
                + coef[2] * right
                + coef[3] * (before + after)
                + coef[4] * read(z + 1, y)
                + coef[5] * read(z - 1, y)
            )
            if y < 0:
                value = value * low
            if y >= NY:
                value = value * high
            write(z, y, value)
            before, cell = cell, after
        return 0

    lax.fori_loop(layers[0], layers[1], layer, 0)


def edges():
    at = lax.axis_index("logic")
    low = jnp.full((8, 128), jnp.where(at > 0, 1.0, 0.0), F32)
    high = jnp.full((8, 128), jnp.where(at < LOGICS - 1, 1.0, 0.0), F32)
    return low, high


def row_of(z, y, halo):
    return pl.ds(pl.multiple_of((z * (NY + 8) + (y + 4)) * 8, 8), 8)


def temperature_kernel(
    table_ref, label_ref, state_ref, low_ref, high_ref, out_ref, coef_ref, cells_ref, a_ref, b_ref,
):
    halo = 4
    fill_coefficients(coef_ref, table_ref, label_ref, halo)

    def spread(z, block, value):
        for xb in range(8):
            cells_ref[z, block, pl.ds(xb * 8, 8), :] = value[:, 128 * xb : 128 * xb + 128]

    def gather(z):
        for y in range(NY):
            a_ref[row_of(z, y, halo), :] = cells_ref[z, y // 8, pl.ds(y % 8, 8, stride=8), :]

    def clear(z, _):
        for y in (-3, -2, -1, NY, NY + 1, NY + 2):
            a_ref[row_of(z, y, halo), :] = jnp.zeros((8, 128), F32)
            b_ref[row_of(z, y, halo), :] = jnp.zeros((8, 128), F32)
        return 0

    lax.fori_loop(0, NZ + 2 * halo, clear, 0)

    def own(z, _):
        for block in range(8):
            spread(z + halo, block, state_ref[z, 8 * block : 8 * block + 8, :])
        gather(z + halo)
        return 0

    lax.fori_loop(0, NZ, own, 0)

    def outer(z, _):
        for base, body in ((0, low_ref), (12, high_ref)):
            for block in range(4):
                two = body[z, 16 * block : 16 * block + 16, :].astype(F32)
                spread(z + base, 2 * block, two[:8])
                spread(z + base, 2 * block + 1, two[8:])
            gather(z + base)
        return 0

    lax.fori_loop(0, halo, outer, 0)
    low, high = edges()
    bufs = (a_ref, b_ref)
    for step in range(4):
        src, dst = bufs[step % 2], bufs[(step + 1) % 2]
        reach = 3 - step
        wide = (1, 2, 1, 0)[step]

        def read(z, y, src=src):
            return src[row_of(z, y, halo), :]

        def write(z, y, value, dst=dst, step=step):
            if step == 3:
                out_ref[pl.ds(pl.multiple_of(((z - halo) * NY + y) * 8, 8), 8), :] = value
            else:
                dst[row_of(z, y, halo), :] = value

        diffuse(
            coef_ref, read, write, (halo - reach, halo + NZ + reach), (-wide, NY + wide), low, high
        )


def source_kernel(
    table_ref, label_ref, source_ref, base_ref, low_ref, high_ref, front_ref, back_ref,
    corner_low_ref, corner_high_ref, out_ref, coarse_ref,
    coef_ref, cells_ref, s_ref, a_ref, b_ref, rim_ref, edge_ref, sums_ref,
):
    halo = 3
    fill_coefficients(coef_ref, table_ref, label_ref, halo)
    zero = jnp.zeros((8, 128), F32)

    def rim_at(z, y):
        slot = y + 4 if y < 1 else y - NY + 6
        return pl.ds(pl.multiple_of(((z + 1) * 10 + slot) * 8, 8), 8)

    def edge_at(z, y):
        slot = y + 3 if y < 1 else y - NY + 5
        return pl.ds(pl.multiple_of((z * 8 + slot) * 8, 8), 8)

    def strips(z, front, back):
        for xb in range(8):
            for kind in range(2):
                cells_ref[kind, pl.ds(xb * 8, 8), :] = front(kind, xb).astype(F32)
                cells_ref[2 + kind, pl.ds(xb * 8, 8), :] = back(kind, xb).astype(F32)
        for at in range(4):
            if at:
                s_ref[row_of(z, at - 4, halo), :] = cells_ref[0, pl.ds(4 + at, 8, stride=8), :]
            rim_ref[rim_at(z, at - 4), :] = cells_ref[1, pl.ds(4 + at, 8, stride=8), :]
            if at < 3:
                s_ref[row_of(z, NY + at, halo), :] = cells_ref[2, pl.ds(at, 8, stride=8), :]
            rim_ref[rim_at(z, NY + at), :] = cells_ref[3, pl.ds(at, 8, stride=8), :]

    rim_ref[pl.ds(0, 80), :] = jnp.zeros((80, 128), F32)
    rim_ref[pl.ds(15 * 80, 80), :] = jnp.zeros((80, 128), F32)

    def own(z, _):
        for y in range(NY):
            start = (z * 8 + y // 8) * 64 + y % 8
            s_ref[row_of(z + halo, y, halo), :] = source_ref[pl.ds(start, 8, stride=8), :]
        strips(
            z + halo, lambda kind, xb: front_ref[kind, z, xb], lambda kind, xb: back_ref[kind, z, xb]
        )
        return 0

    lax.fori_loop(0, NZ, own, 0)

    def outer(z, _):
        for base, body, corner in ((0, low_ref, corner_low_ref), (11, high_ref, corner_high_ref)):
            for block in range(4):
                for xb in range(8):
                    two = body[z * 4 + block, xb].astype(F32)
                    cells_ref[4, pl.ds(xb * 8, 8), :] = two[:8]
                    cells_ref[5, pl.ds(xb * 8, 8), :] = two[8:]
                for y in range(16):
                    s_ref[row_of(z + base, 16 * block + y, halo), :] = cells_ref[
                        4 + y // 8, pl.ds(y % 8, 8, stride=8), :
                    ]
            strips(
                z + base,
                lambda kind, xb: corner[0, kind, z, xb],
                lambda kind, xb: corner[1, kind, z, xb],
            )
        return 0

    lax.fori_loop(0, halo, outer, 0)
    low, high = edges()

    def read_rim(z, y):
        return rim_ref[rim_at(z, y), :]

    def write_edge(z, y, value):
        edge_ref[edge_at(z, y), :] = value + s_ref[row_of(z, y, halo), :]

    def sides(z, _):
        rim_ref[rim_at(z, 0), :] = zero
        rim_ref[rim_at(z, NY - 1), :] = zero
        ky = coef_ref[z, 3]
        write_edge(z, 0, ky * read_rim(z, -1))
        write_edge(z, NY - 1, ky * read_rim(z, NY))
        return 0

    lax.fori_loop(0, NZ + 2 * halo, sides, 0)
    diffuse(coef_ref, read_rim, write_edge, (0, NZ + 2 * halo), (-3, 0), low, high)
    diffuse(coef_ref, read_rim, write_edge, (0, NZ + 2 * halo), (NY, NY + 3), low, high)
    for step in range(3):
        src = (None, a_ref, b_ref)[step]
        dst = (a_ref, b_ref, None)[step]
        reach = 2 - step

        def read(z, y, src=src):
            if src is None:
                if 1 <= y < NY - 1:
                    return s_ref[row_of(z, y, halo), :]
                return edge_ref[edge_at(z, y), :]
            return src[row_of(z, y, halo), :]

        def write(z, y, value, dst=dst, step=step):
            value = value + s_ref[row_of(z, y, halo), :]
            if step < 2:
                dst[row_of(z, y, halo), :] = value
                return
            own = z - halo
            value = value + base_ref[pl.ds(pl.multiple_of((own * NY + y) * 8, 8), 8), :]
            out_ref[own, y // 8, pl.ds(y % 8, 8, stride=8), :] = value
            here = pl.ds(pl.multiple_of((own * 4 + y // 16) * 8, 8), 8)
            if y % 16 == 0:
                sums_ref[here, :] = value
            else:
                sums_ref[here, :] = sums_ref[here, :] + value

        diffuse(
            coef_ref, read, write, (halo - reach, halo + NZ + reach), (-reach, NY + reach), low, high
        )
    exact = lax.Precision.HIGHEST
    lines = lax.dot_general(
        jnp.ones((8, 128), F32), sums_ref[...], (((1,), (1,)), ((), ())),
        precision=exact, preferred_element_type=F32,
    )
    pairs = jnp.where((iota((256, 128), 0) >> 1) == iota((256, 128), 1), 1.0 / 4096.0, 0.0)
    means = jnp.dot(lines, pairs, precision=exact, preferred_element_type=F32)
    coarse_ref[...] = jnp.broadcast_to(means[0:1, :], (DEV, 128))


def vmem(count):
    return [pl.BlockSpec(memory_space=pltpu.VMEM)] * count


def smem(count):
    return [pl.BlockSpec(memory_space=pltpu.SMEM)] * count


def params():
    return pltpu.CompilerParams(vmem_limit_bytes=VMEM)


def cost(flops, moved):
    return pl.CostEstimate(flops=flops, bytes_accessed=moved, transcendentals=0)


def shift(value, axis, by):
    count = lax.axis_size(axis)
    if by > 0:
        pairs = [(i, i + 1) for i in range(count - 1)]
    else:
        pairs = [(i + 1, i) for i in range(count - 1)]
    return lax.ppermute(value, axis, pairs)


def per_device(
    initial_heat_state,
    dynamic_wattage,
    drain_multiplier,
    holder_processor,
    patch_target_slot,
    active_patch_number,
    prior_reduced_heat_map,
    conductivity_lookup,
    substance_of_slab,
):
    state = initial_heat_state
    both = ("logic", "slab")
    shape = jax.ShapeDtypeStruct
    to_high, to_low, t_first, t_last = pl.pallas_call(
        edge_kernel,
        grid=(NZ // 2,),
        out_shape=[
            shape((4, NY, 1024), BF16),
            shape((4, NY, 1024), BF16),
            shape((2, 4, 8, 8, 128), BF16),
            shape((2, 4, 8, 8, 128), BF16),
        ],
        in_specs=[
            pl.BlockSpec((1, NY, 1024), lambda i: (i, 0, 0)),
            pl.BlockSpec((1, NY, 1024), lambda i: (i + NZ // 2, 0, 0)),
        ],
        out_specs=[
            pl.BlockSpec((1, NY, 1024), lambda i: (i, 0, 0)),
            pl.BlockSpec((1, NY, 1024), lambda i: (i, 0, 0)),
            pl.BlockSpec((2, 1, 8, 8, 128), lambda i: (0, i, 0, 0, 0)),
            pl.BlockSpec((2, 1, 8, 8, 128), lambda i: (0, i, 0, 0, 0)),
        ],
        compiler_params=params(),
        cost_estimate=cost(1_000_000, 5_000_000),
        name="edges",
    )(state, state)
    low = shift(to_high, "slab", 1)
    high = shift(to_low, "slab", -1)

    packed = pl.pallas_call(
        pack_kernel,
        out_shape=shape((DEV, ROWS, 128), BF16),
        in_specs=smem(1) + [pl.BlockSpec(memory_space=pltpu.HBM)] * 5,
        out_specs=pl.BlockSpec(memory_space=pltpu.HBM),
        scratch_shapes=[
            pltpu.VMEM((1, TILES), I32),
            pltpu.VMEM((1, TILES), I32),
            pltpu.VMEM((1, TILES), F32),
            pltpu.VMEM((LAYERS, 128), F32),
            pltpu.VMEM((TILES, 256), BF16),
            pltpu.VMEM((DEV, ROWS, 128), BF16),
            pltpu.VMEM((DEV, TILES), F32),
            pltpu.VMEM((CAP, TILES), BF16),
            pltpu.VMEM((DEV, 128), F32),
            pltpu.VMEM((DEV, 128), F32),
            pltpu.VMEM((TILES, 256), BF16),
            pltpu.SemaphoreType.DMA((5,)),
            pltpu.SemaphoreType.DMA((DEV // GROUP,)),
        ],
        compiler_params=params(),
        cost_estimate=cost(5_000_000_000, 4_000_000),
        name="pack",
    )(
        active_patch_number,
        holder_processor.reshape(1, TILES),
        patch_target_slot.reshape(1, TILES),
        drain_multiplier.reshape(1, TILES),
        prior_reduced_heat_map.transpose(1, 2, 0).reshape(128, LAYERS),
        dynamic_wattage,
    )
    packed, low, high = lax.optimization_barrier((packed, low, high))
    got = lax.all_to_all(packed, both, split_axis=0, concat_axis=0, tiled=True)

    base = pl.pallas_call(
        temperature_kernel,
        out_shape=shape((NZ * NY * 8, 128), F32),
        in_specs=smem(2) + vmem(3),
        out_specs=pl.BlockSpec(memory_space=pltpu.VMEM),
        scratch_shapes=[
            pltpu.VMEM((16, 6, 8, 128), F32),
            pltpu.VMEM((16, 8, 64, 128), F32),
            pltpu.VMEM((16 * 72 * 8, 128), F32),
            pltpu.VMEM((16 * 72 * 8, 128), F32),
        ],
        compiler_params=params(),
        cost_estimate=cost(100_000_000, 20_000_000),
        name="diffuse_temperature",
    )(conductivity_lookup, substance_of_slab, state, low, high)
    got, base = lax.optimization_barrier((got, base))

    source, lower, upper, first, last = pl.pallas_call(
        scatter_kernel,
        out_shape=[
            shape((64, 8, 8, 128), F32),
            shape((12, 8, 16, 128), BF16),
            shape((12, 8, 16, 128), BF16),
            shape((2, NZ, 8, 8, 128), BF16),
            shape((2, NZ, 8, 8, 128), BF16),
        ],
        in_specs=vmem(3),
        out_specs=vmem(5),
        scratch_shapes=[pltpu.VMEM((32, 128), I32)],
        compiler_params=params(),
        cost_estimate=cost(5_000_000_000, 6_000_000),
        name="place_tiles",
    )(got, t_first.reshape(NZ, 8, 8, 128), t_last.reshape(NZ, 8, 8, 128))
    s_low = shift(upper, "slab", 1)
    s_high = shift(lower, "slab", -1)
    s_front = shift(last, "logic", 1)
    s_back = shift(first, "logic", -1)
    to_high, to_low = pl.pallas_call(
        corner_kernel,
        out_shape=[shape((2, 2, 3, 8, 8, 128), BF16)] * 2,
        in_specs=vmem(2),
        out_specs=vmem(2),
        compiler_params=params(),
        cost_estimate=cost(1_000_000, 1_000_000),
        name="corners",
    )(s_front, s_back)
    s_corner_low = shift(to_high, "slab", 1)
    s_corner_high = shift(to_low, "slab", -1)

    new_state, coarse = pl.pallas_call(
        source_kernel,
        out_shape=[shape((NZ, 8, 64, 128), F32), shape((DEV, 128), F32)],
        in_specs=smem(2) + vmem(8),
        out_specs=vmem(2),
        scratch_shapes=[
            pltpu.VMEM((14, 6, 8, 128), F32),
            pltpu.VMEM((6, 64, 128), F32),
            pltpu.VMEM((14 * 72 * 8, 128), F32),
            pltpu.VMEM((14 * 72 * 8, 128), F32),
            pltpu.VMEM((14 * 72 * 8, 128), F32),
            pltpu.VMEM((16 * 80, 128), F32),
            pltpu.VMEM((14 * 64, 128), F32),
            pltpu.VMEM((256, 128), F32),
        ],
        compiler_params=params(),
        cost_estimate=cost(100_000_000, 20_000_000),
        name="diffuse_source",
    )(
        conductivity_lookup, substance_of_slab, source.reshape(4096, 128), base,
        s_low, s_high, s_front, s_back, s_corner_low, s_corner_high,
    )
    thermal_state = (
        new_state.reshape(NZ, 8, 8, 8, 128).transpose(0, 1, 3, 2, 4).reshape(NZ, NY, 1024)
    )
    gathered = lax.all_to_all(coarse, both, split_axis=0, concat_axis=0, tiled=True)
    reduced_map = gathered.reshape(LOGICS, SLABS, NZ, 4, 4)
    reduced_map = jnp.transpose(reduced_map, (1, 2, 0, 3, 4)).reshape(LAYERS, 32, 4)
    return (thermal_state, reduced_map)


def solution(mesh):
    return jax.shard_map(
        per_device,
        mesh=mesh,
        in_specs=(
            P("slab", "logic", None),
            P(("logic", "slab"), None),
            P(("logic", "slab")),
            P(("logic", "slab"), None),
            P(("logic", "slab")),
            P(("logic", "slab")),
            P(),
            P(),
            P(),
        ),
        out_specs=(P("slab", "logic", None), P()),
        check_vma=False,
    )
```

```python
import functools

import jax
import jax.numpy as jnp
from jax import lax
from jax.experimental import pallas as pl
from jax.experimental.pallas import tpu as pltpu
from jax.sharding import PartitionSpec as P

LEAK_BETA = 0.7
THERMAL_FACTOR = 0.1

DEV = 128
CAP = 32
TILES = 2048
NZ = 8
NY = 64
LAYERS = 128
SLABS = 16
LOGICS = 8
ROWS = 72
GROUP = 16
VMEM = 28 * 1024 * 1024
F32 = jnp.float32
BF16 = jnp.bfloat16
I32 = jnp.int32


def iota(shape, dim):
    return lax.broadcasted_iota(I32, shape, dim)


def edge_kernel(lower_ref, upper_ref, to_high_ref, to_low_ref, first_ref, last_ref):
    to_low_ref[...] = lower_ref[...].astype(BF16)
    to_high_ref[...] = upper_ref[...].astype(BF16)
    for half, ref in ((0, lower_ref), (1, upper_ref)):
        for xb in range(8):
            cols = slice(128 * xb, 128 * xb + 128)
            first_ref[half, 0, xb] = ref[0, :8, cols].astype(BF16)
            last_ref[half, 0, xb] = ref[0, NY - 8 :, cols].astype(BF16)


def corner_kernel(front_ref, back_ref, low_ref, high_ref):
    for out, first in ((low_ref, NZ - 3), (high_ref, 0)):
        for z in range(3):
            for xb in range(8):
                out[z, xb] = jnp.concatenate(
                    [front_ref[first + z, xb].astype(F32), back_ref[first + z, xb].astype(F32)], axis=0
                ).astype(BF16)


def pack_kernel(
    count_ref, owner_hbm, target_hbm, drain_hbm, prior_hbm, watt_hbm, out_hbm,
    owner_ref, target_ref, drain_ref, prior_ref, watt_ref, out_ref,
    member_ref, pick_ref, high_ref, low_ref, power_ref, in_sems, out_sems,
):
    loads = [
        pltpu.make_async_copy(src, dst, in_sems.at[i])
        for i, (src, dst) in enumerate(
            (
                (owner_hbm, owner_ref),
                (target_hbm, target_ref),
                (prior_hbm, prior_ref),
                (drain_hbm, drain_ref),
                (watt_hbm, watt_ref),
            )
        )
    ]
    for load in loads:
        load.start()
    for load in loads[:4]:
        load.wait()
    owner = owner_ref[...]
    target = target_ref[...]
    live = iota((1, TILES), 1) < count_ref[0]
    layer = (owner & (SLABS - 1)) * NZ + (target >> 8)
    column = (owner >> 4) * 16 + ((target >> 6) & 3) * 4 + (target & 3)
    at_layer = jnp.where(iota((LAYERS, TILES), 0) == layer, 1.0, 0.0).astype(BF16)
    prior = prior_ref[...]
    first = prior.astype(BF16)
    rest = prior - first.astype(F32)
    second = rest.astype(BF16)
    third = (rest - second.astype(F32)).astype(BF16)
    lookup = lambda part: lax.dot_general(
        part, at_layer, (((1,), (0,)), ((), ())), preferred_element_type=F32
    )
    picked = lookup(first) + lookup(second) + lookup(third)
    heat = jnp.sum(
        jnp.where(iota((LAYERS, TILES), 0) == column, picked, 0.0), axis=0, keepdims=True
    )
    scale = 1.0 + drain_ref[...] * jnp.exp(LEAK_BETA * heat)
    member = jnp.where(iota((DEV, TILES), 0) == jnp.where(live, owner, -1), 1.0, 0.0)
    member_ref[...] = member
    before = jnp.where(iota((256, 256), 0) < iota((256, 256), 1), 1.0, 0.0).astype(BF16)
    carry = jnp.zeros((DEV, 1), F32)
    ranks = []
    for b in range(TILES // 256):
        part = member[:, 256 * b : 256 * b + 256]
        earlier = jnp.dot(part.astype(BF16), before, preferred_element_type=F32) + carry
        ranks.append(jnp.sum(earlier * part, axis=0, keepdims=True))
        carry = carry + jnp.sum(part, axis=1, keepdims=True)
    rank = jnp.where(live, jnp.concatenate(ranks, axis=1).astype(I32), -1)
    pick_ref[...] = jnp.where(iota((CAP, TILES), 0) == rank, 1.0, 0.0).astype(BF16)
    slot = (iota((128, TILES), 0) & (CAP - 1)) == rank
    flat = member.astype(BF16)
    spot = lambda value: lax.dot_general(
        flat,
        jnp.where(slot, value.astype(F32), 0.0).astype(BF16),
        (((1,), (1,)), ((), ())),
        preferred_element_type=F32,
    )
    high_ref[...] = spot((target >> 6) + 1)
    low_ref[...] = spot(target & 63)
    row8 = iota((8, 128), 0)
    loads[4].wait()
    for b in range(TILES // 128):
        rows = pl.ds(128 * b, 128)
        spread = jnp.transpose(jnp.broadcast_to(scale[:, 128 * b : 128 * b + 128], (128, 128)))
        for h in range(2):
            cols = pl.ds(128 * h, 128)
            power_ref[rows, cols] = (watt_ref[rows, cols].astype(F32) * spread).astype(BF16)

    def store(g):
        here = pl.ds(g * GROUP, GROUP)
        return pltpu.make_async_copy(out_ref.at[here], out_hbm.at[here], out_sems.at[g])

    def group(g, _):
        pick = pick_ref[...]
        parts = []
        for j in range(GROUP):
            d = g * GROUP + j
            parts.append(pick * member_ref[pl.ds(d, 1), :].astype(BF16))
            label = jnp.where(
                row8 == 0,
                high_ref[pl.ds(d, 1), :],
                jnp.where(row8 == 1, low_ref[pl.ds(d, 1), :], 0.0),
            )
            out_ref[d, 64:72, :] = label.astype(BF16)
        packed = jnp.dot(
            jnp.concatenate(parts, axis=0), power_ref[...], preferred_element_type=F32
        ).astype(BF16)
        here = pl.ds(g * GROUP, GROUP)
        out_ref[here, 0:32, :] = packed[:, :128].reshape(GROUP, CAP, 128)
        out_ref[here, 32:64, :] = packed[:, 128:].reshape(GROUP, CAP, 128)
        store(g).start()
        return 0

    lax.fori_loop(0, DEV // GROUP, group, 0)
    for g in range(DEV // GROUP):
        store(g).wait()


def scatter_kernel(
    got_ref, first_ref, last_ref, source_ref, low_ref, high_ref, front_ref, back_ref, label_ref,
):
    labels = got_ref[:, 64:72, :].reshape(DEV * 8, 128)
    row = iota((DEV * 8, 128), 0)
    lane = iota((DEV * 8, 128), 1)
    labels = jnp.where((lane >> 5) == ((row >> 3) & 3), labels.astype(F32), 0.0).astype(BF16)
    g = iota((32, DEV * 8), 0)
    col = iota((32, DEV * 8), 1)
    weight = jnp.where((col & 7) == 0, 64.0, jnp.where((col & 7) == 1, 1.0, 0.0))
    weight = jnp.where((col >> 5) == g, weight, 0.0).astype(BF16)
    target = jnp.dot(weight, labels, preferred_element_type=F32).astype(I32) - 64
    label_ref[...] = target
    left = got_ref[:, 0:32, :].reshape(DEV * CAP, 128)
    right = got_ref[:, 32:64, :].reshape(DEV * CAP, 128)
    both = jnp.concatenate([left, right], axis=1)
    wanted = iota((512, 128), 0) * 4
    upper = iota((8, 128), 0) < 4
    for c in range(4):
        chosen = jnp.concatenate(
            [
                jnp.where(wanted == label_ref[k : k + 1, :] - c, 1.0, 0.0).astype(BF16)
                for k in range(32)
            ],
            axis=1,
        )
        total = THERMAL_FACTOR * jnp.dot(chosen, both, preferred_element_type=F32)
        for h in range(2):
            xb = 2 * c + h
            part = total[:, 128 * h : 128 * h + 128]
            cells = part.reshape(NZ * 8, 8, 128)
            source_ref[:, xb] = cells
            short = part.astype(BF16).reshape(NZ * 4, 16, 128)
            low_ref[:, xb] = short[:12]
            high_ref[:, xb] = short[20:]
            for z in range(NZ):
                front_ref[z, xb] = jnp.where(
                    upper, first_ref[z, xb].astype(F32), pltpu.roll(cells[8 * z], 4, 0)
                ).astype(BF16)
                back_ref[z, xb] = jnp.where(
                    upper, pltpu.roll(cells[8 * z + 7], 4, 0), last_ref[z, xb].astype(F32)
                ).astype(BF16)


def fill_coefficients(coef_ref, table_ref, label_ref, halo):
    base = lax.axis_index("slab") * NZ - halo
    spot = iota((8, 128), 0) * 128 + iota((8, 128), 1)

    def layer(i, _):
        z = base + i
        inside = jnp.where((z >= 0) & (z < LAYERS), 1.0, 0.0).astype(F32)
        material = lambda at: label_ref[jnp.clip(at, 0, LAYERS - 1)]
        here = material(z)
        splat = lambda m, k: jnp.full((8, 128), table_ref[m, k], F32)
        kx = splat(here, 0)
        ky = splat(here, 1)
        a = splat(here, 2)
        above = splat(material(z + 1), 2)
        below = splat(material(z - 1), 2)
        up = 2.0 * a * above / (a + above)
        down = 2.0 * a * below / (a + below)
        keep = jnp.full((8, 128), inside, F32)
        coef_ref[i, 0] = keep * (1.0 - 2.0 * kx - 2.0 * ky - up - down)
        coef_ref[i, 1] = keep * jnp.where(spot == 0, 0.0, kx)
        coef_ref[i, 2] = keep * jnp.where(spot == 1023, 0.0, kx)
        coef_ref[i, 3] = keep * ky
        coef_ref[i, 4] = keep * up
        coef_ref[i, 5] = keep * down
        return 0

    lax.fori_loop(0, NZ + 2 * halo, layer, 0)


def diffuse(coef_ref, read, write, layers, rows, low, high):
    lane = iota((8, 128), 1)

    def layer(z, _):
        coef = [coef_ref[z, j] for j in range(6)]
        before, cell = read(z, rows[0] - 1), read(z, rows[0])
        for y in range(rows[0], rows[1]):
            after = read(z, y + 1)
            step = pltpu.roll(cell, 127, 1)
            right = jnp.where(lane == 127, pltpu.roll(step, 7, 0), step)
            step = pltpu.roll(cell, 1, 1)
            left = jnp.where(lane == 0, pltpu.roll(step, 1, 0), step)
            value = (
                coef[0] * cell
                + coef[1] * left
                + coef[2] * right
                + coef[3] * (before + after)
                + coef[4] * read(z + 1, y)
                + coef[5] * read(z - 1, y)
            )
            if y < 0:
                value = value * low
            if y >= NY:
                value = value * high
            write(z, y, value)
            before, cell = cell, after
        return 0

    lax.fori_loop(layers[0], layers[1], layer, 0)


def edges(axis, count):
    at = lax.axis_index(axis)
    low = jnp.full((8, 128), jnp.where(at > 0, 1.0, 0.0), F32)
    high = jnp.full((8, 128), jnp.where(at < count - 1, 1.0, 0.0), F32)
    return low, high


def row_of(z, y, halo):
    return pl.ds(pl.multiple_of((z * (NY + 8) + (y + 4)) * 8, 8), 8)


def temperature_kernel(
    table_ref, label_ref, state_ref, low_ref, high_ref, out_ref, coef_ref, cells_ref, a_ref, b_ref,
):
    halo = 4
    fill_coefficients(coef_ref, table_ref, label_ref, halo)

    def spread(z, block, value):
        for xb in range(8):
            cells_ref[z, block, pl.ds(xb * 8, 8), :] = value[:, 128 * xb : 128 * xb + 128]

    def gather(z, keep=None):
        for y in range(NY):
            value = cells_ref[z, y // 8, pl.ds(y % 8, 8, stride=8), :]
            a_ref[row_of(z, y, halo), :] = value if keep is None else value * keep

    def clear(z, _):
        for y in (-3, -2, -1, NY, NY + 1, NY + 2):
            a_ref[row_of(z, y, halo), :] = jnp.zeros((8, 128), F32)
            b_ref[row_of(z, y, halo), :] = jnp.zeros((8, 128), F32)
        return 0

    lax.fori_loop(0, NZ + 2 * halo, clear, 0)

    def own(z, _):
        for block in range(8):
            spread(z + halo, block, state_ref[z, 8 * block : 8 * block + 8, :])
        gather(z + halo)
        return 0

    lax.fori_loop(0, NZ, own, 0)

    below, above = edges("slab", SLABS)

    def outer(z, _):
        for base, body, keep in ((0, low_ref, below), (12, high_ref, above)):
            for block in range(4):
                two = body[z, 16 * block : 16 * block + 16, :].astype(F32)
                spread(z + base, 2 * block, two[:8])
                spread(z + base, 2 * block + 1, two[8:])
            gather(z + base, keep)
        return 0

    lax.fori_loop(0, halo, outer, 0)
    low, high = edges("logic", LOGICS)
    bufs = (a_ref, b_ref)
    for step in range(4):
        src, dst = bufs[step % 2], bufs[(step + 1) % 2]
        reach = 3 - step
        wide = (1, 2, 1, 0)[step]

        def read(z, y, src=src):
            return src[row_of(z, y, halo), :]

        def write(z, y, value, dst=dst, step=step):
            if step == 3:
                out_ref[pl.ds(pl.multiple_of(((z - halo) * NY + y) * 8, 8), 8), :] = value
            else:
                dst[row_of(z, y, halo), :] = value

        diffuse(
            coef_ref, read, write, (halo - reach, halo + NZ + reach), (-wide, NY + wide), low, high
        )


def source_kernel(
    table_ref, label_ref, source_ref, base_ref, low_ref, high_ref, front_ref, back_ref,
    corner_low_ref, corner_high_ref, out_ref, coarse_ref,
    coef_ref, cells_ref, s_ref, a_ref, b_ref, rim_ref, edge_ref, sums_ref,
):
    halo = 3
    fill_coefficients(coef_ref, table_ref, label_ref, halo)
    zero = jnp.zeros((8, 128), F32)

    def rim_at(z, y):
        slot = y + 4 if y < 1 else y - NY + 6
        return pl.ds(pl.multiple_of(((z + 1) * 10 + slot) * 8, 8), 8)

    def edge_at(z, y):
        slot = y + 3 if y < 1 else y - NY + 5
        return pl.ds(pl.multiple_of((z * 8 + slot) * 8, 8), 8)

    low, high = edges("logic", LOGICS)
    below, above = edges("slab", SLABS)

    def strips(z, front, back, keep_front, keep_back):
        for xb in range(8):
            cells_ref[0, pl.ds(xb * 8, 8), :] = front(xb).astype(F32)
            cells_ref[1, pl.ds(xb * 8, 8), :] = back(xb).astype(F32)
        for at in range(8):
            before = cells_ref[0, pl.ds(at, 8, stride=8), :] * keep_front
            after = cells_ref[1, pl.ds(at, 8, stride=8), :] * keep_back
            if at < 4:
                rim_ref[rim_at(z, NY + at), :] = after
                if at:
                    s_ref[row_of(z, at - 4, halo), :] = before
            else:
                rim_ref[rim_at(z, at - 8), :] = before
                if at < 7:
                    s_ref[row_of(z, NY + at - 4, halo), :] = after

    rim_ref[pl.ds(0, 80), :] = jnp.zeros((80, 128), F32)
    rim_ref[pl.ds(15 * 80, 80), :] = jnp.zeros((80, 128), F32)

    def own(z, _):
        for y in range(NY):
            start = (z * 8 + y // 8) * 64 + y % 8
            s_ref[row_of(z + halo, y, halo), :] = source_ref[pl.ds(start, 8, stride=8), :]
        strips(z + halo, lambda xb: front_ref[z, xb], lambda xb: back_ref[z, xb], low, high)
        return 0

    lax.fori_loop(0, NZ, own, 0)

    def outer(z, _):
        for base, body, corner, keep in (
            (0, low_ref, corner_low_ref, below),
            (11, high_ref, corner_high_ref, above),
        ):
            for block in range(4):
                for xb in range(8):
                    two = body[z * 4 + block, xb].astype(F32)
                    cells_ref[4, pl.ds(xb * 8, 8), :] = two[:8]
                    cells_ref[5, pl.ds(xb * 8, 8), :] = two[8:]
                for y in range(16):
                    s_ref[row_of(z + base, 16 * block + y, halo), :] = (
                        cells_ref[4 + y // 8, pl.ds(y % 8, 8, stride=8), :] * keep
                    )
            strips(
                z + base,
                lambda xb: corner[z, xb].astype(F32)[:8],
                lambda xb: corner[z, xb].astype(F32)[8:],
                keep * low,
                keep * high,
            )
        return 0

    lax.fori_loop(0, halo, outer, 0)

    def read_rim(z, y):
        return rim_ref[rim_at(z, y), :]

    def write_edge(z, y, value):
        edge_ref[edge_at(z, y), :] = value + s_ref[row_of(z, y, halo), :]

    def sides(z, _):
        rim_ref[rim_at(z, 0), :] = zero
        rim_ref[rim_at(z, NY - 1), :] = zero
        ky = coef_ref[z, 3]
        write_edge(z, 0, ky * read_rim(z, -1))
        write_edge(z, NY - 1, ky * read_rim(z, NY))
        return 0

    lax.fori_loop(0, NZ + 2 * halo, sides, 0)
    diffuse(coef_ref, read_rim, write_edge, (0, NZ + 2 * halo), (-3, 0), low, high)
    diffuse(coef_ref, read_rim, write_edge, (0, NZ + 2 * halo), (NY, NY + 3), low, high)
    for step in range(3):
        src = (None, a_ref, b_ref)[step]
        dst = (a_ref, b_ref, None)[step]
        reach = 2 - step

        def read(z, y, src=src):
            if src is None:
                if 1 <= y < NY - 1:
                    return s_ref[row_of(z, y, halo), :]
                return edge_ref[edge_at(z, y), :]
            return src[row_of(z, y, halo), :]

        def write(z, y, value, dst=dst, step=step):
            value = value + s_ref[row_of(z, y, halo), :]
            if step < 2:
                dst[row_of(z, y, halo), :] = value
                return
            own = z - halo
            value = value + base_ref[pl.ds(pl.multiple_of((own * NY + y) * 8, 8), 8), :]
            out_ref[own, y // 8, pl.ds(y % 8, 8, stride=8), :] = value
            here = pl.ds(pl.multiple_of((own * 4 + y // 16) * 8, 8), 8)
            if y % 16 == 0:
                sums_ref[here, :] = value
            else:
                sums_ref[here, :] = sums_ref[here, :] + value

        diffuse(
            coef_ref, read, write, (halo - reach, halo + NZ + reach), (-reach, NY + reach), low, high
        )
    exact = lax.Precision.HIGHEST
    lines = lax.dot_general(
        jnp.ones((8, 128), F32), sums_ref[...], (((1,), (1,)), ((), ())),
        precision=exact, preferred_element_type=F32,
    )
    pairs = jnp.where((iota((256, 128), 0) >> 1) == iota((256, 128), 1), 1.0 / 4096.0, 0.0)
    means = jnp.dot(lines, pairs, precision=exact, preferred_element_type=F32)
    coarse_ref[...] = jnp.broadcast_to(means[0:1, :], (DEV, 128))


def vmem(count):
    return [pl.BlockSpec(memory_space=pltpu.VMEM)] * count


def smem(count):
    return [pl.BlockSpec(memory_space=pltpu.SMEM)] * count


def params():
    return pltpu.CompilerParams(vmem_limit_bytes=VMEM)


def cost(flops, moved):
    return pl.CostEstimate(flops=flops, bytes_accessed=moved, transcendentals=0)


def shift(value, axis, by):
    count = lax.axis_size(axis)
    return lax.ppermute(value, axis, [(i, (i + by) % count) for i in range(count)])


def per_device(
    initial_heat_state,
    dynamic_wattage,
    drain_multiplier,
    holder_processor,
    patch_target_slot,
    active_patch_number,
    prior_reduced_heat_map,
    conductivity_lookup,
    substance_of_slab,
):
    state = initial_heat_state
    both = ("logic", "slab")
    shape = jax.ShapeDtypeStruct
    to_high, to_low, t_first, t_last = pl.pallas_call(
        edge_kernel,
        grid=(NZ // 2,),
        out_shape=[
            shape((4, NY, 1024), BF16),
            shape((4, NY, 1024), BF16),
            shape((2, 4, 8, 8, 128), BF16),
            shape((2, 4, 8, 8, 128), BF16),
        ],
        in_specs=[
            pl.BlockSpec((1, NY, 1024), lambda i: (i, 0, 0)),
            pl.BlockSpec((1, NY, 1024), lambda i: (i + NZ // 2, 0, 0)),
        ],
        out_specs=[
            pl.BlockSpec((1, NY, 1024), lambda i: (i, 0, 0)),
            pl.BlockSpec((1, NY, 1024), lambda i: (i, 0, 0)),
            pl.BlockSpec((2, 1, 8, 8, 128), lambda i: (0, i, 0, 0, 0)),
            pl.BlockSpec((2, 1, 8, 8, 128), lambda i: (0, i, 0, 0, 0)),
        ],
        compiler_params=params(),
        cost_estimate=cost(1_000_000, 5_000_000),
        name="edges",
    )(state, state)
    low = shift(to_high, "slab", 1)
    high = shift(to_low, "slab", -1)

    packed = pl.pallas_call(
        pack_kernel,
        out_shape=pltpu.HBM((DEV, ROWS, 128), BF16),
        in_specs=smem(1) + [pl.BlockSpec(memory_space=pltpu.HBM)] * 5,
        out_specs=pl.BlockSpec(memory_space=pltpu.HBM),
        scratch_shapes=[
            pltpu.VMEM((1, TILES), I32),
            pltpu.VMEM((1, TILES), I32),
            pltpu.VMEM((1, TILES), F32),
            pltpu.VMEM((LAYERS, 128), F32),
            pltpu.VMEM((TILES, 256), BF16),
            pltpu.VMEM((DEV, ROWS, 128), BF16),
            pltpu.VMEM((DEV, TILES), F32),
            pltpu.VMEM((CAP, TILES), BF16),
            pltpu.VMEM((DEV, 128), F32),
            pltpu.VMEM((DEV, 128), F32),
            pltpu.VMEM((TILES, 256), BF16),
            pltpu.SemaphoreType.DMA((5,)),
            pltpu.SemaphoreType.DMA((DEV // GROUP,)),
        ],
        compiler_params=params(),
        cost_estimate=cost(5_000_000_000, 4_000_000),
        name="pack",
    )(
        active_patch_number,
        holder_processor.reshape(1, TILES),
        patch_target_slot.reshape(1, TILES),
        drain_multiplier.reshape(1, TILES),
        prior_reduced_heat_map.transpose(1, 2, 0).reshape(128, LAYERS),
        dynamic_wattage,
    )
    packed, low, high = lax.optimization_barrier((packed, low, high))
    got = lax.all_to_all(packed, both, split_axis=0, concat_axis=0, tiled=True)

    base = pl.pallas_call(
        temperature_kernel,
        out_shape=pltpu.VMEM((NZ * NY * 8, 128), F32),
        in_specs=smem(2) + vmem(3),
        out_specs=pl.BlockSpec(memory_space=pltpu.VMEM),
        scratch_shapes=[
            pltpu.VMEM((16, 6, 8, 128), F32),
            pltpu.VMEM((16, 8, 64, 128), F32),
            pltpu.VMEM((16 * 72 * 8, 128), F32),
            pltpu.VMEM((16 * 72 * 8, 128), F32),
        ],
        compiler_params=params(),
        cost_estimate=cost(100_000_000, 20_000_000),
        name="diffuse_temperature",
    )(conductivity_lookup, substance_of_slab, state, low, high)
    got, base = lax.optimization_barrier((got, base))

    source, lower, upper, first, last = pl.pallas_call(
        scatter_kernel,
        out_shape=[
            shape((64, 8, 8, 128), F32),
            shape((12, 8, 16, 128), BF16),
            shape((12, 8, 16, 128), BF16),
            shape((NZ, 8, 8, 128), BF16),
            shape((NZ, 8, 8, 128), BF16),
        ],
        in_specs=vmem(3),
        out_specs=vmem(5),
        scratch_shapes=[pltpu.VMEM((32, 128), I32)],
        compiler_params=params(),
        cost_estimate=cost(5_000_000_000, 6_000_000),
        name="place_tiles",
    )(got, t_first.reshape(NZ, 8, 8, 128), t_last.reshape(NZ, 8, 8, 128))
    s_low = shift(upper, "slab", 1)
    s_high = shift(lower, "slab", -1)
    s_front = shift(last, "logic", 1)
    s_back = shift(first, "logic", -1)
    to_high, to_low = pl.pallas_call(
        corner_kernel,
        out_shape=[shape((3, 8, 16, 128), BF16)] * 2,
        in_specs=vmem(2),
        out_specs=vmem(2),
        compiler_params=params(),
        cost_estimate=cost(1_000_000, 1_000_000),
        name="corners",
    )(s_front, s_back)
    s_corner_low = shift(to_high, "slab", 1)
    s_corner_high = shift(to_low, "slab", -1)

    new_state, coarse = pl.pallas_call(
        source_kernel,
        out_shape=[shape((NZ, 8, 64, 128), F32), shape((DEV, 128), F32)],
        in_specs=smem(2) + vmem(8),
        out_specs=vmem(2),
        scratch_shapes=[
            pltpu.VMEM((14, 6, 8, 128), F32),
            pltpu.VMEM((6, 64, 128), F32),
            pltpu.VMEM((14 * 72 * 8, 128), F32),
            pltpu.VMEM((14 * 72 * 8, 128), F32),
            pltpu.VMEM((14 * 72 * 8, 128), F32),
            pltpu.VMEM((16 * 80, 128), F32),
            pltpu.VMEM((14 * 64, 128), F32),
            pltpu.VMEM((256, 128), F32),
        ],
        compiler_params=params(),
        cost_estimate=cost(100_000_000, 20_000_000),
        name="diffuse_source",
    )(
        conductivity_lookup, substance_of_slab, source.reshape(4096, 128), base,
        s_low, s_high, s_front, s_back, s_corner_low, s_corner_high,
    )
    thermal_state = (
        new_state.reshape(NZ, 8, 8, 8, 128).transpose(0, 1, 3, 2, 4).reshape(NZ, NY, 1024)
    )
    gathered = lax.all_to_all(coarse, both, split_axis=0, concat_axis=0, tiled=True)
    reduced_map = gathered.reshape(LOGICS, SLABS, NZ, 4, 4)
    reduced_map = jnp.transpose(reduced_map, (1, 2, 0, 3, 4)).reshape(LAYERS, 32, 4)
    return (thermal_state, reduced_map)


def solution(mesh):
    return jax.shard_map(
        per_device,
        mesh=mesh,
        in_specs=(
            P("slab", "logic", None),
            P(("logic", "slab"), None),
            P(("logic", "slab")),
            P(("logic", "slab"), None),
            P(("logic", "slab")),
            P(("logic", "slab")),
            P(),
            P(),
            P(),
        ),
        out_specs=(P("slab", "logic", None), P()),
        check_vma=False,
    )
```

```python
import functools

import jax
import jax.numpy as jnp
from jax import lax
from jax.experimental import pallas as pl
from jax.experimental.pallas import tpu as pltpu
from jax.sharding import PartitionSpec as P

LEAK_BETA = 0.7
THERMAL_FACTOR = 0.1

DEV = 128
CAP = 32
TILES = 2048
NZ = 8
NY = 64
LAYERS = 128
SLABS = 16
LOGICS = 8
ROWS = 72
GROUP = 32
VMEM = 28 * 1024 * 1024
F32 = jnp.float32
BF16 = jnp.bfloat16
I32 = jnp.int32


def iota(shape, dim):
    return lax.broadcasted_iota(I32, shape, dim)


def edge_kernel(lower_ref, upper_ref, to_high_ref, to_low_ref, first_ref, last_ref):
    to_low_ref[...] = lower_ref[...].astype(BF16)
    to_high_ref[...] = upper_ref[...].astype(BF16)
    for half, ref in ((0, lower_ref), (1, upper_ref)):
        for xb in range(8):
            cols = slice(128 * xb, 128 * xb + 128)
            first_ref[half, 0, xb] = ref[0, :8, cols].astype(BF16)
            last_ref[half, 0, xb] = ref[0, NY - 8 :, cols].astype(BF16)


def corner_kernel(front_ref, back_ref, low_ref, high_ref):
    for out, first in ((low_ref, NZ - 3), (high_ref, 0)):
        for z in range(3):
            for xb in range(8):
                out[z, xb] = jnp.concatenate(
                    [front_ref[first + z, xb].astype(F32), back_ref[first + z, xb].astype(F32)], axis=0
                ).astype(BF16)


def pack_kernel(
    count_ref, owner_hbm, target_hbm, drain_hbm, prior_hbm, watt_hbm, out_hbm,
    owner_ref, target_ref, drain_ref, prior_ref, watt_ref, out_ref,
    member_ref, pick_ref, high_ref, low_ref, power_ref, in_sems, out_sems,
):
    loads = [
        pltpu.make_async_copy(src, dst, in_sems.at[i])
        for i, (src, dst) in enumerate(
            (
                (owner_hbm, owner_ref),
                (target_hbm, target_ref),
                (prior_hbm, prior_ref),
                (drain_hbm, drain_ref),
                (watt_hbm, watt_ref),
            )
        )
    ]
    for load in loads:
        load.start()
    for load in loads[:4]:
        load.wait()
    owner = owner_ref[...]
    target = target_ref[...]
    live = iota((1, TILES), 1) < count_ref[0]
    layer = (owner & (SLABS - 1)) * NZ + (target >> 8)
    column = (owner >> 4) * 16 + ((target >> 6) & 3) * 4 + (target & 3)
    at_layer = jnp.where(iota((LAYERS, TILES), 0) == layer, 1.0, 0.0).astype(BF16)
    prior = prior_ref[...]
    first = prior.astype(BF16)
    rest = prior - first.astype(F32)
    second = rest.astype(BF16)
    third = (rest - second.astype(F32)).astype(BF16)
    lookup = lambda part: lax.dot_general(
        part, at_layer, (((1,), (0,)), ((), ())), preferred_element_type=F32
    )
    picked = lookup(first) + lookup(second) + lookup(third)
    heat = jnp.sum(
        jnp.where(iota((LAYERS, TILES), 0) == column, picked, 0.0), axis=0, keepdims=True
    )
    scale = 1.0 + drain_ref[...] * jnp.exp(LEAK_BETA * heat)
    member = jnp.where(iota((DEV, TILES), 0) == jnp.where(live, owner, -1), 1.0, 0.0)
    member_ref[...] = member
    before = jnp.where(iota((256, 256), 0) < iota((256, 256), 1), 1.0, 0.0).astype(BF16)
    carry = jnp.zeros((DEV, 1), F32)
    ranks = []
    for b in range(TILES // 256):
        part = member[:, 256 * b : 256 * b + 256]
        earlier = jnp.dot(part.astype(BF16), before, preferred_element_type=F32) + carry
        ranks.append(jnp.sum(earlier * part, axis=0, keepdims=True))
        carry = carry + jnp.sum(part, axis=1, keepdims=True)
    rank = jnp.where(live, jnp.concatenate(ranks, axis=1).astype(I32), -1)
    pick_ref[...] = jnp.where(iota((CAP, TILES), 0) == rank, 1.0, 0.0).astype(BF16)
    slot = (iota((128, TILES), 0) & (CAP - 1)) == rank
    flat = member.astype(BF16)
    spot = lambda value: lax.dot_general(
        flat,
        jnp.where(slot, value.astype(F32), 0.0).astype(BF16),
        (((1,), (1,)), ((), ())),
        preferred_element_type=F32,
    )
    high_ref[...] = spot((target >> 6) + 1)
    low_ref[...] = spot(target & 63)
    row8 = iota((8, 128), 0)
    loads[4].wait()
    for b in range(TILES // 128):
        rows = pl.ds(128 * b, 128)
        spread = jnp.transpose(jnp.broadcast_to(scale[:, 128 * b : 128 * b + 128], (128, 128)))
        for h in range(2):
            cols = pl.ds(128 * h, 128)
            power_ref[rows, cols] = (watt_ref[rows, cols].astype(F32) * spread).astype(BF16)

    def store(g):
        here = pl.ds(g * GROUP, GROUP)
        return pltpu.make_async_copy(out_ref.at[here], out_hbm.at[here], out_sems.at[g])

    def group(g, _):
        pick = pick_ref[...]
        parts = []
        for j in range(GROUP):
            d = g * GROUP + j
            parts.append(pick * member_ref[pl.ds(d, 1), :].astype(BF16))
            label = jnp.where(
                row8 == 0,
                high_ref[pl.ds(d, 1), :],
                jnp.where(row8 == 1, low_ref[pl.ds(d, 1), :], 0.0),
            )
            out_ref[d, 64:72, :] = label.astype(BF16)
        packed = jnp.dot(
            jnp.concatenate(parts, axis=0), power_ref[...], preferred_element_type=F32
        ).astype(BF16)
        here = pl.ds(g * GROUP, GROUP)
        out_ref[here, 0:32, :] = packed[:, :128].reshape(GROUP, CAP, 128)
        out_ref[here, 32:64, :] = packed[:, 128:].reshape(GROUP, CAP, 128)
        store(g).start()
        return 0

    lax.fori_loop(0, DEV // GROUP, group, 0)
    for g in range(DEV // GROUP):
        store(g).wait()


def scatter_kernel(
    got_ref, first_ref, last_ref, source_ref, low_ref, high_ref, front_ref, back_ref, label_ref,
):
    labels = got_ref[:, 64:72, :].reshape(DEV * 8, 128)
    row = iota((DEV * 8, 128), 0)
    lane = iota((DEV * 8, 128), 1)
    labels = jnp.where((lane >> 5) == ((row >> 3) & 3), labels.astype(F32), 0.0).astype(BF16)
    g = iota((32, DEV * 8), 0)
    col = iota((32, DEV * 8), 1)
    weight = jnp.where((col & 7) == 0, 64.0, jnp.where((col & 7) == 1, 1.0, 0.0))
    weight = jnp.where((col >> 5) == g, weight, 0.0).astype(BF16)
    target = jnp.dot(weight, labels, preferred_element_type=F32).astype(I32) - 64
    label_ref[...] = target
    left = got_ref[:, 0:32, :].reshape(DEV * CAP, 128)
    right = got_ref[:, 32:64, :].reshape(DEV * CAP, 128)
    both = jnp.concatenate([left, right], axis=1)
    wanted = iota((512, 128), 0) * 4
    upper = iota((8, 128), 0) < 4
    for c in range(4):
        chosen = jnp.concatenate(
            [
                jnp.where(wanted == label_ref[k : k + 1, :] - c, 1.0, 0.0).astype(BF16)
                for k in range(32)
            ],
            axis=1,
        )
        total = THERMAL_FACTOR * jnp.dot(chosen, both, preferred_element_type=F32)
        for h in range(2):
            xb = 2 * c + h
            part = total[:, 128 * h : 128 * h + 128]
            cells = part.reshape(NZ * 8, 8, 128)
            source_ref[:, xb] = cells
            short = part.astype(BF16).reshape(NZ * 4, 16, 128)
            low_ref[:, xb] = short[:12]
            high_ref[:, xb] = short[20:]
            for z in range(NZ):
                front_ref[z, xb] = jnp.where(
                    upper, first_ref[z, xb].astype(F32), pltpu.roll(cells[8 * z], 4, 0)
                ).astype(BF16)
                back_ref[z, xb] = jnp.where(
                    upper, pltpu.roll(cells[8 * z + 7], 4, 0), last_ref[z, xb].astype(F32)
                ).astype(BF16)


def fill_coefficients(coef_ref, table_ref, label_ref, halo):
    base = lax.axis_index("slab") * NZ - halo
    spot = iota((8, 128), 0) * 128 + iota((8, 128), 1)

    def layer(i, _):
        z = base + i
        inside = jnp.where((z >= 0) & (z < LAYERS), 1.0, 0.0).astype(F32)
        material = lambda at: label_ref[jnp.clip(at, 0, LAYERS - 1)]
        here = material(z)
        splat = lambda m, k: jnp.full((8, 128), table_ref[m, k], F32)
        kx = splat(here, 0)
        ky = splat(here, 1)
        a = splat(here, 2)
        above = splat(material(z + 1), 2)
        below = splat(material(z - 1), 2)
        up = 2.0 * a * above / (a + above)
        down = 2.0 * a * below / (a + below)
        keep = jnp.full((8, 128), inside, F32)
        coef_ref[i, 0] = keep * (1.0 - 2.0 * kx - 2.0 * ky - up - down)
        coef_ref[i, 1] = keep * jnp.where(spot == 0, 0.0, kx)
        coef_ref[i, 2] = keep * jnp.where(spot == 1023, 0.0, kx)
        coef_ref[i, 3] = keep * ky
        coef_ref[i, 4] = keep * up
        coef_ref[i, 5] = keep * down
        return 0

    lax.fori_loop(0, NZ + 2 * halo, layer, 0)


def diffuse(coef, read, write, layers, ranges, low, high):
    lane = iota((8, 128), 1)

    def layer(z, _):
        c = [coef(z, j) for j in range(6)]
        for rows in ranges:
            before, cell = read(z, rows[0] - 1), read(z, rows[0])
            for y in range(rows[0], rows[1]):
                after = read(z, y + 1)
                step = pltpu.roll(cell, 127, 1)
                right = jnp.where(lane == 127, pltpu.roll(step, 7, 0), step)
                step = pltpu.roll(cell, 1, 1)
                left = jnp.where(lane == 0, pltpu.roll(step, 1, 0), step)
                value = (
                    c[0] * cell
                    + c[1] * left
                    + c[2] * right
                    + c[3] * (before + after)
                    + c[4] * read(z + 1, y)
                    + c[5] * read(z - 1, y)
                )
                if y < 0:
                    value = value * low
                if y >= NY:
                    value = value * high
                write(z, y, value)
                before, cell = cell, after
        return 0

    lax.fori_loop(layers[0], layers[1], layer, 0)


def edges(axis, count):
    at = lax.axis_index(axis)
    low = jnp.full((8, 128), jnp.where(at > 0, 1.0, 0.0), F32)
    high = jnp.full((8, 128), jnp.where(at < count - 1, 1.0, 0.0), F32)
    return low, high


def row_of(z, y, halo):
    return pl.ds(pl.multiple_of((z * (NY + 8) + (y + 4)) * 8, 8), 8)


def temperature_kernel(
    table_ref, label_ref, state_ref, low_ref, high_ref, out_ref, coef_ref, cells_ref, a_ref, b_ref,
):
    halo = 4
    fill_coefficients(coef_ref, table_ref, label_ref, halo)

    def spread(z, block, value):
        for xb in range(8):
            cells_ref[z, block, pl.ds(xb * 8, 8), :] = value[:, 128 * xb : 128 * xb + 128]

    def gather(z, keep=None):
        for y in range(NY):
            value = cells_ref[z, y // 8, pl.ds(y % 8, 8, stride=8), :]
            a_ref[row_of(z, y, halo), :] = value if keep is None else value * keep

    def clear(z, _):
        for y in (-3, -2, -1, NY, NY + 1, NY + 2):
            a_ref[row_of(z, y, halo), :] = jnp.zeros((8, 128), F32)
            b_ref[row_of(z, y, halo), :] = jnp.zeros((8, 128), F32)
        return 0

    lax.fori_loop(0, NZ + 2 * halo, clear, 0)

    def own(z, _):
        for block in range(8):
            spread(z + halo, block, state_ref[z, 8 * block : 8 * block + 8, :])
        gather(z + halo)
        return 0

    lax.fori_loop(0, NZ, own, 0)

    below, above = edges("slab", SLABS)

    def outer(z, _):
        for base, body, keep in ((0, low_ref, below), (12, high_ref, above)):
            for block in range(4):
                two = body[z, 16 * block : 16 * block + 16, :].astype(F32)
                spread(z + base, 2 * block, two[:8])
                spread(z + base, 2 * block + 1, two[8:])
            gather(z + base, keep)
        return 0

    lax.fori_loop(0, halo, outer, 0)
    low, high = edges("logic", LOGICS)
    bufs = (a_ref, b_ref)
    for step in range(4):
        src, dst = bufs[step % 2], bufs[(step + 1) % 2]
        reach = 3 - step
        wide = (1, 2, 1, 0)[step]

        def read(z, y, src=src):
            return src[row_of(z, y, halo), :]

        def write(z, y, value, dst=dst, step=step):
            if step == 3:
                out_ref[pl.ds(pl.multiple_of(((z - halo) * NY + y) * 8, 8), 8), :] = value
            else:
                dst[row_of(z, y, halo), :] = value

        diffuse(
            lambda z, j: coef_ref[z, j],
            read,
            write,
            (halo - reach, halo + NZ + reach),
            [(-wide, NY + wide)],
            low,
            high,
        )


def inner_kernel(coef_ref, source_ref, s_ref, a_ref, b_ref):
    halo = 3

    def own(z, _):
        for y in range(NY):
            start = (z * 8 + y // 8) * 64 + y % 8
            s_ref[row_of(z + halo, y, halo), :] = source_ref[pl.ds(start, 8, stride=8), :]
        return 0

    lax.fori_loop(0, NZ, own, 0)
    for step, (src, dst) in enumerate(((s_ref, a_ref), (a_ref, b_ref))):

        def read(z, y, src=src):
            return src[row_of(z, y, halo), :]

        def write(z, y, value, dst=dst):
            dst[row_of(z, y, halo), :] = value + s_ref[row_of(z, y, halo), :]

        diffuse(
            lambda z, j: coef_ref[z + 1, j],
            read,
            write,
            (halo + 1 + step, halo + NZ - 1 - step),
            [(2 + step, NY - 2 - step)],
            None,
            None,
        )


def outer_kernel(
    s_in, a_in, b_in, coef_ref, base_ref, low_ref, high_ref, front_ref, back_ref,
    corner_low_ref, corner_high_ref, out_hbm, coarse_ref,
    s_ref, a_ref, b_ref, out_ref, cells_ref, rim_ref, edge_ref, sums_ref, sems, in_sems,
):
    halo = 3
    zero = jnp.zeros((8, 128), F32)
    coef = lambda z, j: coef_ref[z + 1, j]
    loads = []
    for step, (src, dst) in enumerate(((s_in, s_ref), (a_in, a_ref), (b_in, b_ref))):
        skip = (0, 2, 3)[step]
        for z in range(halo + step, halo + NZ - step):
            rows = pl.ds((z * (NY + 8) + 4 + skip) * 8, (NY - 2 * skip) * 8)
            loads.append(pltpu.make_async_copy(src.at[rows], dst.at[rows], in_sems.at[len(loads)]))
    for load in loads:
        load.start()

    def rim_at(z, y):
        slot = y + 4 if y < 1 else y - NY + 6
        return pl.ds(pl.multiple_of(((z + 1) * 10 + slot) * 8, 8), 8)

    def edge_at(z, y):
        slot = y + 3 if y < 1 else y - NY + 5
        return pl.ds(pl.multiple_of((z * 8 + slot) * 8, 8), 8)

    low, high = edges("logic", LOGICS)
    below, above = edges("slab", SLABS)

    def strips(z, slot, front, back, keep_front, keep_back):
        for xb in range(8):
            cells_ref[slot, pl.ds(xb * 8, 8), :] = front(xb).astype(F32)
            cells_ref[slot + 1, pl.ds(xb * 8, 8), :] = back(xb).astype(F32)
        rim_ref[rim_at(z, 0), :] = zero
        rim_ref[rim_at(z, NY - 1), :] = zero
        for at in range(8):
            before = cells_ref[slot, pl.ds(at, 8, stride=8), :] * keep_front
            after = cells_ref[slot + 1, pl.ds(at, 8, stride=8), :] * keep_back
            if at < 4:
                rim_ref[rim_at(z, NY + at), :] = after
                if at:
                    s_ref[row_of(z, at - 4, halo), :] = before
            else:
                rim_ref[rim_at(z, at - 8), :] = before
                if at < 7:
                    s_ref[row_of(z, NY + at - 4, halo), :] = after

    rim_ref[pl.ds(0, 80), :] = jnp.zeros((80, 128), F32)
    rim_ref[pl.ds(15 * 80, 80), :] = jnp.zeros((80, 128), F32)

    def own(i, _):
        for half in range(2):
            z = 2 * i + half
            strips(
                z + halo, 2 * half, lambda xb: front_ref[z, xb], lambda xb: back_ref[z, xb], low, high
            )
        return 0

    lax.fori_loop(0, NZ // 2, own, 0)

    def outer(z, _):
        for side, (base, body, corner, keep) in enumerate(
            ((0, low_ref, corner_low_ref, below), (11, high_ref, corner_high_ref, above))
        ):
            for block in range(4):
                slot = 8 * side + 2 * block
                for xb in range(8):
                    two = body[z * 4 + block, xb].astype(F32)
                    cells_ref[slot, pl.ds(xb * 8, 8), :] = two[:8]
                    cells_ref[slot + 1, pl.ds(xb * 8, 8), :] = two[8:]
                for y in range(16):
                    s_ref[row_of(z + base, 16 * block + y, halo), :] = (
                        cells_ref[slot + y // 8, pl.ds(y % 8, 8, stride=8), :] * keep
                    )
            strips(
                z + base,
                16 + 2 * side,
                lambda xb: corner[z, xb].astype(F32)[:8],
                lambda xb: corner[z, xb].astype(F32)[8:],
                keep * low,
                keep * high,
            )
        return 0

    lax.fori_loop(0, halo, outer, 0)
    for load in loads[:8]:
        load.wait()

    def read_rim(z, y):
        return rim_ref[rim_at(z, y), :]

    def write_edge(z, y, value):
        edge_ref[edge_at(z, y), :] = value + s_ref[row_of(z, y, halo), :]
        if y == -1:
            edge_ref[edge_at(z, 0), :] = (
                coef(z, 3) * read_rim(z, -1) + s_ref[row_of(z, 0, halo), :]
            )
        if y == NY:
            edge_ref[edge_at(z, NY - 1), :] = (
                coef(z, 3) * read_rim(z, NY) + s_ref[row_of(z, NY - 1, halo), :]
            )

    diffuse(coef, read_rim, write_edge, (0, NZ + 2 * halo), [(-3, 0), (NY, NY + 3)], low, high)

    def first(z, y):
        if 1 <= y < NY - 1:
            return s_ref[row_of(z, y, halo), :]
        return edge_ref[edge_at(z, y), :]

    def second(z, y):
        return a_ref[row_of(z, y, halo), :]

    def third(z, y):
        return b_ref[row_of(z, y, halo), :]

    def to(ref):
        def write(z, y, value):
            ref[row_of(z, y, halo), :] = value + s_ref[row_of(z, y, halo), :]

        return write

    every = lambda reach: [(-reach, NY + reach)]
    diffuse(coef, first, to(a_ref), (1, 4), every(2), low, high)
    diffuse(coef, first, to(a_ref), (10, 13), every(2), low, high)
    diffuse(coef, first, to(a_ref), (4, 10), [(-2, 2), (NY - 2, NY + 2)], low, high)
    for load in loads[8:]:
        load.wait()
    diffuse(coef, second, to(b_ref), (2, 5), every(1), low, high)
    diffuse(coef, second, to(b_ref), (9, 12), every(1), low, high)
    diffuse(coef, second, to(b_ref), (5, 9), [(-1, 3), (NY - 3, NY + 1)], low, high)

    def store(z):
        return pltpu.make_async_copy(out_ref.at[z], out_hbm.at[z], sems.at[z])

    def write_out(z, y, value):
        own = z - halo
        value = value + s_ref[row_of(z, y, halo), :]
        value = value + base_ref[pl.ds(pl.multiple_of((own * NY + y) * 8, 8), 8), :]
        out_ref[own, y // 8, pl.ds(y % 8, 8, stride=8), :] = value
        here = pl.ds(pl.multiple_of((own * 4 + y // 16) * 8, 8), 8)
        if y % 16 == 0:
            sums_ref[here, :] = value
        else:
            sums_ref[here, :] = sums_ref[here, :] + value
        if y == NY - 1:
            store(own).start()

    diffuse(coef, third, write_out, (halo, halo + NZ), every(0), low, high)
    exact = lax.Precision.HIGHEST
    lines = lax.dot_general(
        jnp.ones((8, 128), F32), sums_ref[...], (((1,), (1,)), ((), ())),
        precision=exact, preferred_element_type=F32,
    )
    pairs = jnp.where((iota((256, 128), 0) >> 1) == iota((256, 128), 1), 1.0 / 4096.0, 0.0)
    means = jnp.dot(lines, pairs, precision=exact, preferred_element_type=F32)
    coarse_ref[...] = jnp.broadcast_to(means[0:1, :], (DEV, 128))
    for z in range(NZ):
        store(z).wait()


def vmem(count):
    return [pl.BlockSpec(memory_space=pltpu.VMEM)] * count


def smem(count):
    return [pl.BlockSpec(memory_space=pltpu.SMEM)] * count


def params():
    return pltpu.CompilerParams(vmem_limit_bytes=VMEM)


def cost(flops, moved):
    return pl.CostEstimate(flops=flops, bytes_accessed=moved, transcendentals=0)


def shift(value, axis, by):
    count = lax.axis_size(axis)
    return lax.ppermute(value, axis, [(i, (i + by) % count) for i in range(count)])


def per_device(
    initial_heat_state,
    dynamic_wattage,
    drain_multiplier,
    holder_processor,
    patch_target_slot,
    active_patch_number,
    prior_reduced_heat_map,
    conductivity_lookup,
    substance_of_slab,
):
    state = initial_heat_state
    both = ("logic", "slab")
    shape = jax.ShapeDtypeStruct
    to_high, to_low, t_first, t_last = pl.pallas_call(
        edge_kernel,
        grid=(NZ // 2,),
        out_shape=[
            shape((4, NY, 1024), BF16),
            shape((4, NY, 1024), BF16),
            shape((2, 4, 8, 8, 128), BF16),
            shape((2, 4, 8, 8, 128), BF16),
        ],
        in_specs=[
            pl.BlockSpec((1, NY, 1024), lambda i: (i, 0, 0)),
            pl.BlockSpec((1, NY, 1024), lambda i: (i + NZ // 2, 0, 0)),
        ],
        out_specs=[
            pl.BlockSpec((1, NY, 1024), lambda i: (i, 0, 0)),
            pl.BlockSpec((1, NY, 1024), lambda i: (i, 0, 0)),
            pl.BlockSpec((2, 1, 8, 8, 128), lambda i: (0, i, 0, 0, 0)),
            pl.BlockSpec((2, 1, 8, 8, 128), lambda i: (0, i, 0, 0, 0)),
        ],
        compiler_params=params(),
        cost_estimate=cost(1_000_000, 5_000_000),
        name="edges",
    )(state, state)
    low = shift(to_high, "slab", 1)
    high = shift(to_low, "slab", -1)

    packed = pl.pallas_call(
        pack_kernel,
        out_shape=pltpu.HBM((DEV, ROWS, 128), BF16),
        in_specs=smem(1) + [pl.BlockSpec(memory_space=pltpu.HBM)] * 5,
        out_specs=pl.BlockSpec(memory_space=pltpu.HBM),
        scratch_shapes=[
            pltpu.VMEM((1, TILES), I32),
            pltpu.VMEM((1, TILES), I32),
            pltpu.VMEM((1, TILES), F32),
            pltpu.VMEM((LAYERS, 128), F32),
            pltpu.VMEM((TILES, 256), BF16),
            pltpu.VMEM((DEV, ROWS, 128), BF16),
            pltpu.VMEM((DEV, TILES), F32),
            pltpu.VMEM((CAP, TILES), BF16),
            pltpu.VMEM((DEV, 128), F32),
            pltpu.VMEM((DEV, 128), F32),
            pltpu.VMEM((TILES, 256), BF16),
            pltpu.SemaphoreType.DMA((5,)),
            pltpu.SemaphoreType.DMA((DEV // GROUP,)),
        ],
        compiler_params=params(),
        cost_estimate=cost(5_000_000_000, 4_000_000),
        name="pack",
    )(
        active_patch_number,
        holder_processor.reshape(1, TILES),
        patch_target_slot.reshape(1, TILES),
        drain_multiplier.reshape(1, TILES),
        prior_reduced_heat_map.transpose(1, 2, 0).reshape(128, LAYERS),
        dynamic_wattage,
    )
    packed, low, high = lax.optimization_barrier((packed, low, high))
    got = lax.all_to_all(packed, both, split_axis=0, concat_axis=0, tiled=True)

    base, coef = pl.pallas_call(
        temperature_kernel,
        out_shape=[shape((NZ * NY * 8, 128), F32), shape((16, 6, 8, 128), F32)],
        in_specs=smem(2) + vmem(3),
        out_specs=vmem(2),
        scratch_shapes=[
            pltpu.VMEM((16, 8, 64, 128), F32),
            pltpu.VMEM((16 * 72 * 8, 128), F32),
            pltpu.VMEM((16 * 72 * 8, 128), F32),
        ],
        compiler_params=params(),
        cost_estimate=cost(100_000_000, 20_000_000),
        name="diffuse_temperature",
    )(conductivity_lookup, substance_of_slab, state, low, high)
    got, base, coef = lax.optimization_barrier((got, base, coef))

    source, lower, upper, first, last = pl.pallas_call(
        scatter_kernel,
        out_shape=[
            shape((64, 8, 8, 128), F32),
            shape((12, 8, 16, 128), BF16),
            shape((12, 8, 16, 128), BF16),
            shape((NZ, 8, 8, 128), BF16),
            shape((NZ, 8, 8, 128), BF16),
        ],
        in_specs=vmem(3),
        out_specs=vmem(5),
        scratch_shapes=[pltpu.VMEM((32, 128), I32)],
        compiler_params=params(),
        cost_estimate=cost(5_000_000_000, 6_000_000),
        name="place_tiles",
    )(got, t_first.reshape(NZ, 8, 8, 128), t_last.reshape(NZ, 8, 8, 128))
    s_low = shift(upper, "slab", 1)
    s_high = shift(lower, "slab", -1)
    s_front = shift(last, "logic", 1)
    s_back = shift(first, "logic", -1)
    to_high, to_low = pl.pallas_call(
        corner_kernel,
        out_shape=[shape((3, 8, 16, 128), BF16)] * 2,
        in_specs=vmem(2),
        out_specs=vmem(2),
        compiler_params=params(),
        cost_estimate=cost(1_000_000, 1_000_000),
        name="corners",
    )(s_front, s_back)
    s_corner_low = shift(to_high, "slab", 1)
    s_corner_high = shift(to_low, "slab", -1)

    rows = shape((14 * 72 * 8, 128), F32)
    parts = pl.pallas_call(
        inner_kernel,
        out_shape=[rows] * 3,
        in_specs=vmem(2),
        out_specs=vmem(3),
        compiler_params=params(),
        cost_estimate=cost(20_000_000, 10_000_000),
        name="diffuse_inner",
    )(coef, source.reshape(4096, 128))
    new_state, coarse = pl.pallas_call(
        outer_kernel,
        out_shape=[pltpu.HBM((NZ, 8, 64, 128), F32), shape((DEV, 128), F32)],
        in_specs=[pl.BlockSpec(memory_space=pl.ANY)] * 3 + vmem(8),
        out_specs=[pl.BlockSpec(memory_space=pltpu.HBM)] + vmem(1),
        scratch_shapes=[
            pltpu.VMEM((14 * 72 * 8, 128), F32),
            pltpu.VMEM((14 * 72 * 8, 128), F32),
            pltpu.VMEM((14 * 72 * 8, 128), F32),
            pltpu.VMEM((NZ, 8, 64, 128), F32),
            pltpu.VMEM((20, 64, 128), F32),
            pltpu.VMEM((16 * 80, 128), F32),
            pltpu.VMEM((14 * 64, 128), F32),
            pltpu.VMEM((256, 128), F32),
            pltpu.SemaphoreType.DMA((NZ,)),
            pltpu.SemaphoreType.DMA((18,)),
        ],
        compiler_params=params(),
        cost_estimate=cost(100_000_000, 20_000_000),
        name="diffuse_outer",
    )(*parts, coef, base, s_low, s_high, s_front, s_back, s_corner_low, s_corner_high)
    thermal_state = (
        new_state.reshape(NZ, 8, 8, 8, 128).transpose(0, 1, 3, 2, 4).reshape(NZ, NY, 1024)
    )
    gathered = lax.all_to_all(coarse, both, split_axis=0, concat_axis=0, tiled=True)
    reduced_map = gathered.reshape(LOGICS, SLABS, NZ, 4, 4)
    reduced_map = jnp.transpose(reduced_map, (1, 2, 0, 3, 4)).reshape(LAYERS, 32, 4)
    return (thermal_state, reduced_map)


def solution(mesh):
    return jax.shard_map(
        per_device,
        mesh=mesh,
        in_specs=(
            P("slab", "logic", None),
            P(("logic", "slab"), None),
            P(("logic", "slab")),
            P(("logic", "slab"), None),
            P(("logic", "slab")),
            P(("logic", "slab")),
            P(),
            P(),
            P(),
        ),
        out_specs=(P("slab", "logic", None), P()),
        check_vma=False,
    )
```

```python
import functools

import jax
import jax.numpy as jnp
from jax import lax
from jax.experimental import pallas as pl
from jax.experimental.pallas import tpu as pltpu
from jax.sharding import PartitionSpec as P

LEAK_BETA = 0.7
THERMAL_FACTOR = 0.1

DEV = 128
CAP = 32
TILES = 2048
NZ = 8
NY = 64
LAYERS = 128
SLABS = 16
LOGICS = 8
ROWS = 72
GROUP = 32
VMEM = 28 * 1024 * 1024
F32 = jnp.float32
BF16 = jnp.bfloat16
I32 = jnp.int32


def iota(shape, dim):
    return lax.broadcasted_iota(I32, shape, dim)


def edge_kernel(
    lower_ref, upper_ref, to_high_ref, to_low_ref, far_high_ref, far_low_ref, first_ref, last_ref
):
    step = pl.program_id(0)

    @pl.when(step < 3)
    def _():
        to_low_ref[...] = lower_ref[...].astype(BF16)

    @pl.when(step == 3)
    def _():
        far_low_ref[...] = lower_ref[...].astype(BF16)

    @pl.when(step > 0)
    def _():
        to_high_ref[...] = upper_ref[...].astype(BF16)

    @pl.when(step == 0)
    def _():
        far_high_ref[...] = upper_ref[...].astype(BF16)

    for half, ref in ((0, lower_ref), (1, upper_ref)):
        for xb in range(8):
            cols = slice(128 * xb, 128 * xb + 128)
            first_ref[half, 0, xb] = ref[0, :8, cols].astype(BF16)
            last_ref[half, 0, xb] = ref[0, NY - 8 :, cols].astype(BF16)


def corner_kernel(front_ref, back_ref, low_ref, high_ref):
    for out, first in ((low_ref, NZ - 3), (high_ref, 0)):
        for z in range(3):
            for xb in range(8):
                out[z, xb] = jnp.concatenate(
                    [front_ref[first + z, xb].astype(F32), back_ref[first + z, xb].astype(F32)], axis=0
                ).astype(BF16)


def pack_kernel(
    count_ref, owner_hbm, target_hbm, drain_hbm, prior_hbm, watt_hbm, out_hbm,
    owner_ref, target_ref, drain_ref, prior_ref, watt_ref, out_ref,
    member_ref, pick_ref, high_ref, low_ref, power_ref, in_sems, out_sems,
):
    loads = [
        pltpu.make_async_copy(src, dst, in_sems.at[i])
        for i, (src, dst) in enumerate(
            (
                (owner_hbm, owner_ref),
                (target_hbm, target_ref),
                (prior_hbm, prior_ref),
                (drain_hbm, drain_ref),
                (watt_hbm, watt_ref),
            )
        )
    ]
    for load in loads:
        load.start()
    for load in loads[:4]:
        load.wait()
    owner = owner_ref[...]
    target = target_ref[...]
    live = iota((1, TILES), 1) < count_ref[0]
    layer = (owner & (SLABS - 1)) * NZ + (target >> 8)
    column = (owner >> 4) * 16 + ((target >> 6) & 3) * 4 + (target & 3)
    at_layer = jnp.where(iota((LAYERS, TILES), 0) == layer, 1.0, 0.0).astype(BF16)
    prior = prior_ref[...]
    first = prior.astype(BF16)
    rest = prior - first.astype(F32)
    second = rest.astype(BF16)
    third = (rest - second.astype(F32)).astype(BF16)
    lookup = lambda part: lax.dot_general(
        part, at_layer, (((1,), (0,)), ((), ())), preferred_element_type=F32
    )
    picked = lookup(first) + lookup(second) + lookup(third)
    heat = jnp.sum(
        jnp.where(iota((LAYERS, TILES), 0) == column, picked, 0.0), axis=0, keepdims=True
    )
    scale = 1.0 + drain_ref[...] * jnp.exp(LEAK_BETA * heat)
    member = jnp.where(iota((DEV, TILES), 0) == jnp.where(live, owner, -1), 1.0, 0.0)
    member_ref[...] = member
    before = jnp.where(iota((256, 256), 0) < iota((256, 256), 1), 1.0, 0.0).astype(BF16)
    carry = jnp.zeros((DEV, 1), F32)
    ranks = []
    for b in range(TILES // 256):
        part = member[:, 256 * b : 256 * b + 256]
        earlier = jnp.dot(part.astype(BF16), before, preferred_element_type=F32) + carry
        ranks.append(jnp.sum(earlier * part, axis=0, keepdims=True))
        carry = carry + jnp.sum(part, axis=1, keepdims=True)
    rank = jnp.where(live, jnp.concatenate(ranks, axis=1).astype(I32), -1)
    pick_ref[...] = jnp.where(iota((CAP, TILES), 0) == rank, 1.0, 0.0).astype(BF16)
    slot = (iota((128, TILES), 0) & (CAP - 1)) == rank
    flat = member.astype(BF16)
    spot = lambda value: lax.dot_general(
        flat,
        jnp.where(slot, value.astype(F32), 0.0).astype(BF16),
        (((1,), (1,)), ((), ())),
        preferred_element_type=F32,
    )
    high_ref[...] = spot((target >> 6) + 1)
    low_ref[...] = spot(target & 63)
    row8 = iota((8, 128), 0)
    loads[4].wait()
    for b in range(TILES // 128):
        rows = pl.ds(128 * b, 128)
        spread = jnp.transpose(jnp.broadcast_to(scale[:, 128 * b : 128 * b + 128], (128, 128)))
        for h in range(2):
            cols = pl.ds(128 * h, 128)
            power_ref[rows, cols] = (watt_ref[rows, cols].astype(F32) * spread).astype(BF16)

    def store(g):
        here = pl.ds(g * GROUP, GROUP)
        return pltpu.make_async_copy(out_ref.at[here], out_hbm.at[here], out_sems.at[g])

    def group(g, _):
        pick = pick_ref[...]
        parts = []
        for j in range(GROUP):
            d = g * GROUP + j
            parts.append(pick * member_ref[pl.ds(d, 1), :].astype(BF16))
            label = jnp.where(
                row8 == 0,
                high_ref[pl.ds(d, 1), :],
                jnp.where(row8 == 1, low_ref[pl.ds(d, 1), :], 0.0),
            )
            out_ref[d, 64:72, :] = label.astype(BF16)
        packed = jnp.dot(
            jnp.concatenate(parts, axis=0), power_ref[...], preferred_element_type=F32
        ).astype(BF16)
        here = pl.ds(g * GROUP, GROUP)
        out_ref[here, 0:32, :] = packed[:, :128].reshape(GROUP, CAP, 128)
        out_ref[here, 32:64, :] = packed[:, 128:].reshape(GROUP, CAP, 128)
        store(g).start()
        return 0

    lax.fori_loop(0, DEV // GROUP, group, 0)
    for g in range(DEV // GROUP):
        store(g).wait()


def scatter_kernel(
    got_ref, first_hbm, last_hbm, source_ref, low_ref, high_ref, front_ref, back_ref,
    label_ref, first_ref, last_ref, sems,
):
    loads = [
        pltpu.make_async_copy(first_hbm, first_ref, sems.at[0]),
        pltpu.make_async_copy(last_hbm, last_ref, sems.at[1]),
    ]
    for load in loads:
        load.start()
    labels = got_ref[:, 64:72, :].reshape(DEV * 8, 128)
    row = iota((DEV * 8, 128), 0)
    lane = iota((DEV * 8, 128), 1)
    labels = jnp.where((lane >> 5) == ((row >> 3) & 3), labels.astype(F32), 0.0).astype(BF16)
    g = iota((32, DEV * 8), 0)
    col = iota((32, DEV * 8), 1)
    weight = jnp.where((col & 7) == 0, 64.0, jnp.where((col & 7) == 1, 1.0, 0.0))
    weight = jnp.where((col >> 5) == g, weight, 0.0).astype(BF16)
    target = jnp.dot(weight, labels, preferred_element_type=F32).astype(I32) - 64
    label_ref[...] = target
    left = got_ref[:, 0:32, :].reshape(DEV * CAP, 128)
    right = got_ref[:, 32:64, :].reshape(DEV * CAP, 128)
    both = jnp.concatenate([left, right], axis=1)
    wanted = iota((512, 128), 0) * 4
    upper = iota((8, 128), 0) < 4
    for load in loads:
        load.wait()
    for c in range(4):
        chosen = jnp.concatenate(
            [
                jnp.where(wanted == label_ref[k : k + 1, :] - c, 1.0, 0.0).astype(BF16)
                for k in range(32)
            ],
            axis=1,
        )
        total = THERMAL_FACTOR * jnp.dot(chosen, both, preferred_element_type=F32)
        for h in range(2):
            xb = 2 * c + h
            part = total[:, 128 * h : 128 * h + 128]
            cells = part.reshape(NZ * 8, 8, 128)
            source_ref[:, xb] = cells
            short = part.astype(BF16).reshape(NZ * 4, 16, 128)
            low_ref[:, xb] = short[:12]
            high_ref[:, xb] = short[20:]
            for z in range(NZ):
                front_ref[z, xb] = jnp.where(
                    upper, first_ref[z, xb].astype(F32), pltpu.roll(cells[8 * z], 4, 0)
                ).astype(BF16)
                back_ref[z, xb] = jnp.where(
                    upper, pltpu.roll(cells[8 * z + 7], 4, 0), last_ref[z, xb].astype(F32)
                ).astype(BF16)


def fill_coefficients(coef_ref, table_ref, label_ref, halo):
    base = lax.axis_index("slab") * NZ - halo
    spot = iota((8, 128), 0) * 128 + iota((8, 128), 1)

    def layer(i, _):
        z = base + i
        inside = jnp.where((z >= 0) & (z < LAYERS), 1.0, 0.0).astype(F32)
        material = lambda at: label_ref[jnp.clip(at, 0, LAYERS - 1)]
        here = material(z)
        splat = lambda m, k: jnp.full((8, 128), table_ref[m, k], F32)
        kx = splat(here, 0)
        ky = splat(here, 1)
        a = splat(here, 2)
        above = splat(material(z + 1), 2)
        below = splat(material(z - 1), 2)
        up = 2.0 * a * above / (a + above)
        down = 2.0 * a * below / (a + below)
        keep = jnp.full((8, 128), inside, F32)
        coef_ref[i, 0] = keep * (1.0 - 2.0 * kx - 2.0 * ky - up - down)
        coef_ref[i, 1] = keep * jnp.where(spot == 0, 0.0, kx)
        coef_ref[i, 2] = keep * jnp.where(spot == 1023, 0.0, kx)
        coef_ref[i, 3] = keep * ky
        coef_ref[i, 4] = keep * up
        coef_ref[i, 5] = keep * down
        return 0

    lax.fori_loop(0, NZ + 2 * halo, layer, 0)


def diffuse(coef, read, write, layers, ranges, low, high):
    lane = iota((8, 128), 1)

    def layer(z, _):
        c = [coef(z, j) for j in range(6)]
        for rows in ranges:
            before, cell = read(z, rows[0] - 1), read(z, rows[0])
            for y in range(rows[0], rows[1]):
                after = read(z, y + 1)
                step = pltpu.roll(cell, 127, 1)
                right = jnp.where(lane == 127, pltpu.roll(step, 7, 0), step)
                step = pltpu.roll(cell, 1, 1)
                left = jnp.where(lane == 0, pltpu.roll(step, 1, 0), step)
                value = (
                    c[0] * cell
                    + c[1] * left
                    + c[2] * right
                    + c[3] * (before + after)
                    + c[4] * read(z + 1, y)
                    + c[5] * read(z - 1, y)
                )
                if y < 0:
                    value = value * low
                if y >= NY:
                    value = value * high
                write(z, y, value)
                before, cell = cell, after
        return 0

    count = layers[1] - layers[0]
    unroll = 2 if count % 2 == 0 else 3 if count % 3 == 0 else 1
    lax.fori_loop(layers[0], layers[1], layer, 0, unroll=unroll)


def edges(axis, count):
    at = lax.axis_index(axis)
    low = jnp.full((8, 128), jnp.where(at > 0, 1.0, 0.0), F32)
    high = jnp.full((8, 128), jnp.where(at < count - 1, 1.0, 0.0), F32)
    return low, high


def row_of(z, y, halo):
    return pl.ds(pl.multiple_of((z * (NY + 8) + (y + 4)) * 8, 8), 8)


def temperature_kernel(
    table_ref, label_ref, state_ref, low_ref, high_ref, out_ref, coef_ref, cells_ref, a_ref, b_ref,
):
    halo = 4
    fill_coefficients(coef_ref, table_ref, label_ref, halo)

    def spread(z, block, value):
        for xb in range(8):
            cells_ref[z, block, pl.ds(xb * 8, 8), :] = value[:, 128 * xb : 128 * xb + 128]

    def gather(z, keep=None):
        for y in range(NY):
            value = cells_ref[z, y // 8, pl.ds(y % 8, 8, stride=8), :]
            a_ref[row_of(z, y, halo), :] = value if keep is None else value * keep

    def clear(z, _):
        for y in (-3, -2, -1, NY, NY + 1, NY + 2):
            a_ref[row_of(z, y, halo), :] = jnp.zeros((8, 128), F32)
            b_ref[row_of(z, y, halo), :] = jnp.zeros((8, 128), F32)
        return 0

    lax.fori_loop(0, NZ + 2 * halo, clear, 0)
    for z in (0, NZ + 2 * halo - 1):
        for y in range(NY):
            a_ref[row_of(z, y, halo), :] = jnp.zeros((8, 128), F32)

    def own(z, _):
        for block in range(8):
            spread(z + halo, block, state_ref[z, 8 * block : 8 * block + 8, :])
        gather(z + halo)
        return 0

    lax.fori_loop(0, NZ, own, 0)

    below, above = edges("slab", SLABS)

    def outer(z, _):
        for base, body, keep in ((1, low_ref, below), (12, high_ref, above)):
            for block in range(4):
                two = body[z, 16 * block : 16 * block + 16, :].astype(F32)
                spread(z + base, 2 * block, two[:8])
                spread(z + base, 2 * block + 1, two[8:])
            gather(z + base, keep)
        return 0

    lax.fori_loop(0, halo - 1, outer, 0)
    low, high = edges("logic", LOGICS)
    bufs = (a_ref, b_ref)
    for step in range(4):
        src, dst = bufs[step % 2], bufs[(step + 1) % 2]
        reach = 3 - step
        wide = (1, 2, 1, 0)[step]

        def read(z, y, src=src):
            return src[row_of(z, y, halo), :]

        def write(z, y, value, dst=dst, step=step):
            if step == 3:
                out_ref[pl.ds(pl.multiple_of(((z - halo) * NY + y) * 8, 8), 8), :] = value
            else:
                dst[row_of(z, y, halo), :] = value

        diffuse(
            lambda z, j: coef_ref[z, j],
            read,
            write,
            (halo - reach, halo + NZ + reach),
            [(-wide, NY + wide)],
            low,
            high,
        )


def inner_kernel(coef_ref, source_ref, s_ref, a_ref, b_ref):
    halo = 3

    def own(z, _):
        for y in range(NY):
            start = (z * 8 + y // 8) * 64 + y % 8
            s_ref[row_of(z + halo, y, halo), :] = source_ref[pl.ds(start, 8, stride=8), :]
        return 0

    lax.fori_loop(0, NZ, own, 0)
    for step, (src, dst) in enumerate(((s_ref, a_ref), (a_ref, b_ref))):

        def read(z, y, src=src):
            return src[row_of(z, y, halo), :]

        def write(z, y, value, dst=dst):
            dst[row_of(z, y, halo), :] = value + s_ref[row_of(z, y, halo), :]

        diffuse(
            lambda z, j: coef_ref[z + 1, j],
            read,
            write,
            (halo + 1 + step, halo + NZ - 1 - step),
            [(2 + step, NY - 2 - step)],
            None,
            None,
        )


def outer_kernel(
    _s, _a, _b, coef_ref, base_ref, far_low_ref, far_high_ref, low_ref, high_ref, front_ref, back_ref,
    corner_low_ref, corner_high_ref, out_hbm, coarse_ref, s_ref, a_ref, b_ref,
    out_ref, cells_ref, rim_ref, edge_ref, sums_ref, sems,
):
    halo = 3
    zero = jnp.zeros((8, 128), F32)
    coef = lambda z, j: coef_ref[z + 1, j]

    def rim_at(z, y):
        slot = y + 4 if y < 1 else y - NY + 6
        return pl.ds(pl.multiple_of(((z + 1) * 10 + slot) * 8, 8), 8)

    def edge_at(z, y):
        slot = y + 3 if y < 1 else y - NY + 5
        return pl.ds(pl.multiple_of((z * 8 + slot) * 8, 8), 8)

    low, high = edges("logic", LOGICS)
    below, above = edges("slab", SLABS)

    def strips(z, slot, front, back, keep_front, keep_back):
        for xb in range(8):
            cells_ref[slot, pl.ds(xb * 8, 8), :] = front(xb).astype(F32)
            cells_ref[slot + 1, pl.ds(xb * 8, 8), :] = back(xb).astype(F32)
        rim_ref[rim_at(z, 0), :] = zero
        rim_ref[rim_at(z, NY - 1), :] = zero
        for at in range(8):
            before = cells_ref[slot, pl.ds(at, 8, stride=8), :] * keep_front
            after = cells_ref[slot + 1, pl.ds(at, 8, stride=8), :] * keep_back
            if at < 4:
                rim_ref[rim_at(z, NY + at), :] = after
                if at:
                    s_ref[row_of(z, at - 4, halo), :] = before
            else:
                rim_ref[rim_at(z, at - 8), :] = before
                if at < 7:
                    s_ref[row_of(z, NY + at - 4, halo), :] = after

    rim_ref[pl.ds(0, 80), :] = jnp.zeros((80, 128), F32)
    rim_ref[pl.ds(15 * 80, 80), :] = jnp.zeros((80, 128), F32)

    def own(i, _):
        for half in range(2):
            z = 2 * i + half
            strips(
                z + halo, 2 * half, lambda xb: front_ref[z, xb], lambda xb: back_ref[z, xb], low, high
            )
        return 0

    lax.fori_loop(0, NZ // 2, own, 0)

    def outer(z, _):
        for side, (base, body, corner, keep) in enumerate(
            ((0, low_ref, corner_low_ref, below), (11, high_ref, corner_high_ref, above))
        ):
            for block in range(4):
                slot = 8 * side + 2 * block
                for xb in range(8):
                    two = body[z * 4 + block, xb].astype(F32)
                    cells_ref[slot, pl.ds(xb * 8, 8), :] = two[:8]
                    cells_ref[slot + 1, pl.ds(xb * 8, 8), :] = two[8:]
                for y in range(16):
                    s_ref[row_of(z + base, 16 * block + y, halo), :] = (
                        cells_ref[slot + y // 8, pl.ds(y % 8, 8, stride=8), :] * keep
                    )
            strips(
                z + base,
                16 + 2 * side,
                lambda xb: corner[z, xb].astype(F32)[:8],
                lambda xb: corner[z, xb].astype(F32)[8:],
                keep * low,
                keep * high,
            )
        return 0

    lax.fori_loop(0, halo, outer, 0)
    for side, (z, j, body, keep) in enumerate(((0, 5, far_low_ref, below), (13, 4, far_high_ref, above))):
        factor = coef(z, j) * keep
        for block in range(4):
            slot = 8 * side + 2 * block
            two = body[0, 16 * block : 16 * block + 16, :].astype(F32)
            for xb in range(8):
                part = two[:, 128 * xb : 128 * xb + 128]
                cells_ref[slot, pl.ds(xb * 8, 8), :] = part[:8]
                cells_ref[slot + 1, pl.ds(xb * 8, 8), :] = part[8:]
            for y in range(16):
                at = row_of(z, 16 * block + y, halo)
                s_ref[at, :] = (
                    s_ref[at, :] + factor * cells_ref[slot + y // 8, pl.ds(y % 8, 8, stride=8), :]
                )

    def read_rim(z, y):
        return rim_ref[rim_at(z, y), :]

    def write_edge(z, y, value):
        edge_ref[edge_at(z, y), :] = value + s_ref[row_of(z, y, halo), :]
        if y == -1:
            edge_ref[edge_at(z, 0), :] = (
                coef(z, 3) * read_rim(z, -1) + s_ref[row_of(z, 0, halo), :]
            )
        if y == NY:
            edge_ref[edge_at(z, NY - 1), :] = (
                coef(z, 3) * read_rim(z, NY) + s_ref[row_of(z, NY - 1, halo), :]
            )

    diffuse(coef, read_rim, write_edge, (0, NZ + 2 * halo), [(-3, 0), (NY, NY + 3)], low, high)

    def first(z, y):
        if 1 <= y < NY - 1:
            return s_ref[row_of(z, y, halo), :]
        return edge_ref[edge_at(z, y), :]

    def second(z, y):
        return a_ref[row_of(z, y, halo), :]

    def third(z, y):
        return b_ref[row_of(z, y, halo), :]

    def to(ref):
        def write(z, y, value):
            ref[row_of(z, y, halo), :] = value + s_ref[row_of(z, y, halo), :]

        return write

    every = lambda reach: [(-reach, NY + reach)]
    diffuse(coef, first, to(a_ref), (1, 4), every(2), low, high)
    diffuse(coef, first, to(a_ref), (10, 13), every(2), low, high)
    diffuse(coef, first, to(a_ref), (4, 10), [(-2, 2), (NY - 2, NY + 2)], low, high)
    diffuse(coef, second, to(b_ref), (2, 5), every(1), low, high)
    diffuse(coef, second, to(b_ref), (9, 12), every(1), low, high)
    diffuse(coef, second, to(b_ref), (5, 9), [(-1, 3), (NY - 3, NY + 1)], low, high)

    def store(z):
        return pltpu.make_async_copy(out_ref.at[z], out_hbm.at[z], sems.at[z])

    def write_out(z, y, value):
        own = z - halo
        value = value + s_ref[row_of(z, y, halo), :]
        value = value + base_ref[pl.ds(pl.multiple_of((own * NY + y) * 8, 8), 8), :]
        out_ref[own, y // 8, pl.ds(y % 8, 8, stride=8), :] = value
        here = pl.ds(pl.multiple_of((own * 4 + y // 16) * 8, 8), 8)
        if y % 16 == 0:
            sums_ref[here, :] = value
        else:
            sums_ref[here, :] = sums_ref[here, :] + value
        if y == NY - 1:
            store(own).start()

    diffuse(coef, third, write_out, (halo, halo + NZ), every(0), low, high)
    exact = lax.Precision.HIGHEST
    lines = lax.dot_general(
        jnp.ones((8, 128), F32), sums_ref[...], (((1,), (1,)), ((), ())),
        precision=exact, preferred_element_type=F32,
    )
    pairs = jnp.where((iota((256, 128), 0) >> 1) == iota((256, 128), 1), 1.0 / 4096.0, 0.0)
    means = jnp.dot(lines, pairs, precision=exact, preferred_element_type=F32)
    coarse_ref[...] = jnp.broadcast_to(means[0:1, :], (DEV, 128))
    for z in range(NZ):
        store(z).wait()


def vmem(count):
    return [pl.BlockSpec(memory_space=pltpu.VMEM)] * count


def smem(count):
    return [pl.BlockSpec(memory_space=pltpu.SMEM)] * count


def params():
    return pltpu.CompilerParams(vmem_limit_bytes=VMEM)


def cost(flops, moved):
    return pl.CostEstimate(flops=flops, bytes_accessed=moved, transcendentals=0)


def shift(value, axis, by):
    count = lax.axis_size(axis)
    return lax.ppermute(value, axis, [(i, (i + by) % count) for i in range(count)])


def per_device(
    initial_heat_state,
    dynamic_wattage,
    drain_multiplier,
    holder_processor,
    patch_target_slot,
    active_patch_number,
    prior_reduced_heat_map,
    conductivity_lookup,
    substance_of_slab,
):
    state = initial_heat_state
    both = ("logic", "slab")
    shape = jax.ShapeDtypeStruct
    to_high, to_low, far_high, far_low, t_first, t_last = pl.pallas_call(
        edge_kernel,
        grid=(NZ // 2,),
        out_shape=[
            shape((3, NY, 1024), BF16),
            shape((3, NY, 1024), BF16),
            shape((1, NY, 1024), BF16),
            shape((1, NY, 1024), BF16),
            shape((2, 4, 8, 8, 128), BF16),
            shape((2, 4, 8, 8, 128), BF16),
        ],
        in_specs=[
            pl.BlockSpec((1, NY, 1024), lambda i: (i, 0, 0)),
            pl.BlockSpec((1, NY, 1024), lambda i: (i + NZ // 2, 0, 0)),
        ],
        out_specs=[
            pl.BlockSpec((1, NY, 1024), lambda i: (jnp.maximum(i - 1, 0), 0, 0)),
            pl.BlockSpec((1, NY, 1024), lambda i: (jnp.minimum(i, 2), 0, 0)),
            pl.BlockSpec((1, NY, 1024), lambda i: (0, 0, 0)),
            pl.BlockSpec((1, NY, 1024), lambda i: (0, 0, 0)),
            pl.BlockSpec((2, 1, 8, 8, 128), lambda i: (0, i, 0, 0, 0)),
            pl.BlockSpec((2, 1, 8, 8, 128), lambda i: (0, i, 0, 0, 0)),
        ],
        compiler_params=params(),
        cost_estimate=cost(1_000_000, 5_000_000),
        name="edges",
    )(state, state)
    low = shift(to_high, "slab", 1)
    high = shift(to_low, "slab", -1)

    packed = pl.pallas_call(
        pack_kernel,
        out_shape=pltpu.HBM((DEV, ROWS, 128), BF16),
        in_specs=smem(1) + [pl.BlockSpec(memory_space=pltpu.HBM)] * 5,
        out_specs=pl.BlockSpec(memory_space=pltpu.HBM),
        scratch_shapes=[
            pltpu.VMEM((1, TILES), I32),
            pltpu.VMEM((1, TILES), I32),
            pltpu.VMEM((1, TILES), F32),
            pltpu.VMEM((LAYERS, 128), F32),
            pltpu.VMEM((TILES, 256), BF16),
            pltpu.VMEM((DEV, ROWS, 128), BF16),
            pltpu.VMEM((DEV, TILES), F32),
            pltpu.VMEM((CAP, TILES), BF16),
            pltpu.VMEM((DEV, 128), F32),
            pltpu.VMEM((DEV, 128), F32),
            pltpu.VMEM((TILES, 256), BF16),
            pltpu.SemaphoreType.DMA((5,)),
            pltpu.SemaphoreType.DMA((DEV // GROUP,)),
        ],
        compiler_params=params(),
        cost_estimate=cost(5_000_000_000, 4_000_000),
        name="pack",
    )(
        active_patch_number,
        holder_processor.reshape(1, TILES),
        patch_target_slot.reshape(1, TILES),
        drain_multiplier.reshape(1, TILES),
        prior_reduced_heat_map.transpose(1, 2, 0).reshape(128, LAYERS),
        dynamic_wattage,
    )
    packed, low, high, far_high, far_low = lax.optimization_barrier(
        (packed, low, high, far_high, far_low)
    )
    t_low = shift(far_high, "slab", 1)
    t_high = shift(far_low, "slab", -1)
    got = lax.all_to_all(packed, both, split_axis=0, concat_axis=0, tiled=True)

    base, coef = pl.pallas_call(
        temperature_kernel,
        out_shape=[shape((NZ * NY * 8, 128), F32), shape((16, 6, 8, 128), F32)],
        in_specs=smem(2) + vmem(3),
        out_specs=vmem(2),
        scratch_shapes=[
            pltpu.VMEM((16, 8, 64, 128), F32),
            pltpu.VMEM((16 * 72 * 8, 128), F32),
            pltpu.VMEM((16 * 72 * 8, 128), F32),
        ],
        compiler_params=params(),
        cost_estimate=cost(100_000_000, 20_000_000),
        name="diffuse_temperature",
    )(conductivity_lookup, substance_of_slab, state, low, high)
    got, base, coef = lax.optimization_barrier((got, base, coef))

    source, lower, upper, first, last = pl.pallas_call(
        scatter_kernel,
        out_shape=[
            shape((64, 8, 8, 128), F32),
            shape((12, 8, 16, 128), BF16),
            shape((12, 8, 16, 128), BF16),
            shape((NZ, 8, 8, 128), BF16),
            shape((NZ, 8, 8, 128), BF16),
        ],
        in_specs=vmem(1) + [pl.BlockSpec(memory_space=pltpu.HBM)] * 2,
        out_specs=vmem(5),
        scratch_shapes=[
            pltpu.VMEM((32, 128), I32),
            pltpu.VMEM((NZ, 8, 8, 128), BF16),
            pltpu.VMEM((NZ, 8, 8, 128), BF16),
            pltpu.SemaphoreType.DMA((2,)),
        ],
        compiler_params=params(),
        cost_estimate=cost(5_000_000_000, 6_000_000),
        name="place_tiles",
    )(
        got,
        pltpu.with_memory_space_constraint(t_first.reshape(NZ, 8, 8, 128), pltpu.HBM),
        pltpu.with_memory_space_constraint(t_last.reshape(NZ, 8, 8, 128), pltpu.HBM),
    )
    lower, upper, first, last, t_low, t_high = lax.optimization_barrier(
        (lower, upper, first, last, t_low, t_high)
    )
    s_low = shift(upper, "slab", 1)
    s_high = shift(lower, "slab", -1)
    s_front = shift(last, "logic", 1)
    s_back = shift(first, "logic", -1)
    to_high, to_low = pl.pallas_call(
        corner_kernel,
        out_shape=[shape((3, 8, 16, 128), BF16)] * 2,
        in_specs=vmem(2),
        out_specs=vmem(2),
        compiler_params=params(),
        cost_estimate=cost(1_000_000, 1_000_000),
        name="corners",
    )(s_front, s_back)
    s_corner_low = shift(to_high, "slab", 1)
    s_corner_high = shift(to_low, "slab", -1)

    rows = pltpu.VMEM((14 * 72 * 8, 128), F32)
    parts = pl.pallas_call(
        inner_kernel,
        out_shape=[rows] * 3,
        in_specs=vmem(2),
        out_specs=vmem(3),
        compiler_params=params(),
        cost_estimate=cost(20_000_000, 10_000_000),
        name="diffuse_inner",
    )(coef, source.reshape(4096, 128))
    new_state, coarse, *_ = pl.pallas_call(
        outer_kernel,
        out_shape=[pltpu.HBM((NZ, 8, 64, 128), F32), shape((DEV, 128), F32)] + [rows] * 3,
        in_specs=vmem(13),
        out_specs=[pl.BlockSpec(memory_space=pltpu.HBM)] + vmem(4),
        input_output_aliases={0: 2, 1: 3, 2: 4},
        scratch_shapes=[
            pltpu.VMEM((NZ, 8, 64, 128), F32),
            pltpu.VMEM((20, 64, 128), F32),
            pltpu.VMEM((16 * 80, 128), F32),
            pltpu.VMEM((14 * 64, 128), F32),
            pltpu.VMEM((256, 128), F32),
            pltpu.SemaphoreType.DMA((NZ,)),
        ],
        compiler_params=params(),
        cost_estimate=cost(100_000_000, 20_000_000),
        name="diffuse_outer",
    )(*parts, coef, base, t_low, t_high, s_low, s_high, s_front, s_back, s_corner_low, s_corner_high)
    thermal_state = (
        new_state.reshape(NZ, 8, 8, 8, 128).transpose(0, 1, 3, 2, 4).reshape(NZ, NY, 1024)
    )
    gathered = lax.all_to_all(coarse, both, split_axis=0, concat_axis=0, tiled=True)
    reduced_map = gathered.reshape(LOGICS, SLABS, NZ, 4, 4)
    reduced_map = jnp.transpose(reduced_map, (1, 2, 0, 3, 4)).reshape(LAYERS, 32, 4)
    return (thermal_state, reduced_map)


def solution(mesh):
    return jax.shard_map(
        per_device,
        mesh=mesh,
        in_specs=(
            P("slab", "logic", None),
            P(("logic", "slab"), None),
            P(("logic", "slab")),
            P(("logic", "slab"), None),
            P(("logic", "slab")),
            P(("logic", "slab")),
            P(),
            P(),
            P(),
        ),
        out_specs=(P("slab", "logic", None), P()),
        check_vma=False,
    )
```

```python
import functools

import jax
import jax.numpy as jnp
from jax import lax
from jax.experimental import pallas as pl
from jax.experimental.pallas import tpu as pltpu
from jax.sharding import PartitionSpec as P

LEAK_BETA = 0.7
THERMAL_FACTOR = 0.1

DEV = 128
CAP = 32
TILES = 2048
NZ = 8
NY = 64
LAYERS = 128
SLABS = 16
LOGICS = 8
ROWS = 72
GROUP = 32
VMEM = 28 * 1024 * 1024
F32 = jnp.float32
BF16 = jnp.bfloat16
I32 = jnp.int32


def iota(shape, dim):
    return lax.broadcasted_iota(I32, shape, dim)


def edge_kernel(
    lower_ref, upper_ref, to_high_ref, to_low_ref, far_high_ref, far_low_ref, first_ref, last_ref
):
    step = pl.program_id(0)

    @pl.when(step < 3)
    def _():
        to_low_ref[...] = lower_ref[...].astype(BF16)

    @pl.when(step == 3)
    def _():
        far_low_ref[...] = lower_ref[...].astype(BF16)

    @pl.when(step > 0)
    def _():
        to_high_ref[...] = upper_ref[...].astype(BF16)

    @pl.when(step == 0)
    def _():
        far_high_ref[...] = upper_ref[...].astype(BF16)

    for half, ref in ((0, lower_ref), (1, upper_ref)):
        for xb in range(8):
            cols = slice(128 * xb, 128 * xb + 128)
            first_ref[half, 0, xb] = ref[0, :8, cols].astype(BF16)
            last_ref[half, 0, xb] = ref[0, NY - 8 :, cols].astype(BF16)


def corner_kernel(front_ref, back_ref, low_ref, high_ref):
    for out, first in ((low_ref, NZ - 3), (high_ref, 0)):
        for z in range(3):
            for xb in range(8):
                out[z, xb] = jnp.concatenate(
                    [front_ref[first + z, xb].astype(F32), back_ref[first + z, xb].astype(F32)], axis=0
                ).astype(BF16)


def pack_kernel(
    count_ref, owner_hbm, target_hbm, drain_hbm, prior_hbm, watt_hbm, out_hbm,
    owner_ref, target_ref, drain_ref, prior_ref, watt_ref, out_ref,
    member_ref, pick_ref, high_ref, low_ref, power_ref, in_sems, out_sems,
):
    loads = [
        pltpu.make_async_copy(src, dst, in_sems.at[i])
        for i, (src, dst) in enumerate(
            (
                (owner_hbm, owner_ref),
                (target_hbm, target_ref),
                (prior_hbm, prior_ref),
                (drain_hbm, drain_ref),
                (watt_hbm, watt_ref),
            )
        )
    ]
    for load in loads:
        load.start()
    for load in loads[:4]:
        load.wait()
    owner = owner_ref[...]
    target = target_ref[...]
    live = iota((1, TILES), 1) < count_ref[0]
    layer = (owner & (SLABS - 1)) * NZ + (target >> 8)
    column = (owner >> 4) * 16 + ((target >> 6) & 3) * 4 + (target & 3)
    at_layer = jnp.where(iota((LAYERS, TILES), 0) == layer, 1.0, 0.0).astype(BF16)
    prior = prior_ref[...]
    first = prior.astype(BF16)
    rest = prior - first.astype(F32)
    second = rest.astype(BF16)
    third = (rest - second.astype(F32)).astype(BF16)
    lookup = lambda part: lax.dot_general(
        part, at_layer, (((1,), (0,)), ((), ())), preferred_element_type=F32
    )
    picked = lookup(first) + lookup(second) + lookup(third)
    heat = jnp.sum(
        jnp.where(iota((LAYERS, TILES), 0) == column, picked, 0.0), axis=0, keepdims=True
    )
    scale = 1.0 + drain_ref[...] * jnp.exp(LEAK_BETA * heat)
    member = jnp.where(iota((DEV, TILES), 0) == jnp.where(live, owner, -1), 1.0, 0.0)
    member_ref[...] = member
    before = jnp.where(iota((256, 256), 0) < iota((256, 256), 1), 1.0, 0.0).astype(BF16)
    carry = jnp.zeros((DEV, 1), F32)
    ranks = []
    for b in range(TILES // 256):
        part = member[:, 256 * b : 256 * b + 256]
        earlier = jnp.dot(part.astype(BF16), before, preferred_element_type=F32) + carry
        ranks.append(jnp.sum(earlier * part, axis=0, keepdims=True))
        carry = carry + jnp.sum(part, axis=1, keepdims=True)
    rank = jnp.where(live, jnp.concatenate(ranks, axis=1).astype(I32), -1)
    pick_ref[...] = jnp.where(iota((CAP, TILES), 0) == rank, 1.0, 0.0).astype(BF16)
    slot = (iota((128, TILES), 0) & (CAP - 1)) == rank
    flat = member.astype(BF16)
    spot = lambda value: lax.dot_general(
        flat,
        jnp.where(slot, value.astype(F32), 0.0).astype(BF16),
        (((1,), (1,)), ((), ())),
        preferred_element_type=F32,
    )
    high_ref[...] = spot((target >> 6) + 1)
    low_ref[...] = spot(target & 63)
    row8 = iota((8, 128), 0)
    loads[4].wait()
    for b in range(TILES // 128):
        rows = pl.ds(128 * b, 128)
        spread = jnp.transpose(jnp.broadcast_to(scale[:, 128 * b : 128 * b + 128], (128, 128)))
        for h in range(2):
            cols = pl.ds(128 * h, 128)
            power_ref[rows, cols] = (watt_ref[rows, cols].astype(F32) * spread).astype(BF16)

    def store(g):
        here = pl.ds(g * GROUP, GROUP)
        return pltpu.make_async_copy(out_ref.at[here], out_hbm.at[here], out_sems.at[g])

    def group(g, _):
        pick = pick_ref[...]
        parts = []
        for j in range(GROUP):
            d = g * GROUP + j
            parts.append(pick * member_ref[pl.ds(d, 1), :].astype(BF16))
            label = jnp.where(
                row8 == 0,
                high_ref[pl.ds(d, 1), :],
                jnp.where(row8 == 1, low_ref[pl.ds(d, 1), :], 0.0),
            )
            out_ref[d, 64:72, :] = label.astype(BF16)
        packed = jnp.dot(
            jnp.concatenate(parts, axis=0), power_ref[...], preferred_element_type=F32
        ).astype(BF16)
        here = pl.ds(g * GROUP, GROUP)
        out_ref[here, 0:32, :] = packed[:, :128].reshape(GROUP, CAP, 128)
        out_ref[here, 32:64, :] = packed[:, 128:].reshape(GROUP, CAP, 128)
        store(g).start()
        return 0

    lax.fori_loop(0, DEV // GROUP, group, 0)
    for g in range(DEV // GROUP):
        store(g).wait()


def scatter_kernel(
    got_ref, first_hbm, last_hbm, source_ref, low_ref, high_ref, front_ref, back_ref,
    label_ref, first_ref, last_ref, sems,
):
    loads = [
        pltpu.make_async_copy(first_hbm, first_ref, sems.at[0]),
        pltpu.make_async_copy(last_hbm, last_ref, sems.at[1]),
    ]
    for load in loads:
        load.start()
    labels = got_ref[:, 64:72, :].reshape(DEV * 8, 128)
    row = iota((DEV * 8, 128), 0)
    lane = iota((DEV * 8, 128), 1)
    labels = jnp.where((lane >> 5) == ((row >> 3) & 3), labels.astype(F32), 0.0).astype(BF16)
    g = iota((32, DEV * 8), 0)
    col = iota((32, DEV * 8), 1)
    weight = jnp.where((col & 7) == 0, 64.0, jnp.where((col & 7) == 1, 1.0, 0.0))
    weight = jnp.where((col >> 5) == g, weight, 0.0).astype(BF16)
    target = jnp.dot(weight, labels, preferred_element_type=F32).astype(I32) - 64
    label_ref[...] = target
    left = got_ref[:, 0:32, :].reshape(DEV * CAP, 128)
    right = got_ref[:, 32:64, :].reshape(DEV * CAP, 128)
    both = jnp.concatenate([left, right], axis=1)
    wanted = iota((512, 128), 0) * 4
    upper = iota((8, 128), 0) < 4
    for load in loads:
        load.wait()
    for c in range(4):
        chosen = jnp.concatenate(
            [
                jnp.where(wanted == label_ref[k : k + 1, :] - c, 1.0, 0.0).astype(BF16)
                for k in range(32)
            ],
            axis=1,
        )
        total = THERMAL_FACTOR * jnp.dot(chosen, both, preferred_element_type=F32)
        for h in range(2):
            xb = 2 * c + h
            part = total[:, 128 * h : 128 * h + 128]
            cells = part.reshape(NZ * 8, 8, 128)
            source_ref[:, xb] = cells
            short = part.astype(BF16).reshape(NZ * 4, 16, 128)
            low_ref[:, xb] = short[:12]
            high_ref[:, xb] = short[20:]
            for z in range(NZ):
                front_ref[z, xb] = jnp.where(
                    upper, first_ref[z, xb].astype(F32), pltpu.roll(cells[8 * z], 4, 0)
                ).astype(BF16)
                back_ref[z, xb] = jnp.where(
                    upper, pltpu.roll(cells[8 * z + 7], 4, 0), last_ref[z, xb].astype(F32)
                ).astype(BF16)


def fill_coefficients(coef_ref, table_ref, label_ref, halo):
    base = lax.axis_index("slab") * NZ - halo
    spot = iota((8, 128), 0) * 128 + iota((8, 128), 1)

    def layer(i, _):
        z = base + i
        inside = jnp.where((z >= 0) & (z < LAYERS), 1.0, 0.0).astype(F32)
        material = lambda at: label_ref[jnp.clip(at, 0, LAYERS - 1)]
        here = material(z)
        splat = lambda m, k: jnp.full((8, 128), table_ref[m, k], F32)
        kx = splat(here, 0)
        ky = splat(here, 1)
        a = splat(here, 2)
        above = splat(material(z + 1), 2)
        below = splat(material(z - 1), 2)
        up = 2.0 * a * above / (a + above)
        down = 2.0 * a * below / (a + below)
        keep = jnp.full((8, 128), inside, F32)
        coef_ref[i, 0] = keep * (1.0 - 2.0 * kx - 2.0 * ky - up - down)
        coef_ref[i, 1] = keep * jnp.where(spot == 0, 0.0, kx)
        coef_ref[i, 2] = keep * jnp.where(spot == 1023, 0.0, kx)
        coef_ref[i, 3] = keep * ky
        coef_ref[i, 4] = keep * up
        coef_ref[i, 5] = keep * down
        return 0

    lax.fori_loop(0, NZ + 2 * halo, layer, 0)


def diffuse(coef, read, write, layers, ranges, low, high):
    lane = iota((8, 128), 1)

    def layer(z, _):
        c = [coef(z, j) for j in range(6)]
        for rows in ranges:
            before, cell = read(z, rows[0] - 1), read(z, rows[0])
            for y in range(rows[0], rows[1]):
                after = read(z, y + 1)
                step = pltpu.roll(cell, 127, 1)
                right = jnp.where(lane == 127, pltpu.roll(step, 7, 0), step)
                step = pltpu.roll(cell, 1, 1)
                left = jnp.where(lane == 0, pltpu.roll(step, 1, 0), step)
                value = (
                    c[0] * cell
                    + c[1] * left
                    + c[2] * right
                    + c[3] * (before + after)
                    + c[4] * read(z + 1, y)
                    + c[5] * read(z - 1, y)
                )
                if y < 0:
                    value = value * low
                if y >= NY:
                    value = value * high
                write(z, y, value)
                before, cell = cell, after
        return 0

    count = layers[1] - layers[0]
    unroll = 2 if count % 2 == 0 else 3 if count % 3 == 0 else 1
    lax.fori_loop(layers[0], layers[1], layer, 0, unroll=unroll)


def edges(axis, count):
    at = lax.axis_index(axis)
    low = jnp.full((8, 128), jnp.where(at > 0, 1.0, 0.0), F32)
    high = jnp.full((8, 128), jnp.where(at < count - 1, 1.0, 0.0), F32)
    return low, high


def row_of(z, y, halo):
    return pl.ds(pl.multiple_of((z * (NY + 8) + (y + 4)) * 8, 8), 8)


def temperature_kernel(
    table_ref, label_ref, state_ref, low_ref, high_ref, out_ref, coef_ref, cells_ref, a_ref, b_ref,
):
    halo = 4
    fill_coefficients(coef_ref, table_ref, label_ref, halo)

    def spread(z, block, value):
        for xb in range(8):
            cells_ref[z, block, pl.ds(xb * 8, 8), :] = value[:, 128 * xb : 128 * xb + 128]

    def gather(z, keep=None):
        for y in range(NY):
            value = cells_ref[z, y // 8, pl.ds(y % 8, 8, stride=8), :]
            a_ref[row_of(z, y, halo), :] = value if keep is None else value * keep

    def clear(z, _):
        for y in (-3, -2, -1, NY, NY + 1, NY + 2):
            a_ref[row_of(z, y, halo), :] = jnp.zeros((8, 128), F32)
            b_ref[row_of(z, y, halo), :] = jnp.zeros((8, 128), F32)
        return 0

    lax.fori_loop(0, NZ + 2 * halo, clear, 0)
    for z in (0, NZ + 2 * halo - 1):
        for y in range(NY):
            a_ref[row_of(z, y, halo), :] = jnp.zeros((8, 128), F32)

    def own(z, _):
        for block in range(8):
            spread(z + halo, block, state_ref[z, 8 * block : 8 * block + 8, :])
        gather(z + halo)
        return 0

    lax.fori_loop(0, NZ, own, 0)

    below, above = edges("slab", SLABS)

    def outer(z, _):
        for base, body, keep in ((1, low_ref, below), (12, high_ref, above)):
            for block in range(4):
                two = body[z, 16 * block : 16 * block + 16, :].astype(F32)
                spread(z + base, 2 * block, two[:8])
                spread(z + base, 2 * block + 1, two[8:])
            gather(z + base, keep)
        return 0

    lax.fori_loop(0, halo - 1, outer, 0)
    low, high = edges("logic", LOGICS)
    bufs = (a_ref, b_ref)
    for step in range(4):
        src, dst = bufs[step % 2], bufs[(step + 1) % 2]
        reach = 3 - step
        wide = (1, 2, 1, 0)[step]

        def read(z, y, src=src):
            return src[row_of(z, y, halo), :]

        def write(z, y, value, dst=dst, step=step):
            if step == 3:
                out_ref[pl.ds(pl.multiple_of(((z - halo) * NY + y) * 8, 8), 8), :] = value
            else:
                dst[row_of(z, y, halo), :] = value

        diffuse(
            lambda z, j: coef_ref[z, j],
            read,
            write,
            (halo - reach, halo + NZ + reach),
            [(-wide, NY + wide)],
            low,
            high,
        )


def inner_kernel(coef_ref, source_ref, s_ref, a_ref, b_ref):
    halo = 3

    def own(z, _):
        for y in range(NY):
            start = (z * 8 + y // 8) * 64 + y % 8
            s_ref[row_of(z + halo, y, halo), :] = source_ref[pl.ds(start, 8, stride=8), :]
        return 0

    lax.fori_loop(0, NZ, own, 0)
    for step, (src, dst) in enumerate(((s_ref, a_ref), (a_ref, b_ref))):

        def read(z, y, src=src):
            return src[row_of(z, y, halo), :]

        def write(z, y, value, dst=dst):
            dst[row_of(z, y, halo), :] = value + s_ref[row_of(z, y, halo), :]

        diffuse(
            lambda z, j: coef_ref[z + 1, j],
            read,
            write,
            (halo + 1 + step, halo + NZ - 1 - step),
            [(2 + step, NY - 2 - step)],
            None,
            None,
        )


def outer_kernel(
    _s, _a, _b, coef_ref, base_ref, far_low_ref, far_high_ref, low_ref, high_ref, front_ref, back_ref,
    corner_low_ref, corner_high_ref, out_hbm, coarse_ref, s_ref, a_ref, b_ref,
    out_ref, cells_ref, rim_ref, edge_ref, sums_ref, sems,
):
    halo = 3
    zero = jnp.zeros((8, 128), F32)
    coef = lambda z, j: coef_ref[z + 1, j]

    def rim_at(z, y):
        slot = y + 4 if y < 1 else y - NY + 6
        return pl.ds(pl.multiple_of(((z + 1) * 10 + slot) * 8, 8), 8)

    def edge_at(z, y):
        slot = y + 3 if y < 1 else y - NY + 5
        return pl.ds(pl.multiple_of((z * 8 + slot) * 8, 8), 8)

    low, high = edges("logic", LOGICS)
    below, above = edges("slab", SLABS)

    def strips(z, slot, front, back, keep_front, keep_back):
        for xb in range(8):
            cells_ref[slot, pl.ds(xb * 8, 8), :] = front(xb).astype(F32)
            cells_ref[slot + 1, pl.ds(xb * 8, 8), :] = back(xb).astype(F32)
        rim_ref[rim_at(z, 0), :] = zero
        rim_ref[rim_at(z, NY - 1), :] = zero
        for at in range(8):
            before = cells_ref[slot, pl.ds(at, 8, stride=8), :] * keep_front
            after = cells_ref[slot + 1, pl.ds(at, 8, stride=8), :] * keep_back
            if at < 4:
                rim_ref[rim_at(z, NY + at), :] = after
                if at:
                    s_ref[row_of(z, at - 4, halo), :] = before
            else:
                rim_ref[rim_at(z, at - 8), :] = before
                if at < 7:
                    s_ref[row_of(z, NY + at - 4, halo), :] = after

    rim_ref[pl.ds(0, 80), :] = jnp.zeros((80, 128), F32)
    rim_ref[pl.ds(15 * 80, 80), :] = jnp.zeros((80, 128), F32)

    def own(i, _):
        for half in range(2):
            z = 2 * i + half
            strips(
                z + halo, 2 * half, lambda xb: front_ref[z, xb], lambda xb: back_ref[z, xb], low, high
            )
        return 0

    lax.fori_loop(0, NZ // 2, own, 0)

    def outer(z, _):
        for side, (base, body, corner, keep) in enumerate(
            ((0, low_ref, corner_low_ref, below), (11, high_ref, corner_high_ref, above))
        ):
            for block in range(4):
                slot = 8 * side + 2 * block
                for xb in range(8):
                    two = body[z * 4 + block, xb].astype(F32)
                    cells_ref[slot, pl.ds(xb * 8, 8), :] = two[:8]
                    cells_ref[slot + 1, pl.ds(xb * 8, 8), :] = two[8:]
                for y in range(16):
                    s_ref[row_of(z + base, 16 * block + y, halo), :] = (
                        cells_ref[slot + y // 8, pl.ds(y % 8, 8, stride=8), :] * keep
                    )
            strips(
                z + base,
                16 + 2 * side,
                lambda xb: corner[z, xb].astype(F32)[:8],
                lambda xb: corner[z, xb].astype(F32)[8:],
                keep * low,
                keep * high,
            )
        return 0

    lax.fori_loop(0, halo, outer, 0)
    for side, (z, j, body, keep) in enumerate(((0, 5, far_low_ref, below), (13, 4, far_high_ref, above))):
        factor = coef(z, j) * keep
        for block in range(4):
            slot = 8 * side + 2 * block
            two = body[0, 16 * block : 16 * block + 16, :].astype(F32)
            for xb in range(8):
                part = two[:, 128 * xb : 128 * xb + 128]
                cells_ref[slot, pl.ds(xb * 8, 8), :] = part[:8]
                cells_ref[slot + 1, pl.ds(xb * 8, 8), :] = part[8:]
            for y in range(16):
                at = row_of(z, 16 * block + y, halo)
                s_ref[at, :] = (
                    s_ref[at, :] + factor * cells_ref[slot + y // 8, pl.ds(y % 8, 8, stride=8), :]
                )

    def read_rim(z, y):
        return rim_ref[rim_at(z, y), :]

    def write_edge(z, y, value):
        edge_ref[edge_at(z, y), :] = value + s_ref[row_of(z, y, halo), :]
        if y == -1:
            edge_ref[edge_at(z, 0), :] = (
                coef(z, 3) * read_rim(z, -1) + s_ref[row_of(z, 0, halo), :]
            )
        if y == NY:
            edge_ref[edge_at(z, NY - 1), :] = (
                coef(z, 3) * read_rim(z, NY) + s_ref[row_of(z, NY - 1, halo), :]
            )

    diffuse(coef, read_rim, write_edge, (0, NZ + 2 * halo), [(-3, 0), (NY, NY + 3)], low, high)

    def first(z, y):
        if 1 <= y < NY - 1:
            return s_ref[row_of(z, y, halo), :]
        return edge_ref[edge_at(z, y), :]

    def second(z, y):
        return a_ref[row_of(z, y, halo), :]

    def third(z, y):
        return b_ref[row_of(z, y, halo), :]

    def to(ref):
        def write(z, y, value):
            ref[row_of(z, y, halo), :] = value + s_ref[row_of(z, y, halo), :]

        return write

    every = lambda reach: [(-reach, NY + reach)]
    diffuse(coef, first, to(a_ref), (1, 4), every(2), low, high)
    diffuse(coef, first, to(a_ref), (10, 13), every(2), low, high)
    diffuse(coef, first, to(a_ref), (4, 10), [(-2, 2), (NY - 2, NY + 2)], low, high)
    diffuse(coef, second, to(b_ref), (2, 5), every(1), low, high)
    diffuse(coef, second, to(b_ref), (9, 12), every(1), low, high)
    diffuse(coef, second, to(b_ref), (5, 9), [(-1, 3), (NY - 3, NY + 1)], low, high)

    def store(z):
        return pltpu.make_async_copy(out_ref.at[z], out_hbm.at[z], sems.at[z])

    def write_out(z, y, value):
        own = z - halo
        value = value + s_ref[row_of(z, y, halo), :]
        value = value + base_ref[pl.ds(pl.multiple_of((own * NY + y) * 8, 8), 8), :]
        out_ref[own, y // 8, pl.ds(y % 8, 8, stride=8), :] = value
        here = pl.ds(pl.multiple_of((own * 4 + y // 16) * 8, 8), 8)
        if y % 16 == 0:
            sums_ref[here, :] = value
        else:
            sums_ref[here, :] = sums_ref[here, :] + value
        if y == NY - 1:
            store(own).start()

    diffuse(coef, third, write_out, (halo, halo + NZ), every(0), low, high)
    exact = lax.Precision.HIGHEST
    lines = lax.dot_general(
        jnp.ones((8, 128), F32), sums_ref[...], (((1,), (1,)), ((), ())),
        precision=exact, preferred_element_type=F32,
    )
    pairs = jnp.where((iota((256, 128), 0) >> 1) == iota((256, 128), 1), 1.0 / 4096.0, 0.0)
    means = jnp.dot(lines, pairs, precision=exact, preferred_element_type=F32)
    coarse_ref[...] = jnp.broadcast_to(means[0:1, :], (DEV, 128))
    for z in range(NZ):
        store(z).wait()


def vmem(count):
    return [pl.BlockSpec(memory_space=pltpu.VMEM)] * count


def smem(count):
    return [pl.BlockSpec(memory_space=pltpu.SMEM)] * count


def params():
    return pltpu.CompilerParams(vmem_limit_bytes=VMEM)


def cost(flops, moved):
    return pl.CostEstimate(flops=flops, bytes_accessed=moved, transcendentals=0)


def shift(value, axis, by):
    count = lax.axis_size(axis)
    return lax.ppermute(value, axis, [(i, (i + by) % count) for i in range(count)])


def per_device(
    initial_heat_state,
    dynamic_wattage,
    drain_multiplier,
    holder_processor,
    patch_target_slot,
    active_patch_number,
    prior_reduced_heat_map,
    conductivity_lookup,
    substance_of_slab,
):
    state = initial_heat_state
    both = ("logic", "slab")
    shape = jax.ShapeDtypeStruct
    to_high, to_low, far_high, far_low, t_first, t_last = pl.pallas_call(
        edge_kernel,
        grid=(NZ // 2,),
        out_shape=[
            shape((3, NY, 1024), BF16),
            shape((3, NY, 1024), BF16),
            shape((1, NY, 1024), BF16),
            shape((1, NY, 1024), BF16),
            shape((2, 4, 8, 8, 128), BF16),
            shape((2, 4, 8, 8, 128), BF16),
        ],
        in_specs=[
            pl.BlockSpec((1, NY, 1024), lambda i: (i, 0, 0)),
            pl.BlockSpec((1, NY, 1024), lambda i: (i + NZ // 2, 0, 0)),
        ],
        out_specs=[
            pl.BlockSpec((1, NY, 1024), lambda i: (jnp.maximum(i - 1, 0), 0, 0)),
            pl.BlockSpec((1, NY, 1024), lambda i: (jnp.minimum(i, 2), 0, 0)),
            pl.BlockSpec((1, NY, 1024), lambda i: (0, 0, 0)),
            pl.BlockSpec((1, NY, 1024), lambda i: (0, 0, 0)),
            pl.BlockSpec((2, 1, 8, 8, 128), lambda i: (0, i, 0, 0, 0)),
            pl.BlockSpec((2, 1, 8, 8, 128), lambda i: (0, i, 0, 0, 0)),
        ],
        compiler_params=params(),
        cost_estimate=cost(1_000_000, 5_000_000),
        name="edges",
    )(state, state)
    low = shift(to_high, "slab", 1)
    high = shift(to_low, "slab", -1)

    packed = pl.pallas_call(
        pack_kernel,
        out_shape=pltpu.HBM((DEV, ROWS, 128), BF16),
        in_specs=smem(1) + [pl.BlockSpec(memory_space=pltpu.HBM)] * 5,
        out_specs=pl.BlockSpec(memory_space=pltpu.HBM),
        scratch_shapes=[
            pltpu.VMEM((1, TILES), I32),
            pltpu.VMEM((1, TILES), I32),
            pltpu.VMEM((1, TILES), F32),
            pltpu.VMEM((LAYERS, 128), F32),
            pltpu.VMEM((TILES, 256), BF16),
            pltpu.VMEM((DEV, ROWS, 128), BF16),
            pltpu.VMEM((DEV, TILES), F32),
            pltpu.VMEM((CAP, TILES), BF16),
            pltpu.VMEM((DEV, 128), F32),
            pltpu.VMEM((DEV, 128), F32),
            pltpu.VMEM((TILES, 256), BF16),
            pltpu.SemaphoreType.DMA((5,)),
            pltpu.SemaphoreType.DMA((DEV // GROUP,)),
        ],
        compiler_params=params(),
        cost_estimate=cost(5_000_000_000, 4_000_000),
        name="pack",
    )(
        active_patch_number,
        holder_processor.reshape(1, TILES),
        patch_target_slot.reshape(1, TILES),
        drain_multiplier.reshape(1, TILES),
        prior_reduced_heat_map.transpose(1, 2, 0).reshape(128, LAYERS),
        dynamic_wattage,
    )
    packed, low, high, far_high, far_low = lax.optimization_barrier(
        (packed, low, high, far_high, far_low)
    )
    t_low = shift(far_high, "slab", 1)
    t_high = shift(far_low, "slab", -1)
    got = lax.all_to_all(packed, both, split_axis=0, concat_axis=0, tiled=True)

    base, coef = pl.pallas_call(
        temperature_kernel,
        out_shape=[shape((NZ * NY * 8, 128), F32), shape((16, 6, 8, 128), F32)],
        in_specs=smem(2) + vmem(3),
        out_specs=vmem(2),
        scratch_shapes=[
            pltpu.VMEM((16, 8, 64, 128), F32),
            pltpu.VMEM((16 * 72 * 8, 128), F32),
            pltpu.VMEM((16 * 72 * 8, 128), F32),
        ],
        compiler_params=params(),
        cost_estimate=cost(100_000_000, 20_000_000),
        name="diffuse_temperature",
    )(conductivity_lookup, substance_of_slab, state, low, high)
    got, base, coef = lax.optimization_barrier((got, base, coef))

    source, lower, upper, first, last = pl.pallas_call(
        scatter_kernel,
        out_shape=[
            shape((64, 8, 8, 128), F32),
            shape((12, 8, 16, 128), BF16),
            shape((12, 8, 16, 128), BF16),
            shape((NZ, 8, 8, 128), BF16),
            shape((NZ, 8, 8, 128), BF16),
        ],
        in_specs=vmem(1) + [pl.BlockSpec(memory_space=pltpu.HBM)] * 2,
        out_specs=vmem(5),
        scratch_shapes=[
            pltpu.VMEM((32, 128), I32),
            pltpu.VMEM((NZ, 8, 8, 128), BF16),
            pltpu.VMEM((NZ, 8, 8, 128), BF16),
            pltpu.SemaphoreType.DMA((2,)),
        ],
        compiler_params=params(),
        cost_estimate=cost(5_000_000_000, 6_000_000),
        name="place_tiles",
    )(
        got,
        pltpu.with_memory_space_constraint(t_first.reshape(NZ, 8, 8, 128), pltpu.HBM),
        pltpu.with_memory_space_constraint(t_last.reshape(NZ, 8, 8, 128), pltpu.HBM),
    )
    lower, upper, first, last, t_low, t_high = lax.optimization_barrier(
        (lower, upper, first, last, t_low, t_high)
    )
    s_front = shift(last, "logic", 1)
    s_back = shift(first, "logic", -1)
    s_low = shift(upper, "slab", 1)
    s_high = shift(lower, "slab", -1)
    to_high, to_low = pl.pallas_call(
        corner_kernel,
        out_shape=[shape((3, 8, 16, 128), BF16)] * 2,
        in_specs=vmem(2),
        out_specs=vmem(2),
        compiler_params=params(),
        cost_estimate=cost(8_000_000_000, 1_000_000),
        name="corners",
    )(s_front, s_back)
    s_corner_low = shift(to_high, "slab", 1)
    s_corner_high = shift(to_low, "slab", -1)

    rows = pltpu.VMEM((14 * 72 * 8, 128), F32)
    parts = pl.pallas_call(
        inner_kernel,
        out_shape=[rows] * 3,
        in_specs=vmem(2),
        out_specs=vmem(3),
        compiler_params=params(),
        cost_estimate=cost(20_000_000, 10_000_000),
        name="diffuse_inner",
    )(coef, source.reshape(4096, 128))
    new_state, coarse, *_ = pl.pallas_call(
        outer_kernel,
        out_shape=[pltpu.HBM((NZ, 8, 64, 128), F32), shape((DEV, 128), F32)] + [rows] * 3,
        in_specs=vmem(13),
        out_specs=[pl.BlockSpec(memory_space=pltpu.HBM)] + vmem(4),
        input_output_aliases={0: 2, 1: 3, 2: 4},
        scratch_shapes=[
            pltpu.VMEM((NZ, 8, 64, 128), F32),
            pltpu.VMEM((20, 64, 128), F32),
            pltpu.VMEM((16 * 80, 128), F32),
            pltpu.VMEM((14 * 64, 128), F32),
            pltpu.VMEM((256, 128), F32),
            pltpu.SemaphoreType.DMA((NZ,)),
        ],
        compiler_params=params(),
        cost_estimate=cost(100_000_000, 20_000_000),
        name="diffuse_outer",
    )(*parts, coef, base, t_low, t_high, s_low, s_high, s_front, s_back, s_corner_low, s_corner_high)
    thermal_state = (
        new_state.reshape(NZ, 8, 8, 8, 128).transpose(0, 1, 3, 2, 4).reshape(NZ, NY, 1024)
    )
    gathered = lax.all_to_all(coarse, both, split_axis=0, concat_axis=0, tiled=True)
    reduced_map = gathered.reshape(LOGICS, SLABS, NZ, 4, 4)
    reduced_map = jnp.transpose(reduced_map, (1, 2, 0, 3, 4)).reshape(LAYERS, 32, 4)
    return (thermal_state, reduced_map)


def solution(mesh):
    return jax.shard_map(
        per_device,
        mesh=mesh,
        in_specs=(
            P("slab", "logic", None),
            P(("logic", "slab"), None),
            P(("logic", "slab")),
            P(("logic", "slab"), None),
            P(("logic", "slab")),
            P(("logic", "slab")),
            P(),
            P(),
            P(),
        ),
        out_specs=(P("slab", "logic", None), P()),
        check_vma=False,
    )
```

```python
import functools

import jax
import jax.numpy as jnp
from jax import lax
from jax.experimental import pallas as pl
from jax.experimental.pallas import tpu as pltpu
from jax.sharding import PartitionSpec as P

LEAK_BETA = 0.7
THERMAL_FACTOR = 0.1

DEV = 128
CAP = 32
TILES = 2048
NZ = 8
NY = 64
LAYERS = 128
SLABS = 16
LOGICS = 8
ROWS = 72
GROUP = 32
VMEM = 28 * 1024 * 1024
F32 = jnp.float32
BF16 = jnp.bfloat16
I32 = jnp.int32


def iota(shape, dim):
    return lax.broadcasted_iota(I32, shape, dim)


def edge_kernel(lower_ref, upper_ref, to_high_ref, to_low_ref):
    to_low_ref[...] = lower_ref[...].astype(BF16)
    to_high_ref[...] = upper_ref[...].astype(BF16)


def far_kernel(lower_ref, upper_ref, far_high_ref, far_low_ref, first_ref, last_ref):
    step = pl.program_id(0)

    @pl.when(step == 3)
    def _():
        far_low_ref[...] = lower_ref[...].astype(BF16)

    @pl.when(step == 0)
    def _():
        far_high_ref[...] = upper_ref[...].astype(BF16)

    for half, ref in ((0, lower_ref), (1, upper_ref)):
        for xb in range(8):
            cols = slice(128 * xb, 128 * xb + 128)
            first_ref[half, 0, xb] = ref[0, :8, cols].astype(BF16)
            last_ref[half, 0, xb] = ref[0, NY - 8 :, cols].astype(BF16)


def corner_kernel(front_ref, back_ref, low_ref, high_ref):
    for out, first in ((low_ref, NZ - 3), (high_ref, 0)):
        for z in range(3):
            for xb in range(8):
                out[z, xb] = jnp.concatenate(
                    [front_ref[first + z, xb].astype(F32), back_ref[first + z, xb].astype(F32)], axis=0
                ).astype(BF16)


def pack_kernel(
    count_ref, owner_hbm, target_hbm, drain_hbm, prior_hbm, watt_hbm, out_hbm,
    owner_ref, target_ref, drain_ref, prior_ref, watt_ref, out_ref,
    member_ref, pick_ref, high_ref, low_ref, power_ref, in_sems, out_sems,
):
    loads = [
        pltpu.make_async_copy(src, dst, in_sems.at[i])
        for i, (src, dst) in enumerate(
            (
                (owner_hbm, owner_ref),
                (target_hbm, target_ref),
                (prior_hbm, prior_ref),
                (drain_hbm, drain_ref),
                (watt_hbm, watt_ref),
            )
        )
    ]
    for load in loads:
        load.start()
    for load in loads[:4]:
        load.wait()
    owner = owner_ref[...]
    target = target_ref[...]
    live = iota((1, TILES), 1) < count_ref[0]
    layer = (owner & (SLABS - 1)) * NZ + (target >> 8)
    column = (owner >> 4) * 16 + ((target >> 6) & 3) * 4 + (target & 3)
    at_layer = jnp.where(iota((LAYERS, TILES), 0) == layer, 1.0, 0.0).astype(BF16)
    prior = prior_ref[...]
    first = prior.astype(BF16)
    rest = prior - first.astype(F32)
    second = rest.astype(BF16)
    third = (rest - second.astype(F32)).astype(BF16)
    lookup = lambda part: lax.dot_general(
        part, at_layer, (((1,), (0,)), ((), ())), preferred_element_type=F32
    )
    picked = lookup(first) + lookup(second) + lookup(third)
    heat = jnp.sum(
        jnp.where(iota((LAYERS, TILES), 0) == column, picked, 0.0), axis=0, keepdims=True
    )
    scale = 1.0 + drain_ref[...] * jnp.exp(LEAK_BETA * heat)
    member = jnp.where(iota((DEV, TILES), 0) == jnp.where(live, owner, -1), 1.0, 0.0)
    member_ref[...] = member
    before = jnp.where(iota((256, 256), 0) < iota((256, 256), 1), 1.0, 0.0).astype(BF16)
    carry = jnp.zeros((DEV, 1), F32)
    ranks = []
    for b in range(TILES // 256):
        part = member[:, 256 * b : 256 * b + 256]
        earlier = jnp.dot(part.astype(BF16), before, preferred_element_type=F32) + carry
        ranks.append(jnp.sum(earlier * part, axis=0, keepdims=True))
        carry = carry + jnp.sum(part, axis=1, keepdims=True)
    rank = jnp.where(live, jnp.concatenate(ranks, axis=1).astype(I32), -1)
    pick_ref[...] = jnp.where(iota((CAP, TILES), 0) == rank, 1.0, 0.0).astype(BF16)
    slot = (iota((128, TILES), 0) & (CAP - 1)) == rank
    flat = member.astype(BF16)
    spot = lambda value: lax.dot_general(
        flat,
        jnp.where(slot, value.astype(F32), 0.0).astype(BF16),
        (((1,), (1,)), ((), ())),
        preferred_element_type=F32,
    )
    high_ref[...] = spot((target >> 6) + 1)
    low_ref[...] = spot(target & 63)
    row8 = iota((8, 128), 0)
    loads[4].wait()
    for b in range(TILES // 128):
        rows = pl.ds(128 * b, 128)
        spread = jnp.transpose(jnp.broadcast_to(scale[:, 128 * b : 128 * b + 128], (128, 128)))
        for h in range(2):
            cols = pl.ds(128 * h, 128)
            power_ref[rows, cols] = (watt_ref[rows, cols].astype(F32) * spread).astype(BF16)

    def store(g):
        here = pl.ds(g * GROUP, GROUP)
        return pltpu.make_async_copy(out_ref.at[here], out_hbm.at[here], out_sems.at[g])

    def group(g, _):
        pick = pick_ref[...]
        parts = []
        for j in range(GROUP):
            d = g * GROUP + j
            parts.append(pick * member_ref[pl.ds(d, 1), :].astype(BF16))
            label = jnp.where(
                row8 == 0,
                high_ref[pl.ds(d, 1), :],
                jnp.where(row8 == 1, low_ref[pl.ds(d, 1), :], 0.0),
            )
            out_ref[d, 64:72, :] = label.astype(BF16)
        packed = jnp.dot(
            jnp.concatenate(parts, axis=0), power_ref[...], preferred_element_type=F32
        ).astype(BF16)
        here = pl.ds(g * GROUP, GROUP)
        out_ref[here, 0:32, :] = packed[:, :128].reshape(GROUP, CAP, 128)
        out_ref[here, 32:64, :] = packed[:, 128:].reshape(GROUP, CAP, 128)
        store(g).start()
        return 0

    lax.fori_loop(0, DEV // GROUP, group, 0)
    for g in range(DEV // GROUP):
        store(g).wait()


def scatter_kernel(
    got_ref, first_hbm, last_hbm, source_ref, low_ref, high_ref, front_ref, back_ref,
    label_ref, first_ref, last_ref, sems,
):
    loads = [
        pltpu.make_async_copy(first_hbm, first_ref, sems.at[0]),
        pltpu.make_async_copy(last_hbm, last_ref, sems.at[1]),
    ]
    for load in loads:
        load.start()
    labels = got_ref[:, 64:72, :].reshape(DEV * 8, 128)
    row = iota((DEV * 8, 128), 0)
    lane = iota((DEV * 8, 128), 1)
    labels = jnp.where((lane >> 5) == ((row >> 3) & 3), labels.astype(F32), 0.0).astype(BF16)
    g = iota((32, DEV * 8), 0)
    col = iota((32, DEV * 8), 1)
    weight = jnp.where((col & 7) == 0, 64.0, jnp.where((col & 7) == 1, 1.0, 0.0))
    weight = jnp.where((col >> 5) == g, weight, 0.0).astype(BF16)
    target = jnp.dot(weight, labels, preferred_element_type=F32).astype(I32) - 64
    label_ref[...] = target
    left = got_ref[:, 0:32, :].reshape(DEV * CAP, 128)
    right = got_ref[:, 32:64, :].reshape(DEV * CAP, 128)
    both = jnp.concatenate([left, right], axis=1)
    wanted = iota((512, 128), 0) * 4
    upper = iota((8, 128), 0) < 4
    for load in loads:
        load.wait()
    for c in range(4):
        chosen = jnp.concatenate(
            [
                jnp.where(wanted == label_ref[k : k + 1, :] - c, 1.0, 0.0).astype(BF16)
                for k in range(32)
            ],
            axis=1,
        )
        total = THERMAL_FACTOR * jnp.dot(chosen, both, preferred_element_type=F32)
        for h in range(2):
            xb = 2 * c + h
            part = total[:, 128 * h : 128 * h + 128]
            cells = part.reshape(NZ * 8, 8, 128)
            source_ref[:, xb] = cells
            short = part.astype(BF16).reshape(NZ * 4, 16, 128)
            low_ref[:, xb] = short[:12]
            high_ref[:, xb] = short[20:]
            for z in range(NZ):
                front_ref[z, xb] = jnp.where(
                    upper, first_ref[z, xb].astype(F32), pltpu.roll(cells[8 * z], 4, 0)
                ).astype(BF16)
                back_ref[z, xb] = jnp.where(
                    upper, pltpu.roll(cells[8 * z + 7], 4, 0), last_ref[z, xb].astype(F32)
                ).astype(BF16)


def fill_coefficients(coef_ref, table_ref, label_ref, halo):
    base = lax.axis_index("slab") * NZ - halo
    spot = iota((8, 128), 0) * 128 + iota((8, 128), 1)

    def layer(i, _):
        z = base + i
        inside = jnp.where((z >= 0) & (z < LAYERS), 1.0, 0.0).astype(F32)
        material = lambda at: label_ref[jnp.clip(at, 0, LAYERS - 1)]
        here = material(z)
        splat = lambda m, k: jnp.full((8, 128), table_ref[m, k], F32)
        kx = splat(here, 0)
        ky = splat(here, 1)
        a = splat(here, 2)
        above = splat(material(z + 1), 2)
        below = splat(material(z - 1), 2)
        up = 2.0 * a * above / (a + above)
        down = 2.0 * a * below / (a + below)
        keep = jnp.full((8, 128), inside, F32)
        coef_ref[i, 0] = keep * (1.0 - 2.0 * kx - 2.0 * ky - up - down)
        coef_ref[i, 1] = keep * jnp.where(spot == 0, 0.0, kx)
        coef_ref[i, 2] = keep * jnp.where(spot == 1023, 0.0, kx)
        coef_ref[i, 3] = keep * ky
        coef_ref[i, 4] = keep * up
        coef_ref[i, 5] = keep * down
        return 0

    lax.fori_loop(0, NZ + 2 * halo, layer, 0)


def diffuse(coef, read, write, layers, ranges, low, high):
    lane = iota((8, 128), 1)

    def layer(z, _):
        c = [coef(z, j) for j in range(6)]
        for rows in ranges:
            before, cell = read(z, rows[0] - 1), read(z, rows[0])
            for y in range(rows[0], rows[1]):
                after = read(z, y + 1)
                step = pltpu.roll(cell, 127, 1)
                right = jnp.where(lane == 127, pltpu.roll(step, 7, 0), step)
                step = pltpu.roll(cell, 1, 1)
                left = jnp.where(lane == 0, pltpu.roll(step, 1, 0), step)
                value = (
                    c[0] * cell
                    + c[1] * left
                    + c[2] * right
                    + c[3] * (before + after)
                    + c[4] * read(z + 1, y)
                    + c[5] * read(z - 1, y)
                )
                if y < 0:
                    value = value * low
                if y >= NY:
                    value = value * high
                write(z, y, value)
                before, cell = cell, after
        return 0

    count = layers[1] - layers[0]
    unroll = 4 if count % 4 == 0 else 2 if count % 2 == 0 else 3 if count % 3 == 0 else 1
    lax.fori_loop(layers[0], layers[1], layer, 0, unroll=unroll)


def edges(axis, count):
    at = lax.axis_index(axis)
    low = jnp.full((8, 128), jnp.where(at > 0, 1.0, 0.0), F32)
    high = jnp.full((8, 128), jnp.where(at < count - 1, 1.0, 0.0), F32)
    return low, high


def row_of(z, y, halo):
    return pl.ds(pl.multiple_of((z * (NY + 8) + (y + 4)) * 8, 8), 8)


def temperature_kernel(
    table_ref, label_ref, state_ref, low_ref, high_ref, out_ref, coef_ref, cells_ref, a_ref, b_ref,
):
    halo = 4
    fill_coefficients(coef_ref, table_ref, label_ref, halo)

    def spread(z, block, value):
        for xb in range(8):
            cells_ref[z, block, pl.ds(xb * 8, 8), :] = value[:, 128 * xb : 128 * xb + 128]

    def gather(z, keep=None):
        for y in range(NY):
            value = cells_ref[z, y // 8, pl.ds(y % 8, 8, stride=8), :]
            a_ref[row_of(z, y, halo), :] = value if keep is None else value * keep

    def clear(z, _):
        for y in (-3, -2, -1, NY, NY + 1, NY + 2):
            a_ref[row_of(z, y, halo), :] = jnp.zeros((8, 128), F32)
            b_ref[row_of(z, y, halo), :] = jnp.zeros((8, 128), F32)
        return 0

    lax.fori_loop(0, NZ + 2 * halo, clear, 0)
    for z in (0, NZ + 2 * halo - 1):
        for y in range(NY):
            a_ref[row_of(z, y, halo), :] = jnp.zeros((8, 128), F32)

    def own(z, _):
        for block in range(8):
            spread(z + halo, block, state_ref[z, 8 * block : 8 * block + 8, :])
        gather(z + halo)
        return 0

    lax.fori_loop(0, NZ, own, 0)

    below, above = edges("slab", SLABS)

    def outer(z, _):
        for base, body, keep in ((1, low_ref, below), (12, high_ref, above)):
            for block in range(4):
                two = body[z, 16 * block : 16 * block + 16, :].astype(F32)
                spread(z + base, 2 * block, two[:8])
                spread(z + base, 2 * block + 1, two[8:])
            gather(z + base, keep)
        return 0

    lax.fori_loop(0, halo - 1, outer, 0)
    low, high = edges("logic", LOGICS)
    bufs = (a_ref, b_ref)
    for step in range(4):
        src, dst = bufs[step % 2], bufs[(step + 1) % 2]
        reach = 3 - step
        wide = (1, 2, 1, 0)[step]

        def read(z, y, src=src):
            return src[row_of(z, y, halo), :]

        def write(z, y, value, dst=dst, step=step):
            if step == 3:
                out_ref[pl.ds(pl.multiple_of(((z - halo) * NY + y) * 8, 8), 8), :] = value
            else:
                dst[row_of(z, y, halo), :] = value

        diffuse(
            lambda z, j: coef_ref[z, j],
            read,
            write,
            (halo - reach, halo + NZ + reach),
            [(-wide, NY + wide)],
            low,
            high,
        )


def inner_kernel(coef_ref, source_ref, s_ref, a_ref, b_ref):
    halo = 3

    def own(z, _):
        for y in range(NY):
            start = (z * 8 + y // 8) * 64 + y % 8
            s_ref[row_of(z + halo, y, halo), :] = source_ref[pl.ds(start, 8, stride=8), :]
        return 0

    lax.fori_loop(0, NZ, own, 0)
    for step, (src, dst) in enumerate(((s_ref, a_ref), (a_ref, b_ref))):

        def read(z, y, src=src):
            return src[row_of(z, y, halo), :]

        def write(z, y, value, dst=dst):
            dst[row_of(z, y, halo), :] = value + s_ref[row_of(z, y, halo), :]

        diffuse(
            lambda z, j: coef_ref[z + 1, j],
            read,
            write,
            (halo + 1 + step, halo + NZ - 1 - step),
            [(2 + step, NY - 2 - step)],
            None,
            None,
        )


def outer_kernel(
    _s, _a, _b, coef_ref, base_ref, far_low_ref, far_high_ref, low_ref, high_ref, front_ref, back_ref,
    corner_low_ref, corner_high_ref, out_hbm, coarse_ref, s_ref, a_ref, b_ref,
    out_ref, cells_ref, rim_ref, edge_ref, sums_ref, sems,
):
    halo = 3
    zero = jnp.zeros((8, 128), F32)
    coef = lambda z, j: coef_ref[z + 1, j]

    def rim_at(z, y):
        slot = y + 4 if y < 1 else y - NY + 6
        return pl.ds(pl.multiple_of(((z + 1) * 10 + slot) * 8, 8), 8)

    def edge_at(z, y):
        slot = y + 3 if y < 1 else y - NY + 5
        return pl.ds(pl.multiple_of((z * 8 + slot) * 8, 8), 8)

    low, high = edges("logic", LOGICS)
    below, above = edges("slab", SLABS)

    def strips(z, slot, front, back, keep_front, keep_back):
        for xb in range(8):
            cells_ref[slot, pl.ds(xb * 8, 8), :] = front(xb).astype(F32)
            cells_ref[slot + 1, pl.ds(xb * 8, 8), :] = back(xb).astype(F32)
        rim_ref[rim_at(z, 0), :] = zero
        rim_ref[rim_at(z, NY - 1), :] = zero
        for at in range(8):
            before = cells_ref[slot, pl.ds(at, 8, stride=8), :] * keep_front
            after = cells_ref[slot + 1, pl.ds(at, 8, stride=8), :] * keep_back
            if at < 4:
                rim_ref[rim_at(z, NY + at), :] = after
                if at:
                    s_ref[row_of(z, at - 4, halo), :] = before
            else:
                rim_ref[rim_at(z, at - 8), :] = before
                if at < 7:
                    s_ref[row_of(z, NY + at - 4, halo), :] = after

    rim_ref[pl.ds(0, 80), :] = jnp.zeros((80, 128), F32)
    rim_ref[pl.ds(15 * 80, 80), :] = jnp.zeros((80, 128), F32)

    def own(i, _):
        for half in range(2):
            z = 2 * i + half
            strips(
                z + halo, 2 * half, lambda xb: front_ref[z, xb], lambda xb: back_ref[z, xb], low, high
            )
        return 0

    lax.fori_loop(0, NZ // 2, own, 0)

    def outer(z, _):
        for side, (base, body, corner, keep) in enumerate(
            ((0, low_ref, corner_low_ref, below), (11, high_ref, corner_high_ref, above))
        ):
            for block in range(4):
                slot = 8 * side + 2 * block
                for xb in range(8):
                    two = body[z * 4 + block, xb].astype(F32)
                    cells_ref[slot, pl.ds(xb * 8, 8), :] = two[:8]
                    cells_ref[slot + 1, pl.ds(xb * 8, 8), :] = two[8:]
                for y in range(16):
                    s_ref[row_of(z + base, 16 * block + y, halo), :] = (
                        cells_ref[slot + y // 8, pl.ds(y % 8, 8, stride=8), :] * keep
                    )
            strips(
                z + base,
                16 + 2 * side,
                lambda xb: corner[z, xb].astype(F32)[:8],
                lambda xb: corner[z, xb].astype(F32)[8:],
                keep * low,
                keep * high,
            )
        return 0

    lax.fori_loop(0, halo, outer, 0)
    for side, (z, j, body, keep) in enumerate(((0, 5, far_low_ref, below), (13, 4, far_high_ref, above))):
        factor = coef(z, j) * keep
        for block in range(4):
            slot = 8 * side + 2 * block
            two = body[0, 16 * block : 16 * block + 16, :].astype(F32)
            for xb in range(8):
                part = two[:, 128 * xb : 128 * xb + 128]
                cells_ref[slot, pl.ds(xb * 8, 8), :] = part[:8]
                cells_ref[slot + 1, pl.ds(xb * 8, 8), :] = part[8:]
            for y in range(16):
                at = row_of(z, 16 * block + y, halo)
                s_ref[at, :] = (
                    s_ref[at, :] + factor * cells_ref[slot + y // 8, pl.ds(y % 8, 8, stride=8), :]
                )

    def read_rim(z, y):
        return rim_ref[rim_at(z, y), :]

    def write_edge(z, y, value):
        edge_ref[edge_at(z, y), :] = value + s_ref[row_of(z, y, halo), :]
        if y == -1:
            edge_ref[edge_at(z, 0), :] = (
                coef(z, 3) * read_rim(z, -1) + s_ref[row_of(z, 0, halo), :]
            )
        if y == NY:
            edge_ref[edge_at(z, NY - 1), :] = (
                coef(z, 3) * read_rim(z, NY) + s_ref[row_of(z, NY - 1, halo), :]
            )

    diffuse(coef, read_rim, write_edge, (0, NZ + 2 * halo), [(-3, 0), (NY, NY + 3)], low, high)

    def first(z, y):
        if 1 <= y < NY - 1:
            return s_ref[row_of(z, y, halo), :]
        return edge_ref[edge_at(z, y), :]

    def second(z, y):
        return a_ref[row_of(z, y, halo), :]

    def third(z, y):
        return b_ref[row_of(z, y, halo), :]

    def to(ref):
        def write(z, y, value):
            ref[row_of(z, y, halo), :] = value + s_ref[row_of(z, y, halo), :]

        return write

    every = lambda reach: [(-reach, NY + reach)]
    diffuse(coef, first, to(a_ref), (1, 4), every(2), low, high)
    diffuse(coef, first, to(a_ref), (10, 13), every(2), low, high)
    diffuse(coef, first, to(a_ref), (4, 10), [(-2, 2), (NY - 2, NY + 2)], low, high)
    diffuse(coef, second, to(b_ref), (2, 5), every(1), low, high)
    diffuse(coef, second, to(b_ref), (9, 12), every(1), low, high)
    diffuse(coef, second, to(b_ref), (5, 9), [(-1, 3), (NY - 3, NY + 1)], low, high)

    def store(z):
        return pltpu.make_async_copy(out_ref.at[z], out_hbm.at[z], sems.at[z])

    def write_out(z, y, value):
        own = z - halo
        value = value + s_ref[row_of(z, y, halo), :]
        value = value + base_ref[pl.ds(pl.multiple_of((own * NY + y) * 8, 8), 8), :]
        out_ref[own, y // 8, pl.ds(y % 8, 8, stride=8), :] = value
        here = pl.ds(pl.multiple_of((own * 4 + y // 16) * 8, 8), 8)
        if y % 16 == 0:
            sums_ref[here, :] = value
        else:
            sums_ref[here, :] = sums_ref[here, :] + value
        if y == NY - 1:
            store(own).start()

    diffuse(coef, third, write_out, (halo, halo + NZ), every(0), low, high)
    exact = lax.Precision.HIGHEST
    lines = lax.dot_general(
        jnp.ones((8, 128), F32), sums_ref[...], (((1,), (1,)), ((), ())),
        precision=exact, preferred_element_type=F32,
    )
    pairs = jnp.where((iota((256, 128), 0) >> 1) == iota((256, 128), 1), 1.0 / 4096.0, 0.0)
    means = jnp.dot(lines, pairs, precision=exact, preferred_element_type=F32)
    coarse_ref[...] = jnp.broadcast_to(means[0:1, :], (DEV, 128))
    for z in range(NZ):
        store(z).wait()


def vmem(count):
    return [pl.BlockSpec(memory_space=pltpu.VMEM)] * count


def smem(count):
    return [pl.BlockSpec(memory_space=pltpu.SMEM)] * count


def params():
    return pltpu.CompilerParams(vmem_limit_bytes=VMEM)


def cost(flops, moved):
    return pl.CostEstimate(flops=flops, bytes_accessed=moved, transcendentals=0)


def shift(value, axis, by):
    count = lax.axis_size(axis)
    return lax.ppermute(value, axis, [(i, (i + by) % count) for i in range(count)])


def per_device(
    initial_heat_state,
    dynamic_wattage,
    drain_multiplier,
    holder_processor,
    patch_target_slot,
    active_patch_number,
    prior_reduced_heat_map,
    conductivity_lookup,
    substance_of_slab,
):
    state = initial_heat_state
    both = ("logic", "slab")
    shape = jax.ShapeDtypeStruct
    to_high, to_low = pl.pallas_call(
        edge_kernel,
        grid=(3,),
        out_shape=[shape((3, NY, 1024), BF16)] * 2,
        in_specs=[
            pl.BlockSpec((1, NY, 1024), lambda i: (i, 0, 0)),
            pl.BlockSpec((1, NY, 1024), lambda i: (i + 5, 0, 0)),
        ],
        out_specs=[pl.BlockSpec((1, NY, 1024), lambda i: (i, 0, 0))] * 2,
        compiler_params=params(),
        cost_estimate=cost(1_000_000, 3_000_000),
        name="edges",
    )(state, state)
    low = shift(to_high, "slab", 1)
    high = shift(to_low, "slab", -1)
    far_high, far_low, t_first, t_last = pl.pallas_call(
        far_kernel,
        grid=(NZ // 2,),
        out_shape=[
            shape((1, NY, 1024), BF16),
            shape((1, NY, 1024), BF16),
            shape((2, 4, 8, 8, 128), BF16),
            shape((2, 4, 8, 8, 128), BF16),
        ],
        in_specs=[
            pl.BlockSpec((1, NY, 1024), lambda i: (i, 0, 0)),
            pl.BlockSpec((1, NY, 1024), lambda i: (i + NZ // 2, 0, 0)),
        ],
        out_specs=[
            pl.BlockSpec((1, NY, 1024), lambda i: (0, 0, 0)),
            pl.BlockSpec((1, NY, 1024), lambda i: (0, 0, 0)),
            pl.BlockSpec((2, 1, 8, 8, 128), lambda i: (0, i, 0, 0, 0)),
            pl.BlockSpec((2, 1, 8, 8, 128), lambda i: (0, i, 0, 0, 0)),
        ],
        compiler_params=params(),
        cost_estimate=cost(1_000_000, 5_000_000),
        name="far_edges",
    )(state, state)

    packed = pl.pallas_call(
        pack_kernel,
        out_shape=pltpu.HBM((DEV, ROWS, 128), BF16),
        in_specs=smem(1) + [pl.BlockSpec(memory_space=pltpu.HBM)] * 5,
        out_specs=pl.BlockSpec(memory_space=pltpu.HBM),
        scratch_shapes=[
            pltpu.VMEM((1, TILES), I32),
            pltpu.VMEM((1, TILES), I32),
            pltpu.VMEM((1, TILES), F32),
            pltpu.VMEM((LAYERS, 128), F32),
            pltpu.VMEM((TILES, 256), BF16),
            pltpu.VMEM((DEV, ROWS, 128), BF16),
            pltpu.VMEM((DEV, TILES), F32),
            pltpu.VMEM((CAP, TILES), BF16),
            pltpu.VMEM((DEV, 128), F32),
            pltpu.VMEM((DEV, 128), F32),
            pltpu.VMEM((TILES, 256), BF16),
            pltpu.SemaphoreType.DMA((5,)),
            pltpu.SemaphoreType.DMA((DEV // GROUP,)),
        ],
        compiler_params=params(),
        cost_estimate=cost(5_000_000_000, 4_000_000),
        name="pack",
    )(
        active_patch_number,
        holder_processor.reshape(1, TILES),
        patch_target_slot.reshape(1, TILES),
        drain_multiplier.reshape(1, TILES),
        prior_reduced_heat_map.transpose(1, 2, 0).reshape(128, LAYERS),
        dynamic_wattage,
    )
    packed, low, high = lax.optimization_barrier((packed, low, high))
    t_low = shift(far_high, "slab", 1)
    t_high = shift(far_low, "slab", -1)
    got = lax.all_to_all(packed, both, split_axis=0, concat_axis=0, tiled=True)

    base, coef = pl.pallas_call(
        temperature_kernel,
        out_shape=[shape((NZ * NY * 8, 128), F32), shape((16, 6, 8, 128), F32)],
        in_specs=smem(2) + vmem(3),
        out_specs=vmem(2),
        scratch_shapes=[
            pltpu.VMEM((16, 8, 64, 128), F32),
            pltpu.VMEM((16 * 72 * 8, 128), F32),
            pltpu.VMEM((16 * 72 * 8, 128), F32),
        ],
        compiler_params=params(),
        cost_estimate=cost(100_000_000, 20_000_000),
        name="diffuse_temperature",
    )(conductivity_lookup, substance_of_slab, state, low, high)
    got, base, coef = lax.optimization_barrier((got, base, coef))

    source, lower, upper, first, last = pl.pallas_call(
        scatter_kernel,
        out_shape=[
            shape((64, 8, 8, 128), F32),
            shape((12, 8, 16, 128), BF16),
            shape((12, 8, 16, 128), BF16),
            shape((NZ, 8, 8, 128), BF16),
            shape((NZ, 8, 8, 128), BF16),
        ],
        in_specs=vmem(1) + [pl.BlockSpec(memory_space=pltpu.HBM)] * 2,
        out_specs=vmem(5),
        scratch_shapes=[
            pltpu.VMEM((32, 128), I32),
            pltpu.VMEM((NZ, 8, 8, 128), BF16),
            pltpu.VMEM((NZ, 8, 8, 128), BF16),
            pltpu.SemaphoreType.DMA((2,)),
        ],
        compiler_params=params(),
        cost_estimate=cost(5_000_000_000, 6_000_000),
        name="place_tiles",
    )(
        got,
        pltpu.with_memory_space_constraint(t_first.reshape(NZ, 8, 8, 128), pltpu.HBM),
        pltpu.with_memory_space_constraint(t_last.reshape(NZ, 8, 8, 128), pltpu.HBM),
    )
    lower, upper, first, last, t_low, t_high = lax.optimization_barrier(
        (lower, upper, first, last, t_low, t_high)
    )
    s_front = shift(last, "logic", 1)
    s_back = shift(first, "logic", -1)
    s_low = shift(upper, "slab", 1)
    s_high = shift(lower, "slab", -1)
    to_high, to_low = pl.pallas_call(
        corner_kernel,
        out_shape=[shape((3, 8, 16, 128), BF16)] * 2,
        in_specs=vmem(2),
        out_specs=vmem(2),
        compiler_params=params(),
        cost_estimate=cost(8_000_000_000, 1_000_000),
        name="corners",
    )(s_front, s_back)
    s_corner_low = shift(to_high, "slab", 1)
    s_corner_high = shift(to_low, "slab", -1)

    rows = pltpu.VMEM((14 * 72 * 8, 128), F32)
    parts = pl.pallas_call(
        inner_kernel,
        out_shape=[rows] * 3,
        in_specs=vmem(2),
        out_specs=vmem(3),
        compiler_params=params(),
        cost_estimate=cost(20_000_000, 10_000_000),
        name="diffuse_inner",
    )(coef, source.reshape(4096, 128))
    new_state, coarse, *_ = pl.pallas_call(
        outer_kernel,
        out_shape=[pltpu.HBM((NZ, 8, 64, 128), F32), shape((DEV, 128), F32)] + [rows] * 3,
        in_specs=vmem(13),
        out_specs=[pl.BlockSpec(memory_space=pltpu.HBM)] + vmem(4),
        input_output_aliases={0: 2, 1: 3, 2: 4},
        scratch_shapes=[
            pltpu.VMEM((NZ, 8, 64, 128), F32),
            pltpu.VMEM((20, 64, 128), F32),
            pltpu.VMEM((16 * 80, 128), F32),
            pltpu.VMEM((14 * 64, 128), F32),
            pltpu.VMEM((256, 128), F32),
            pltpu.SemaphoreType.DMA((NZ,)),
        ],
        compiler_params=params(),
        cost_estimate=cost(100_000_000, 20_000_000),
        name="diffuse_outer",
    )(*parts, coef, base, t_low, t_high, s_low, s_high, s_front, s_back, s_corner_low, s_corner_high)
    thermal_state = (
        new_state.reshape(NZ, 8, 8, 8, 128).transpose(0, 1, 3, 2, 4).reshape(NZ, NY, 1024)
    )
    gathered = lax.all_to_all(coarse, both, split_axis=0, concat_axis=0, tiled=True)
    reduced_map = gathered.reshape(LOGICS, SLABS, NZ, 4, 4)
    reduced_map = jnp.transpose(reduced_map, (1, 2, 0, 3, 4)).reshape(LAYERS, 32, 4)
    return (thermal_state, reduced_map)


def solution(mesh):
    return jax.shard_map(
        per_device,
        mesh=mesh,
        in_specs=(
            P("slab", "logic", None),
            P(("logic", "slab"), None),
            P(("logic", "slab")),
            P(("logic", "slab"), None),
            P(("logic", "slab")),
            P(("logic", "slab")),
            P(),
            P(),
            P(),
        ),
        out_specs=(P("slab", "logic", None), P()),
        check_vma=False,
    )
```
